128 devices in a mesh: sp: 16 (over x, y_hi, core), fl: 8 (over z, y_lo).
Axes of the slice: x: 4, y: 4 (y_hi: 2, y_lo: 2; y = y_hi * 2 + y_lo), z: 4, core: 2. Of those that a mesh axis runs over, the one named last changes fastest.
Arguments:
- inputs: bfloat16 [32, 64, 32, 256], P('sp', 'fl'), may hold values from -6 to 6
- weight_fine: bfloat16 [27, 256, 256], replicated, may hold values from -0.078125 to 0.078125
- weight_coarse: bfloat16 [27, 256, 512], P(None, None, 'fl'), may hold values from -0.078125 to 0.078125
- cotangent: bfloat16 [16, 32, 16, 512], P('sp', None, None, 'fl'), may hold values from -24 to 24
Outputs:
- coarse_out: bfloat16 [16, 32, 16, 512], P('sp', None, None, 'fl')
- grad_input: bfloat16 [32, 64, 32, 256], P('sp', 'fl')
- grad_fine: float32 [1769472], P(('sp', 'fl'))
- grad_coarse: float32 [6912, 512], P('sp', 'fl')
The draws below stay inside these ranges and needn't reach their ends.
All inputs are finite; a program needn't handle non-finite values.
Results may differ from the reference program's by a relative error of at most 0.022.
Values may be sent and summed in bfloat16 or wider, within the bound.
No kernel may reach another device: no remote copies, remote signals or barrier semaphores. Data moves between devices by JAX's collectives and lax.ppermute only.
A program may use at most 128 MiB of HBM per device.

```python
import math
import jax
import jax.numpy as jnp
from jax import lax

C = 256
C2 = 512
NZ = 32
NX = 32
NY = 64


def raised(array, rng, source, target, parts, factor):
    def block_of(axis_at):
        return (jnp.arange(array.shape[axis_at]) // (array.shape[axis_at] // parts)).reshape((-1,) + (1,) * (array.ndim - 1 - axis_at))

    one_side = jax.random.permutation(rng, parts)[block_of(target)]
    other_side = (block_of(target) + parts // 2) % parts
    return jnp.where((block_of(source) == one_side) | (block_of(source) == other_side), factor * array, array)


def level_of(rng, shape, cuts, smallest, high):
    level, own = 1.0, jax.random.fold_in(rng, 6)
    for dim, parts in cuts:
        draws = jnp.exp(jax.random.uniform(jax.random.fold_in(own, dim), (parts,), jnp.float32, smallest / len(cuts), high / len(cuts)))
        level = level * jnp.repeat(draws, shape[dim] // parts).reshape([-1 if axis == dim else 1 for axis in range(len(shape))])
    return level


def noise(rng, shape, spread, most, cuts=(), dtype=jnp.bfloat16):
    level = level_of(rng, shape, cuts, -0.22, 0.18) if cuts else 1.0
    entries = jax.random.normal(rng, shape, jnp.float32) * spread * level
    return jnp.minimum(jnp.maximum(entries, -most), most).astype(dtype)


def gaussian_with(rng, dims, scale, bound, shards, heavy, held_as=jnp.bfloat16):
    entries = scale * jax.random.normal(rng, dims, jnp.float32)
    if shards:
        entries = entries * level_of(rng, dims, shards, -0.22, 0.18)
    return jnp.clip(raised(entries, jax.random.fold_in(rng, 3), *heavy), -bound, bound).astype(held_as)


def setup_inputs(seed: int = 0) -> dict:
    key_of = jax.random.split(jax.random.key(seed), 5)
    return {
        "inputs": gaussian_with(key_of[0], (NX, NY, NZ, C), 1.0, 6.0, ((0, 16), (1, 8)), (0, 3, 16, 2.0)),
        "weight_fine": noise(key_of[1], (27, C, C), (27 * C) ** -0.5, 0.078125),
        "weight_coarse": noise(key_of[2], (27, C, C2), (27 * C) ** -0.5, 0.078125, ((2, 8),)),
        "cotangent": noise(key_of[3], (NX // 2, NY // 2, NZ // 2, C2), 4.0, 24.0, ((0, 16), (3, 8))),
    }


def tap_offsets():
    return [(first, second, third) for first in range(3) for second in range(3) for third in range(3)]

def pad_cells(values):
    return jnp.pad(values, ((1, 1), (1, 1), (1, 1), (0, 0)))

def forward_taps(padded, weight, extent):
    rows_x, rows_y, depth = extent
    total = jnp.zeros((rows_x * rows_y * depth, weight.shape[2]), jnp.float32)
    for number, (first, second, third) in enumerate(tap_offsets()):
        window = padded[first:first + rows_x, second:second + rows_y, third:third + depth, :]
        total = total + jnp.dot(window.reshape(-1, window.shape[-1]), weight[number], preferred_element_type=jnp.float32)
    return total.reshape(rows_x, rows_y, depth, weight.shape[2])

def backward_taps(padded, weight, extent):
    rows_x, rows_y, depth = extent
    total = jnp.zeros((rows_x * rows_y * depth, weight.shape[1]), jnp.float32)
    for number, (first, second, third) in enumerate(tap_offsets()):
        window = padded[2 - first:2 - first + rows_x, 2 - second:2 - second + rows_y, 2 - third:2 - third + depth, :]
        total = total + lax.dot_general(window.reshape(-1, window.shape[-1]), weight[number], (((1,), (1,)), ((), ())), preferred_element_type=jnp.float32)
    return total.reshape(rows_x, rows_y, depth, weight.shape[1])

def weight_taps(padded, grads, extent):
    rows_x, rows_y, depth = extent
    flat_grads = grads.reshape(-1, grads.shape[-1])
    pieces = []
    for first, second, third in tap_offsets():
        window = padded[first:first + rows_x, second:second + rows_y, third:third + depth, :]
        pieces.append(lax.dot_general(window.reshape(-1, window.shape[-1]), flat_grads, (((0,), (0,)), ((), ())), preferred_element_type=jnp.float32))
    return jnp.stack(pieces)

def pool_cells(values):
    rows_x, rows_y, depth, width = values.shape
    blocks = values.astype(jnp.float32).reshape(rows_x // 2, 2, rows_y // 2, 2, depth // 2, 2, width)
    return lax.optimization_barrier(jnp.mean(blocks, axis=(1, 3, 5))).astype(jnp.bfloat16)

def spread_cells(values):
    rows_x, rows_y, depth, width = values.shape
    wide = jnp.broadcast_to(values[:, None, :, None, :, None, :], (rows_x, 2, rows_y, 2, depth, 2, width))
    return wide.reshape(rows_x * 2, rows_y * 2, depth * 2, width)

def silu_slope(values):
    sigma = jax.nn.sigmoid(values)
    return sigma * (1.0 + values * (1.0 - sigma))

def reference(inputs, weight_fine, weight_coarse, cotangent):
    rows_x, rows_y, depth, width = inputs.shape
    fine_extent = (rows_x, rows_y, depth)
    coarse_extent = (rows_x // 2, rows_y // 2, depth // 2)
    cells = rows_x * rows_y * depth
    padded_in = pad_cells(inputs)
    fine_pre = forward_taps(padded_in, weight_fine, fine_extent)
    fine_act = (fine_pre * jax.nn.sigmoid(fine_pre)).astype(jnp.bfloat16)
    pooled = pool_cells(fine_act)
    padded_pool = pad_cells(pooled)
    coarse_out = forward_taps(padded_pool, weight_coarse, coarse_extent).astype(jnp.bfloat16)
    grad_coarse = weight_taps(padded_pool, cotangent, coarse_extent).reshape(-1, cotangent.shape[-1]) * (1.0 / math.sqrt(cells // 8))
    pooled_grad = backward_taps(pad_cells(cotangent), weight_coarse, coarse_extent).astype(jnp.bfloat16)
    fine_grad = (spread_cells(pooled_grad.astype(jnp.float32)) * 0.125 * silu_slope(fine_pre)).astype(jnp.bfloat16)
    grad_fine = weight_taps(padded_in, fine_grad, fine_extent).reshape(-1) * (1.0 / math.sqrt(cells))
    grad_input = backward_taps(pad_cells(fine_grad), weight_fine, fine_extent).astype(jnp.bfloat16)
    return (coarse_out, grad_input, grad_fine, grad_coarse)
```

```python
import math

import jax
import jax.numpy as jnp
from jax import lax
from jax.sharding import PartitionSpec as P


def padded_2(cells, sides, width):
    for axis, dim in sides:
        count = lax.axis_size(axis)
        ends = count - 1
        head = lax.slice_in_dim(cells, 0, width, axis=dim)
        tail = lax.slice_in_dim(cells, cells.shape[dim] - width, cells.shape[dim], axis=dim)
        cells = jnp.concatenate(
            [
                lax.ppermute(tail, axis, [(i, (i + 1) % count) for i in range(ends)]),
                cells,
                lax.ppermute(head, axis, [((i + 1) % count, i) for i in range(ends)]),
            ],
            axis=dim,
        )
    return cells


def tap_offsets():
    return [
        (first, second, third) for first in range(3) for second in range(3) for third in range(3)
    ]


def forward_taps(padded, weight, extent):
    rows_x, rows_y, depth = extent
    total = jnp.zeros((rows_x * rows_y * depth, weight.shape[2]), jnp.float32)
    for number, (first, second, third) in enumerate(tap_offsets()):
        window = padded[first : first + rows_x, second : second + rows_y, third : third + depth, :]
        total = total + jnp.dot(
            window.reshape(-1, window.shape[-1]), weight[number], preferred_element_type=jnp.float32
        )
    return total.reshape(rows_x, rows_y, depth, weight.shape[2])


def backward_taps(padded, weight, extent):
    rows_x, rows_y, depth = extent
    total = jnp.zeros((rows_x * rows_y * depth, weight.shape[1]), jnp.float32)
    for number, (first, second, third) in enumerate(tap_offsets()):
        window = padded[
            2 - first : 2 - first + rows_x,
            2 - second : 2 - second + rows_y,
            2 - third : 2 - third + depth,
            :,
        ]
        total = total + lax.dot_general(
            window.reshape(-1, window.shape[-1]),
            weight[number],
            (((1,), (1,)), ((), ())),
            preferred_element_type=jnp.float32,
        )
    return total.reshape(rows_x, rows_y, depth, weight.shape[1])


def weight_taps(padded, grads, extent):
    rows_x, rows_y, depth = extent
    flat_grads = grads.reshape(-1, grads.shape[-1])
    pieces = []
    for first, second, third in tap_offsets():
        window = padded[first : first + rows_x, second : second + rows_y, third : third + depth, :]
        pieces.append(
            lax.dot_general(
                window.reshape(-1, window.shape[-1]),
                flat_grads,
                (((0,), (0,)), ((), ())),
                preferred_element_type=jnp.float32,
            )
        )
    return jnp.stack(pieces)


def pool_cells(values):
    rows_x, rows_y, depth, width = values.shape
    blocks = values.astype(jnp.float32).reshape(
        rows_x // 2, 2, rows_y // 2, 2, depth // 2, 2, width
    )
    return jnp.mean(blocks, axis=(1, 3, 5)).astype(jnp.bfloat16)


def spread_cells(values):
    rows_x, rows_y, depth, width = values.shape
    wide = jnp.broadcast_to(
        values[:, None, :, None, :, None, :], (rows_x, 2, rows_y, 2, depth, 2, width)
    )
    return wide.reshape(rows_x * 2, rows_y * 2, depth * 2, width)


def silu_slope(values):
    sigma = jax.nn.sigmoid(values)
    return sigma * (1.0 + values * (1.0 - sigma))


def fine_rim(values):
    extended = padded_2(values, ((SP, 0), (FL, 1)), 1)
    return jnp.pad(extended, ((0, 0), (0, 0), (1, 1), (0, 0)))


def coarse_rim_pad(extended):
    return jnp.pad(extended, ((0, 0), (1, 1), (1, 1), (0, 0)))


def body(inputs, weight_fine, weight_coarse, cotangent):
    rows_x, rows_y, depth, width = inputs.shape
    fine_extent = (rows_x, rows_y, depth)
    cells = rows_x * 16 * rows_y * 8 * depth
    core = lax.axis_index("c")
    padded_cot = coarse_rim_pad(padded_2(cotangent, ((SP, 0),), 1))
    padded_in = fine_rim(inputs)
    coarse_extent = cotangent.shape[:3]
    partial_grad = backward_taps(padded_cot, weight_coarse, coarse_extent).astype(jnp.bfloat16)
    fine_pre = forward_taps(padded_in, weight_fine, fine_extent)
    fine_act = (fine_pre * jax.nn.sigmoid(fine_pre)).astype(jnp.bfloat16)
    pooled = pool_cells(fine_act)
    half = pooled.reshape(-1, width)
    parts = partial_grad.reshape(8, -1, width)
    sent = jnp.concatenate([jnp.broadcast_to(half[None], parts.shape), parts], axis=1)
    got = lax.all_to_all(sent, FL, 0, 0, tiled=True)
    gathered = got[:, : half.shape[0]].reshape(coarse_extent + (width,))
    pooled_grad = (
        got[:, half.shape[0] :].astype(jnp.float32).sum(0).astype(jnp.bfloat16).reshape(pooled.shape)
    )
    fine_grad = (
        spread_cells(pooled_grad.astype(jnp.float32)) * 0.125 * silu_slope(fine_pre)
    ).astype(jnp.bfloat16)
    fine_terms = weight_taps(padded_in, fine_grad, fine_extent).astype(jnp.bfloat16)
    fine_terms = fine_terms.reshape(8, 2, 8, -1, width)
    theirs = jnp.where(core == 0, fine_terms[:, 1], fine_terms[:, 0])
    mine = jnp.where(core == 0, fine_terms[:, 0], fine_terms[:, 1])
    arrived = lax.ppermute(theirs, "c", [(0, 1), (1, 0)])
    pair = (mine.astype(jnp.float32) + arrived.astype(jnp.float32)).astype(jnp.bfloat16)
    spread = lax.all_to_all(
        pair.reshape((64,) + pair.shape[2:]), ("x", "yh", "z", "yl"), 0, 0, tiled=True
    )
    grad_fine = spread.astype(jnp.float32).sum(0).reshape(-1) * (1.0 / math.sqrt(cells))
    grad_input = backward_taps(fine_rim(fine_grad), weight_fine, fine_extent).astype(jnp.bfloat16)

    flat = gathered.reshape(-1, width)
    pieces = []
    for first, second, third in tap_offsets():
        window = padded_cot[
            2 - first : 2 - first + 1, 2 - second : 2 - second + 32, 2 - third : 2 - third + 16, :
        ]
        pieces.append(
            lax.dot_general(
                flat,
                window.reshape(-1, window.shape[-1]),
                (((0,), (0,)), ((), ())),
                preferred_element_type=jnp.float32,
            )
        )
    coarse_terms = jnp.stack(pieces).astype(jnp.bfloat16).reshape(8, 2, -1, cotangent.shape[-1])
    theirs = jnp.where(core == 0, coarse_terms[:, 1], coarse_terms[:, 0])
    mine = jnp.where(core == 0, coarse_terms[:, 0], coarse_terms[:, 1])
    arrived = lax.ppermute(theirs, "c", [(0, 1), (1, 0)])
    pair = (mine.astype(jnp.float32) + arrived.astype(jnp.float32)).astype(jnp.bfloat16)
    spread = lax.all_to_all(pair, ("x", "yh"), 0, 0, tiled=True)
    grad_coarse = spread.astype(jnp.float32).sum(0) * (1.0 / math.sqrt(cells // 8))
    padded_pool = coarse_rim_pad(padded_2(gathered, ((SP, 0),), 1))
    coarse_out = forward_taps(padded_pool, weight_coarse, coarse_extent).astype(jnp.bfloat16)
    return (coarse_out, grad_input, grad_fine, grad_coarse)


SP = ("x", "yh", "c")
FL = ("z", "yl")


def solution(mesh):
    fine_mesh = jax.sharding.Mesh(mesh.devices.reshape(4, 2, 2, 4, 2), SP + FL)
    return jax.shard_map(
        body,
        mesh=fine_mesh,
        in_specs=(P(SP, FL, None, None), P(), P(None, None, FL), P(SP, None, None, FL)),
        out_specs=(P(SP, None, None, FL), P(SP, FL, None, None), P(SP + FL), P(SP, FL)),
        check_vma=False,
    )
```

```python
import functools
import math

import jax
import jax.numpy as jnp
from jax import lax
from jax.experimental import pallas as pl
from jax.experimental.pallas import tpu as pltpu
from jax.sharding import PartitionSpec as P

SP = ("x", "yh", "c")
FL = ("z", "yl")
BF = jnp.bfloat16
F32 = jnp.float32
VMEM = pl.BlockSpec(memory_space=pltpu.VMEM)
SMEM = pl.BlockSpec(memory_space=pltpu.SMEM)
ANY = pl.BlockSpec(memory_space=pl.ANY)


def call(kernel, out_shape, in_specs, scratch=(), flops=0, moved=0, limit=24):
    return pl.pallas_call(
        kernel,
        out_shape=out_shape,
        in_specs=in_specs,
        out_specs=jax.tree.map(lambda _: VMEM, out_shape),
        scratch_shapes=list(scratch),
        compiler_params=pltpu.CompilerParams(vmem_limit_bytes=limit * 2**20),
        cost_estimate=pl.CostEstimate(flops=flops, bytes_accessed=moved, transcendentals=0),
    )


def along_depth(rows, order):
    count, depth, width = rows.shape
    flat = rows.astype(F32).reshape(count * depth, width)
    place = lax.broadcasted_iota(jnp.int32, flat.shape, 0) & (depth - 1)
    before = jnp.where(place == 0, 0.0, pltpu.roll(flat, 1, 0)).astype(BF)
    after = jnp.where(place == depth - 1, 0.0, pltpu.roll(flat, count * depth - 1, 0)).astype(BF)
    middle = flat.astype(BF)
    trio = (before, middle, after) if order > 0 else (after, middle, before)
    return jnp.concatenate(trio, axis=1).reshape(count, depth, 3 * width)


def fetch(source, target, sems):
    copies = [
        pltpu.make_async_copy(source.at[k], target.at[k], sems.at[k]) for k in range(sems.shape[0])
    ]
    for copy in copies:
        copy.start()
    return copies


def assemble(own, xlo, xhi, ylo, yhi, wide, order):
    planes = (xlo[0], own[0], own[1], xhi[0])
    for x in range(4):
        rows = jnp.concatenate([ylo[x : x + 1], planes[x], yhi[x : x + 1]], axis=0)
        wide[x] = along_depth(rows, order)


def fine_forward_kernel(own, xlo, xhi, ylo, yhi, w_hbm, pooled, slope, wide, w, pre, sums, sems):
    copies = fetch(w_hbm, w, sems)
    assemble(own, xlo, xhi, ylo, yhi, wide, 1)
    for k in range(9):
        a, b = divmod(k, 3)
        copies[k].wait()
        window = wide[a : a + 2, b : b + 8].reshape(512, 768)
        term = jnp.dot(window, w[k], preferred_element_type=F32)
        pre[...] = term if k == 0 else pre[...] + term
    for y in range(4):
        total = jnp.zeros((32, 256), F32)
        for x in range(2):
            for half in range(2):
                at = x * 256 + (2 * y + half) * 32
                value = pre[at : at + 32]
                sigma = 1.0 / (1.0 + jnp.exp(-value))
                total = total + (value * sigma).astype(BF).astype(F32)
                slope[at : at + 32] = 0.125 * sigma * (1.0 + value * (1.0 - sigma))
        sums[0, y * 32 : y * 32 + 32] = total[:, :128]
        sums[1, y * 32 : y * 32 + 32] = total[:, 128:]
    for side in range(2):
        even = sums[side, pl.ds(0, 64, stride=2)]
        odd = sums[side, pl.ds(1, 64, stride=2)]
        pooled[:, side * 128 : side * 128 + 128] = ((even + odd) * 0.125).astype(BF)


def fine_forward(own, xlo, xhi, ylo, yhi, weight):
    return call(
        fine_forward_kernel,
        (jax.ShapeDtypeStruct((64, 256), BF), jax.ShapeDtypeStruct((512, 256), F32)),
        [VMEM] * 5 + [ANY],
        [
            pltpu.VMEM((4, 10, 32, 768), BF),
            pltpu.VMEM((9, 768, 256), BF),
            pltpu.VMEM((512, 256), F32),
            pltpu.VMEM((2, 128, 128), F32),
            pltpu.SemaphoreType.DMA((9,)),
        ],
        flops=2 * 512 * 6912 * 256,
        moved=5 * 2**20,
    )(own, xlo, xhi, ylo, yhi, weight.reshape(9, 768, 256))


def turn_kernel(own, xlo, xhi, ylo, yhi, turned):
    planes = (xlo[0], own[0], own[1], xhi[0])
    for x in range(4):
        rows = jnp.concatenate([ylo[x : x + 1], planes[x], yhi[x : x + 1]], axis=0)
        wide = along_depth(rows, 1)
        for b in range(3):
            for c in range(3):
                window = wide[b : b + 8, :, c * 256 : c * 256 + 256].reshape(256, 256)
                turned[b * 3 + c, :, x * 256 : x * 256 + 256] = window.T


def turn(own, xlo, xhi, ylo, yhi):
    return call(
        turn_kernel,
        jax.ShapeDtypeStruct((9, 256, 1024), BF),
        [VMEM] * 5,
        flops=2 * 512 * 6912 * 64,
        moved=6 * 2**20,
    )(own, xlo, xhi, ylo, yhi)


def fine_weight_kernel(core, parts, slope, turned, grad, terms, spread, total):
    summed = parts[0].astype(F32)
    for k in range(1, 8):
        summed = summed + parts[k].astype(F32)
    summed = summed.astype(BF).astype(F32)
    for side in range(2):
        half = summed[:, side * 128 : side * 128 + 128]
        spread[side, pl.ds(0, 64, stride=2)] = half
        spread[side, pl.ds(1, 64, stride=2)] = half
    for y in range(4):
        wide = jnp.concatenate([spread[0, y * 32 : y * 32 + 32], spread[1, y * 32 : y * 32 + 32]], axis=1)
        for x in range(2):
            for half in range(2):
                at = x * 256 + (2 * y + half) * 32
                grad[at : at + 32] = (wide * slope[at : at + 32]).astype(BF)
    right = grad[...]
    me = core[0]
    done = 0
    for tap in range(27):
        a, bc = divmod(tap, 9)
        total[tap * 256 : tap * 256 + 256] = jnp.dot(
            turned[bc, :, a * 256 : a * 256 + 512], right, preferred_element_type=F32
        )
        while done < 128 and (done + 1) * 54 <= (tap + 1) * 256:
            block, f = divmod(done, 8)
            k, c = divmod(block, 2)
            value = total[done * 54 : done * 54 + 54].astype(BF)
            terms[lax.rem(me + c, 2), k * 8 + f] = value
            done += 1


def fine_weight(core, parts, slope, turned):
    return call(
        fine_weight_kernel,
        (jax.ShapeDtypeStruct((512, 256), BF), jax.ShapeDtypeStruct((2, 64, 54, 256), BF)),
        [SMEM] + [VMEM] * 3,
        [pltpu.VMEM((2, 128, 128), F32), pltpu.VMEM((6912, 256), F32)],
        flops=2 * 512 * 6912 * 256,
        moved=9 * 2**20,
        limit=32,
    )(core, parts, slope, turned)


def fine_back_kernel(own, xlo, xhi, ylo, yhi, w_hbm, out, wide, w, total, sems):
    copies = fetch(w_hbm, w, sems)
    assemble(own, xlo, xhi, ylo, yhi, wide, -1)
    for k in range(9):
        a, b = divmod(k, 3)
        copies[k].wait()
        window = wide[2 - a : 4 - a, 2 - b : 10 - b].reshape(512, 768)
        right = jnp.concatenate([w[k, 0], w[k, 1], w[k, 2]], axis=1)
        term = lax.dot_general(window, right, (((1,), (1,)), ((), ())), preferred_element_type=F32)
        total[...] = term if k == 0 else total[...] + term
    out[...] = total[...].astype(BF)


def fine_back(own, xlo, xhi, ylo, yhi, weight):
    return call(
        fine_back_kernel,
        jax.ShapeDtypeStruct((512, 256), BF),
        [VMEM] * 5 + [ANY],
        [
            pltpu.VMEM((4, 10, 32, 768), BF),
            pltpu.VMEM((9, 3, 256, 256), BF),
            pltpu.VMEM((512, 256), F32),
            pltpu.SemaphoreType.DMA((9,)),
        ],
        flops=2 * 512 * 6912 * 256,
        moved=5 * 2**20,
    )(own, xlo, xhi, ylo, yhi, weight.reshape(9, 3, 256, 256))


def pad_rows(plane):
    edge = jnp.zeros((1,) + plane.shape[1:], plane.dtype)
    return jnp.concatenate([edge, plane, edge], axis=0)


def coarse_back_kernel(own, xlo, xhi, w, partial, wide):
    for x, plane in enumerate((xlo, own, xhi)):
        wide[x] = along_depth(pad_rows(plane[0]), -1)
    total = None
    for k in range(9):
        a, b = divmod(k, 3)
        window = wide[2 - a, 2 - b : 34 - b].reshape(512, 192)
        term = jnp.dot(window, w[k], preferred_element_type=F32)
        total = term if k == 0 else total + term
    partial[...] = total.astype(BF)


def coarse_back(own, xlo, xhi, weight):
    turned = jnp.swapaxes(weight, 1, 2).reshape(9, 192, 256)
    return call(
        coarse_back_kernel,
        (jax.ShapeDtypeStruct((512, 256), BF), jax.ShapeDtypeStruct((3, 34, 16, 192), BF)),
        [VMEM] * 4,
        flops=2 * 512 * 1728 * 256,
        moved=3 * 2**20,
    )(own, xlo, xhi, turned)


def coarse_weight_kernel(core, pooled, wide, terms, total):
    left = pooled[...].T
    for k in range(9):
        a, b = divmod(k, 3)
        window = wide[2 - a, 2 - b : 34 - b].reshape(512, 192)
        term = jnp.dot(left, window, preferred_element_type=F32)
        for c in range(3):
            at = (3 * k + c) * 256
            total[at : at + 256] = term[:, c * 64 : c * 64 + 64]
    me = core[0]
    for block in range(16):
        k, c = divmod(block, 2)
        at = block * 432
        upper = total[at : at + 224]
        lower = jnp.concatenate([total[at + 224 : at + 432], jnp.zeros((16, 64), F32)], axis=0)
        terms[lax.rem(me + c, 2), k] = jnp.concatenate([upper, lower], axis=1).astype(BF)


def coarse_weight(core, pooled, wide):
    return call(
        coarse_weight_kernel,
        jax.ShapeDtypeStruct((2, 8, 224, 128), BF),
        [SMEM, VMEM, VMEM],
        [pltpu.VMEM((6912, 64), F32)],
        flops=2 * 512 * 1728 * 256,
        moved=3 * 2**20,
    )(core, pooled, wide)


def coarse_forward_kernel(own, xlo, xhi, w, out, wide):
    for x, plane in enumerate((xlo, own, xhi)):
        wide[x] = along_depth(pad_rows(plane[...]), 1)
    total = None
    for k in range(9):
        a, b = divmod(k, 3)
        window = wide[a, b : b + 32].reshape(512, 768)
        term = jnp.dot(window, w[k], preferred_element_type=F32)
        total = term if k == 0 else total + term
    out[...] = total.astype(BF)


def coarse_forward(own, xlo, xhi, weight):
    return call(
        coarse_forward_kernel,
        jax.ShapeDtypeStruct((512, 64), BF),
        [VMEM] * 4,
        [pltpu.VMEM((3, 34, 16, 768), BF)],
        flops=2 * 512 * 6912 * 128,
        moved=3 * 2**20,
    )(own, xlo, xhi, weight.reshape(9, 768, 64))


def fine_sum_kernel(scale, parts, out):
    total = parts[0].astype(F32)
    for k in range(1, 64):
        total = total + parts[k].astype(F32)
    out[...] = total * scale


def coarse_sum_kernel(scale, parts, out):
    total = parts[0].astype(F32)
    for k in range(1, 8):
        total = total + parts[k].astype(F32)
    total = total * scale
    out[:224] = total[:, :64]
    out[224:] = total[:208, 64:]


def halo(block, axis, dim):
    count = lax.axis_size(axis)
    size = block.shape[dim]
    low = lax.slice_in_dim(block, 0, 1, axis=dim)
    high = lax.slice_in_dim(block, size - 1, size, axis=dim)
    return (
        lax.ppermute(high, axis, [(i, i + 1) for i in range(count - 1)]),
        lax.ppermute(low, axis, [(i + 1, i) for i in range(count - 1)]),
    )


def fine_halo(block):
    xlo, xhi = halo(block, SP, 0)
    low = jnp.concatenate([xlo[:, :1], block[:, :1], xhi[:, :1]], axis=0)
    high = jnp.concatenate([xlo[:, -1:], block[:, -1:], xhi[:, -1:]], axis=0)
    count = lax.axis_size(FL)
    ylo = lax.ppermute(high, FL, [(i, i + 1) for i in range(count - 1)])
    yhi = lax.ppermute(low, FL, [(i + 1, i) for i in range(count - 1)])
    return block, xlo, xhi, ylo[:, 0], yhi[:, 0]


def pair_sum(terms):
    arrived = lax.ppermute(terms[1], "c", [(0, 1), (1, 0)])
    return (terms[0].astype(F32) + arrived.astype(F32)).astype(BF)


def body(inputs, weight_fine, weight_coarse, cotangent):
    cells = 65536
    core = lax.axis_index("c").astype(jnp.int32).reshape(1)
    cot_lo, cot_hi = halo(cotangent, SP, 0)
    blocks = fine_halo(inputs)
    partial, wide_cot = coarse_back(cotangent, cot_lo, cot_hi, weight_coarse)
    pooled, slope = fine_forward(*blocks, weight_fine)
    sent = jnp.concatenate(
        [jnp.broadcast_to(pooled[None], (8, 64, 256)), partial.reshape(8, 64, 256)], axis=1
    )
    got = lax.all_to_all(sent, FL, 0, 0, tiled=True)
    turned = turn(*blocks)
    grad, terms = fine_weight(core, got[:, 64:], slope, turned)
    spread = lax.all_to_all(pair_sum(terms), ("x", "yh", "z", "yl"), 0, 0, tiled=True)

    gathered = got[:, :64].reshape(512, 256)
    coarse_terms = coarse_weight(core, gathered, wide_cot)
    coarse_spread = lax.all_to_all(pair_sum(coarse_terms), ("x", "yh"), 0, 0, tiled=True)
    grad_input = fine_back(*fine_halo(grad.reshape(2, 8, 32, 256)), weight_fine)
    slab = gathered.reshape(32, 16, 256)
    pool_lo, pool_hi = halo(slab[None], SP, 0)
    coarse_out = coarse_forward(slab, pool_lo[0], pool_hi[0], weight_coarse)
    grad_coarse = call(
        functools.partial(coarse_sum_kernel, 1.0 / math.sqrt(cells // 8)),
        jax.ShapeDtypeStruct((432, 64), F32),
        [VMEM],
    )(coarse_spread)
    grad_fine = call(
        functools.partial(fine_sum_kernel, 1.0 / math.sqrt(cells)),
        jax.ShapeDtypeStruct((54, 256), F32),
        [VMEM],
    )(spread)
    return (
        coarse_out.reshape(1, 32, 16, 64),
        grad_input.reshape(2, 8, 32, 256),
        grad_fine.reshape(-1),
        grad_coarse,
    )


def solution(mesh):
    fine_mesh = jax.sharding.Mesh(mesh.devices.reshape(4, 2, 2, 4, 2), SP + FL)
    return jax.shard_map(
        body,
        mesh=fine_mesh,
        in_specs=(P(SP, FL, None, None), P(), P(None, None, FL), P(SP, None, None, FL)),
        out_specs=(P(SP, None, None, FL), P(SP, FL, None, None), P(SP + FL), P(SP, FL)),
        check_vma=False,
    )
```

```python
import functools
import math

import jax
import jax.numpy as jnp
from jax import lax
from jax.experimental import pallas as pl
from jax.experimental.pallas import tpu as pltpu
from jax.sharding import PartitionSpec as P

SP = ("x", "yh", "c")
FL = ("z", "yl")
BF = jnp.bfloat16
F32 = jnp.float32
VMEM = pl.BlockSpec(memory_space=pltpu.VMEM)
SMEM = pl.BlockSpec(memory_space=pltpu.SMEM)
SWAP = [(0, 1), (1, 0)]


def call(kernel, out_shape, in_specs, scratch=(), limit=12, flops=2**20):
    return pl.pallas_call(
        kernel,
        out_shape=out_shape,
        in_specs=in_specs,
        out_specs=jax.tree.map(lambda _: VMEM, out_shape),
        scratch_shapes=list(scratch),
        compiler_params=pltpu.CompilerParams(vmem_limit_bytes=limit * 2**20),
        cost_estimate=pl.CostEstimate(flops=flops, bytes_accessed=2**16, transcendentals=0),
    )


def array(*shape, dtype=BF):
    return jax.ShapeDtypeStruct(shape, dtype)


def along_depth(rows, order):
    count, depth, width = rows.shape
    flat = rows.astype(F32).reshape(count * depth, width)
    place = lax.broadcasted_iota(jnp.int32, flat.shape, 0) & (depth - 1)
    before = jnp.where(place == 0, 0.0, pltpu.roll(flat, 1, 0)).astype(BF)
    after = jnp.where(place == depth - 1, 0.0, pltpu.roll(flat, count * depth - 1, 0)).astype(BF)
    middle = flat.astype(BF)
    trio = (before, middle, after) if order > 0 else (after, middle, before)
    return jnp.concatenate(trio, axis=1).reshape(count, depth, 3 * width)


def pad_rows(plane):
    edge = jnp.zeros((1,) + plane.shape[1:], plane.dtype)
    return jnp.concatenate([edge, plane, edge], axis=0)


def unpacked(block):
    strips = [block[:, 64 * k : 64 * k + 64] for k in range(4)]
    return jnp.concatenate(strips, axis=0).reshape(32, 16, 64)


def pack_kernel(own, cot, up, down):
    flat = cot[0].reshape(512, 64)
    packed = jnp.concatenate([flat[128 * k : 128 * k + 128] for k in range(4)], axis=1)
    up[:256] = own[1].reshape(256, 256)
    down[:256] = own[0].reshape(256, 256)
    up[256:] = packed
    down[256:] = packed


def plane_of(own, lo, hi, x):
    if x == 0 or x == 3:
        return (lo if x == 0 else hi)[:256].reshape(8, 32, 256)
    return own[x - 1]


def edge_kernel(own, lo, hi, low, high):
    for x in range(4):
        plane = plane_of(own, lo, hi, x)
        low[32 * x : 32 * x + 32] = plane[0]
        high[32 * x : 32 * x + 32] = plane[7]


def whole_plane(own, lo, hi, ylo, yhi, x):
    rows = slice(32 * x, 32 * x + 32)
    return jnp.concatenate([ylo[rows][None], plane_of(own, lo, hi, x), yhi[rows][None]], axis=0)


def coarse_back_kernel(cot, lo, hi, w, partial, wide):
    planes = (unpacked(lo[256:384]), cot[0], unpacked(hi[256:384]))
    for x in range(3):
        wide[x] = along_depth(pad_rows(planes[x]), -1)
    total = None
    for k in range(9):
        a, b = divmod(k, 3)
        window = wide[2 - a, 2 - b : 34 - b].reshape(512, 192)
        term = jnp.dot(window, w[k], preferred_element_type=F32)
        total = term if k == 0 else total + term
    partial[...] = total.astype(BF)


def fine_forward_kernel(place, own, lo, hi, ylo, yhi, w, pooled, slope, far, wide, pre, sums):
    for x in range(4):
        plane = whole_plane(own, lo, hi, ylo, yhi, x)
        wide[x] = along_depth(plane, 1)

        @pl.when(place[0] == x // 2)
        def _():
            far[320 * (x % 2) : 320 * (x % 2) + 320] = plane.reshape(320, 256)

    far[640:] = jnp.where(place[0] == 0, lo[256:384], hi[256:384])
    for k in range(9):
        a, b = divmod(k, 3)
        window = wide[a : a + 2, b : b + 8].reshape(512, 768)
        term = jnp.dot(window, w[k], preferred_element_type=F32)
        pre[...] = term if k == 0 else pre[...] + term
    for y in range(4):
        total = jnp.zeros((32, 256), F32)
        for x in range(2):
            for half in range(2):
                at = x * 256 + (2 * y + half) * 32
                value = pre[at : at + 32]
                sigma = 1.0 / (1.0 + jnp.exp(-value))
                total = total + (value * sigma).astype(BF).astype(F32)
                slope[at : at + 32] = 0.125 * sigma * (1.0 + value * (1.0 - sigma))
        sums[0, y * 32 : y * 32 + 32] = total[:, :128]
        sums[1, y * 32 : y * 32 + 32] = total[:, 128:]
    for side in range(2):
        even = sums[side, pl.ds(0, 64, stride=2)]
        odd = sums[side, pl.ds(1, 64, stride=2)]
        pooled[:, side * 128 : side * 128 + 128] = ((even + odd) * 0.125).astype(BF)


def fine_grad_kernel(place, parts, slope, pooled, grad, sent, spread):
    summed = parts[0].astype(F32)
    for k in range(1, 8):
        summed = summed + parts[k].astype(F32)
    summed = summed.astype(BF).astype(F32)
    for side in range(2):
        half = summed[:, side * 128 : side * 128 + 128]
        spread[side, pl.ds(0, 64, stride=2)] = half
        spread[side, pl.ds(1, 64, stride=2)] = half
    for y in range(4):
        wide = jnp.concatenate([spread[0, y * 32 : y * 32 + 32], spread[1, y * 32 : y * 32 + 32]], axis=1)
        for x in range(2):
            for half in range(2):
                at = x * 256 + (2 * y + half) * 32
                grad[at : at + 32] = (wide * slope[at : at + 32]).astype(BF)
    low = jnp.concatenate([grad[0:32], grad[256:288]], axis=0)
    high = jnp.concatenate([grad[224:256], grad[480:512]], axis=0)
    for k in range(8):
        sent[k, :64] = pooled[...]
        sent[k, 64:] = jnp.where(k < place[3], low, high)


def fine_weight_kernel(
    place, own, lo, hi, ylo, yhi, far, grad, other, terms, wide, turned, total
):
    for core in range(2):

        @pl.when(place[0] == core)
        def _():
            planes, windows = set(), set()

            def prepare(bc, slot):
                if (bc, slot) in windows:
                    return
                windows.add((bc, slot))
                if slot not in planes:
                    planes.add(slot)
                    x = slot - 2 * core
                    if 0 <= x < 4:
                        rows = whole_plane(own, lo, hi, ylo, yhi, x)
                    else:
                        at = 320 * (slot % 2)
                        rows = far[at : at + 320].reshape(10, 32, 256)
                    wide[slot] = along_depth(rows, 1)
                b, c = divmod(bc, 3)
                window = wide[slot, b : b + 8, :, c * 256 : c * 256 + 256]
                turned[bc, slot] = window.reshape(256, 256).T

            pair = (grad, other) if core == 0 else (other, grad)
            right = jnp.concatenate([pair[0][...], pair[1][...]], axis=0)
            for k in range(8):
                at = 432 * (2 * k + core)
                end = at + 432
                pieces = []
                while at < end:
                    tap, low = divmod(at, 256)
                    high = min(256, low + end - at)
                    a, bc = divmod(tap, 9)
                    for plane in range(4):
                        prepare(bc, a + plane)
                    strips = [turned[bc, a + plane, low:high] for plane in range(4)]
                    pieces.append(jnp.concatenate(strips, axis=1))
                    at += high - low
                left = jnp.concatenate(pieces, axis=0)
                total[k % 2] = jnp.dot(left, right, preferred_element_type=F32)
                for f in range(8):
                    terms[k * 8 + f] = total[k % 2, f * 54 : f * 54 + 54].astype(BF)


def grad_plane(place, grad, got, x):
    below = got[jnp.maximum(place[3] - 1, 0), 64 + 32 * x : 96 + 32 * x]
    above = got[jnp.minimum(place[3] + 1, 7), 64 + 32 * x : 96 + 32 * x]
    below = jnp.where(place[3] > 0, below, jnp.zeros_like(below))
    above = jnp.where(place[3] < 7, above, jnp.zeros_like(above))
    middle = grad[256 * x : 256 * x + 256].reshape(8, 32, 256)
    return jnp.concatenate([below[None], middle, above[None]], axis=0)


def ship_kernel(place, grad, got, up, down, slab):
    down[:320] = grad_plane(place, grad, got, 0).reshape(320, 256)
    up[:320] = grad_plane(place, grad, got, 1).reshape(320, 256)
    for k in range(8):
        up[320 + 64 * k : 384 + 64 * k] = got[k, :64]
        down[320 + 64 * k : 384 + 64 * k] = got[k, :64]
        slab[64 * k : 64 * k + 64] = got[k, :64]


def fine_back_kernel(up, down, lo, hi, w, out, wide, total):
    for x, plane in enumerate((lo, down, up, hi)):
        wide[x] = along_depth(plane[:320].reshape(10, 32, 256), -1)
    for k in range(9):
        a, b = divmod(k, 3)
        window = wide[2 - a : 4 - a, 2 - b : 10 - b].reshape(512, 768)
        right = jnp.concatenate([w[k, 0], w[k, 1], w[k, 2]], axis=1)
        term = lax.dot_general(window, right, (((1,), (1,)), ((), ())), preferred_element_type=F32)
        total[...] = term if k == 0 else total[...] + term
    out[...] = total[...].astype(BF)


def coarse_weight_kernel(place, slab, other, wide, far, terms, outer, total):
    outer[...] = along_depth(pad_rows(unpacked(far[640:768])), -1)
    left = jnp.concatenate([slab[...].T, other[...].T], axis=1)
    for core in range(2):

        @pl.when(place[0] == core)
        def _():
            for k in range(9):
                a, b = divmod(k, 3)
                rows = slice(2 - b, 34 - b)
                at = 2 - a + (1 if core == 0 else -1)
                across = wide[at, rows] if 0 <= at < 3 else outer[rows]
                right = jnp.concatenate(
                    [wide[2 - a, rows].reshape(512, 192), across.reshape(512, 192)], axis=0
                )
                term = jnp.dot(left, right, preferred_element_type=F32)
                for c in range(3):
                    row = (3 * k + c) * 256
                    total[row : row + 256] = term[:, c * 64 : c * 64 + 64]
            for block in range(8):
                x, yh = divmod(block, 2)
                row = (2 * block + core) * 432
                upper = total[row : row + 224]
                lower = jnp.concatenate(
                    [total[row + 224 : row + 432], jnp.zeros((16, 64), F32)], axis=0
                )
                at = lax.rem(4 + x - place[2], 4) * 2 + lax.rem(place[1] + yh, 2)
                terms[at] = jnp.concatenate([upper, lower], axis=1).astype(BF)


def coarse_forward_kernel(slab, lo, hi, w, out, wide):
    for x, plane in enumerate((lo, slab, hi)):
        wide[x] = along_depth(pad_rows(plane[320:832].reshape(32, 16, 256)), 1)
    total = None
    for k in range(9):
        a, b = divmod(k, 3)
        window = wide[a, b : b + 32].reshape(512, 768)
        turned = w[k].T
        right = jnp.concatenate([turned[:, 64 * c : 64 * c + 64] for c in range(3)], axis=0)
        term = jnp.dot(window, right, preferred_element_type=F32)
        total = term if k == 0 else total + term
    out[...] = total.astype(BF)


def fine_sum_kernel(scale, parts, out):
    total = parts[0].astype(F32)
    for k in range(1, 64):
        total = total + parts[k].astype(F32)
    total = total * scale
    out[pl.ds(0, 54, stride=2)] = total[:, :128]
    out[pl.ds(1, 54, stride=2)] = total[:, 128:]


def quad_kernel(own, first, second, third, out):
    total = own[...].astype(F32) + first[...].astype(F32)
    total = total + second[...].astype(F32) + third[...].astype(F32)
    out[...] = total.astype(BF)


def coarse_sum_kernel(scale, own, other, out):
    total = own[:224].astype(F32) + other[...].astype(F32)
    total = total * scale
    out[...] = jnp.concatenate([total[:, :64], total[:208, 64:]], axis=0).T


def swap_sides(up, down, axis):
    steps = range(lax.axis_size(axis) - 1)
    return (
        lax.ppermute(up, axis, [(i, i + 1) for i in steps]),
        lax.ppermute(down, axis, [(i + 1, i) for i in steps]),
    )


def body(inputs, weight_fine, weight_coarse, cotangent):
    cells = 65536
    place = [lax.axis_index(name) for name in ("c", "yh", "x", FL)]
    place = jnp.stack(place).astype(jnp.int32)
    turned_coarse = jnp.swapaxes(weight_coarse, 1, 2).reshape(9, 192, 256)

    pack = call(pack_kernel, (array(384, 256), array(384, 256)), [VMEM] * 2, limit=60)
    lo, hi = swap_sides(*pack(inputs, cotangent), SP)
    edge = call(edge_kernel, (array(128, 256), array(128, 256)), [VMEM] * 3)
    low, high = edge(inputs, lo, hi)
    ylo, yhi = swap_sides(high, low, FL)
    partial, wide_cot = call(
        coarse_back_kernel,
        (array(512, 256), array(3, 34, 16, 192)),
        [VMEM] * 4,
        limit=60,
    )(cotangent, lo, hi, turned_coarse)
    parts = lax.all_to_all(partial.reshape(8, 64, 256), FL, 0, 0, tiled=True)
    parts, ylo, yhi = lax.optimization_barrier((parts, ylo, yhi))
    blocks = (inputs, lo, hi, ylo, yhi)
    pooled, slope, far = call(
        fine_forward_kernel,
        (array(64, 256), array(512, 256, dtype=F32), array(768, 256)),
        [SMEM] + [VMEM] * 6,
        [
            pltpu.VMEM((4, 10, 32, 768), BF),
            pltpu.VMEM((512, 256), F32),
            pltpu.VMEM((2, 128, 128), F32),
        ],
    )(place, *blocks, weight_fine.reshape(9, 768, 256))
    grad, sent = call(
        fine_grad_kernel,
        (array(512, 256), array(8, 128, 256)),
        [SMEM] + [VMEM] * 3,
        [pltpu.VMEM((2, 128, 128), F32)],
    )(place, parts, slope, pooled)
    far = lax.ppermute(far, "c", SWAP)
    got = lax.all_to_all(sent, FL, 0, 0, tiled=True)
    terms = call(
        fine_weight_kernel,
        array(64, 54, 256),
        [SMEM] + [VMEM] * 8,
        [
            pltpu.VMEM((6, 10, 32, 768), BF),
            pltpu.VMEM((9, 6, 256, 256), BF),
            pltpu.VMEM((2, 432, 256), F32),
        ],
        limit=24,
    )(place, *blocks, far, grad, lax.ppermute(grad, "c", SWAP))
    terms, got = lax.optimization_barrier((terms, got))
    shapes = (array(832, 256), array(832, 256), array(512, 256))
    up, down, slab = call(ship_kernel, shapes, [SMEM] + [VMEM] * 2)(place, grad, got)
    terms, up, down, slab = lax.optimization_barrier((terms, up, down, slab))
    across = lax.ppermute(slab, "c", SWAP)
    lo, hi = swap_sides(up, down, SP)
    spread = lax.all_to_all(terms, ("x", "yh", "z", "yl"), 0, 0, tiled=True)

    coarse_terms = call(
        coarse_weight_kernel,
        array(8, 224, 128),
        [SMEM] + [VMEM] * 4,
        [pltpu.VMEM((34, 16, 192), BF), pltpu.VMEM((6912, 64), F32)],
    )(place, slab, across, wide_cot, far)
    coarse_terms = coarse_terms.reshape(4, 448, 128)
    arrived = [
        lax.ppermute(coarse_terms[step], "x", [(i, (i + step) % 4) for i in range(4)])
        for step in range(1, 4)
    ]
    coarse_terms = call(quad_kernel, array(448, 128), [VMEM] * 4)(coarse_terms[0], *arrived)
    arrived = lax.ppermute(coarse_terms[224:], "yh", SWAP)
    grad_input = call(
        fine_back_kernel,
        array(512, 256),
        [VMEM] * 5,
        [pltpu.VMEM((4, 10, 32, 768), BF), pltpu.VMEM((512, 256), F32)],
        flops=2**31,
    )(up, down, lo, hi, weight_fine.reshape(9, 3, 256, 256))
    coarse_out = call(
        coarse_forward_kernel,
        array(512, 64),
        [VMEM] * 4,
        [pltpu.VMEM((3, 34, 16, 768), BF)],
        flops=2**31,
    )(up, lo, hi, turned_coarse)
    grad_coarse = call(
        functools.partial(coarse_sum_kernel, 1.0 / math.sqrt(cells // 8)),
        array(64, 432, dtype=F32),
        [VMEM] * 2,
    )(coarse_terms, arrived)
    grad_fine = call(
        functools.partial(fine_sum_kernel, 1.0 / math.sqrt(cells)),
        array(108, 128, dtype=F32),
        [VMEM],
    )(spread)
    return (
        coarse_out.reshape(1, 32, 16, 64),
        grad_input.reshape(2, 8, 32, 256),
        grad_fine.reshape(-1),
        grad_coarse.T,
    )


def solution(mesh):
    fine_mesh = jax.sharding.Mesh(mesh.devices.reshape(4, 2, 2, 4, 2), SP + FL)
    return jax.shard_map(
        body,
        mesh=fine_mesh,
        in_specs=(P(SP, FL, None, None), P(), P(None, None, FL), P(SP, None, None, FL)),
        out_specs=(P(SP, None, None, FL), P(SP, FL, None, None), P(SP + FL), P(SP, FL)),
        check_vma=False,
    )
```

```python
import functools
import math

import jax
import jax.numpy as jnp
from jax import lax
from jax.experimental import pallas as pl
from jax.experimental.pallas import tpu as pltpu
from jax.sharding import PartitionSpec as P

SP = ("x", "yh", "c")
FL = ("z", "yl")
BF = jnp.bfloat16
F32 = jnp.float32
VMEM = pl.BlockSpec(memory_space=pltpu.VMEM)
SMEM = pl.BlockSpec(memory_space=pltpu.SMEM)
SWAP = [(0, 1), (1, 0)]


def call(kernel, out_shape, in_specs, scratch=(), limit=12, flops=2**20):
    return pl.pallas_call(
        kernel,
        out_shape=out_shape,
        in_specs=in_specs,
        out_specs=jax.tree.map(lambda _: VMEM, out_shape),
        scratch_shapes=list(scratch),
        compiler_params=pltpu.CompilerParams(vmem_limit_bytes=limit * 2**20),
        cost_estimate=pl.CostEstimate(flops=flops, bytes_accessed=2**16, transcendentals=0),
    )


def array(*shape, dtype=BF):
    return jax.ShapeDtypeStruct(shape, dtype)


def along_depth(rows, order):
    count, depth, width = rows.shape
    flat = rows.astype(F32).reshape(count * depth, width)
    place = lax.broadcasted_iota(jnp.int32, flat.shape, 0) & (depth - 1)
    before = jnp.where(place == 0, 0.0, pltpu.roll(flat, 1, 0)).astype(BF)
    after = jnp.where(place == depth - 1, 0.0, pltpu.roll(flat, count * depth - 1, 0)).astype(BF)
    middle = flat.astype(BF)
    trio = (before, middle, after) if order > 0 else (after, middle, before)
    return jnp.concatenate(trio, axis=1).reshape(count, depth, 3 * width)


def pad_rows(plane):
    edge = jnp.zeros((1,) + plane.shape[1:], plane.dtype)
    return jnp.concatenate([edge, plane, edge], axis=0)


def unpacked(block):
    strips = [block[:, 64 * k : 64 * k + 64] for k in range(4)]
    return jnp.concatenate(strips, axis=0).reshape(32, 16, 64)


def pack_kernel(own, cot, up, down):
    flat = cot[0].reshape(512, 64)
    packed = jnp.concatenate([flat[128 * k : 128 * k + 128] for k in range(4)], axis=1)
    up[:256] = own[1].reshape(256, 256)
    down[:256] = own[0].reshape(256, 256)
    up[256:] = packed
    down[256:] = packed


def plane_of(own, lo, hi, x):
    if x == 0 or x == 3:
        return (lo if x == 0 else hi)[:256].reshape(8, 32, 256)
    return own[x - 1]


def edge_kernel(own, lo, hi, low, high):
    for x in range(4):
        plane = plane_of(own, lo, hi, x)
        low[64 * x : 64 * x + 64] = plane[:2].reshape(64, 256)
        high[64 * x : 64 * x + 64] = plane[6:].reshape(64, 256)


def whole_plane(own, lo, hi, ylo, yhi, x):
    below = ylo[64 * x : 64 * x + 64].reshape(2, 32, 256)
    above = yhi[64 * x : 64 * x + 64].reshape(2, 32, 256)
    return jnp.concatenate([below, plane_of(own, lo, hi, x), above], axis=0)


def coarse_back_kernel(cot, lo, hi, w, partial, wide):
    planes = (unpacked(lo[256:384]), cot[0], unpacked(hi[256:384]))
    for x in range(3):
        wide[x] = along_depth(pad_rows(planes[x]), -1)
    total = None
    for k in range(9):
        a, b = divmod(k, 3)
        window = wide[2 - a, 2 - b : 34 - b].reshape(512, 192)
        term = jnp.dot(window, w[k], preferred_element_type=F32)
        total = term if k == 0 else total + term
    partial[...] = total.astype(BF)


def fine_forward_kernel(
    place, own, lo, hi, ylo, yhi, partial, w, sent, slope, far, wide, pre, sums, padded
):
    for x in range(4):
        plane = whole_plane(own, lo, hi, ylo, yhi, x)
        wide[x] = along_depth(plane, 1)

        @pl.when(place[0] == x // 2)
        def _():
            far[320 * (x % 2) : 320 * (x % 2) + 320] = plane[1:11].reshape(320, 256)

    far[640:] = jnp.where(place[0] == 0, lo[256:384], hi[256:384])
    for k in range(9):
        a, b = divmod(k, 3)
        window = wide[a : a + 2, b : b + 10].reshape(640, 768)
        term = jnp.dot(window, w[k], preferred_element_type=F32)
        pre[...] = term if k == 0 else pre[...] + term
    for y in range(6):
        total = jnp.zeros((32, 256), F32)
        for x in range(2):
            for row in (2 * y - 1, 2 * y):
                if 0 <= row < 10:
                    at = x * 320 + row * 32
                    value = pre[at : at + 32]
                    sigma = 1.0 / (1.0 + jnp.exp(-value))
                    total = total + (value * sigma).astype(BF).astype(F32)
                    slope[at : at + 32] = 0.125 * sigma * (1.0 + value * (1.0 - sigma))
        if 0 < y < 5:
            sums[0, y * 32 - 32 : y * 32] = total[:, :128]
            sums[1, y * 32 - 32 : y * 32] = total[:, 128:]
    pooled = []
    for side in range(2):
        even = sums[side, pl.ds(0, 64, stride=2)]
        odd = sums[side, pl.ds(1, 64, stride=2)]
        pooled.append(((even + odd) * 0.125).astype(BF))
    pooled = jnp.concatenate(pooled, axis=1)
    padded[:16] = jnp.zeros((16, 256), BF)
    padded[16:528] = partial[...]
    padded[528:] = jnp.zeros((16, 256), BF)
    for k in range(8):
        sent[k, :64] = pooled
        sent[k, 64:] = padded[64 * k : 64 * k + 96]


def fine_grad_kernel(place, got, slope, grad, up, down, slab, spread):
    for y in range(6):
        rows = slice(64 + 16 * y, 80 + 16 * y)
        total = got[0, rows].astype(F32)
        for k in range(1, 8):
            total = total + got[k, rows].astype(F32)
        total = total.astype(BF).astype(F32)
        if y == 0:
            total = jnp.where(place[3] > 0, total, 0.0)
        if y == 5:
            total = jnp.where(place[3] < 7, total, 0.0)
        for side in range(2):
            half = total[:, side * 128 : side * 128 + 128]
            spread[side, pl.ds(32 * y, 16, stride=2)] = half
            spread[side, pl.ds(32 * y + 1, 16, stride=2)] = half
        at = slice(y * 32, y * 32 + 32)
        wide = jnp.concatenate([spread[0, at], spread[1, at]], axis=1)
        for x, out in enumerate((down, up)):
            for row in (2 * y - 1, 2 * y):
                if 0 <= row < 10:
                    at = x * 320 + row * 32
                    value = (wide * slope[at : at + 32]).astype(BF)
                    out[row * 32 : row * 32 + 32] = value
                    if 0 < row < 9:
                        at = x * 256 + row * 32 - 32
                        grad[at : at + 32] = value
    for k in range(8):
        slab[64 * k : 64 * k + 64] = got[k, :64]


def fine_weight_kernel(
    place, own, lo, hi, ylo, yhi, far, grad, other, terms, wide, turned, total
):
    for core in range(2):

        @pl.when(place[0] == core)
        def _():
            planes, windows = set(), set()

            def prepare(bc, slot):
                if (bc, slot) in windows:
                    return
                windows.add((bc, slot))
                if slot not in planes:
                    planes.add(slot)
                    x = slot - 2 * core
                    if 0 <= x < 4:
                        rows = whole_plane(own, lo, hi, ylo, yhi, x)[1:11]
                    else:
                        at = 320 * (slot % 2)
                        rows = far[at : at + 320].reshape(10, 32, 256)
                    wide[slot] = along_depth(rows, 1)
                b, c = divmod(bc, 3)
                window = wide[slot, b : b + 8, :, c * 256 : c * 256 + 256]
                turned[bc, slot] = window.reshape(256, 256).T

            pair = (grad, other) if core == 0 else (other, grad)
            right = jnp.concatenate([pair[0][...], pair[1][...]], axis=0)
            for k in range(8):
                at = 432 * (2 * k + core)
                end = at + 432
                pieces = []
                while at < end:
                    tap, low = divmod(at, 256)
                    high = min(256, low + end - at)
                    a, bc = divmod(tap, 9)
                    for plane in range(4):
                        prepare(bc, a + plane)
                    strips = [turned[bc, a + plane, low:high] for plane in range(4)]
                    pieces.append(jnp.concatenate(strips, axis=1))
                    at += high - low
                left = jnp.concatenate(pieces, axis=0)
                total[k % 2] = jnp.dot(left, right, preferred_element_type=F32)
                for f in range(8):
                    terms[k * 8 + f] = total[k % 2, f * 54 : f * 54 + 54].astype(BF)


def fine_back_kernel(up, down, lo, hi, w, out, wide, total):
    for x, plane in enumerate((lo, down, up, hi)):
        wide[x] = along_depth(plane[...].reshape(10, 32, 256), -1)
    for k in range(9):
        a, b = divmod(k, 3)
        window = wide[2 - a : 4 - a, 2 - b : 10 - b].reshape(512, 768)
        right = jnp.concatenate([w[k, 0], w[k, 1], w[k, 2]], axis=1)
        term = lax.dot_general(window, right, (((1,), (1,)), ((), ())), preferred_element_type=F32)
        total[...] = term if k == 0 else total[...] + term
    out[...] = total[...].astype(BF)


def coarse_weight_kernel(place, slab, other, wide, far, terms, outer, total):
    outer[...] = along_depth(pad_rows(unpacked(far[640:768])), -1)
    left = jnp.concatenate([slab[...].T, other[...].T], axis=1)
    for core in range(2):

        @pl.when(place[0] == core)
        def _():
            for k in range(9):
                a, b = divmod(k, 3)
                rows = slice(2 - b, 34 - b)
                at = 2 - a + (1 if core == 0 else -1)
                across = wide[at, rows] if 0 <= at < 3 else outer[rows]
                right = jnp.concatenate(
                    [wide[2 - a, rows].reshape(512, 192), across.reshape(512, 192)], axis=0
                )
                term = jnp.dot(left, right, preferred_element_type=F32)
                for c in range(3):
                    row = (3 * k + c) * 256
                    total[row : row + 256] = term[:, c * 64 : c * 64 + 64]
            for block in range(8):
                x, yh = divmod(block, 2)
                row = (2 * block + core) * 432
                upper = total[row : row + 224]
                lower = jnp.concatenate(
                    [total[row + 224 : row + 432], jnp.zeros((16, 64), F32)], axis=0
                )
                at = lax.rem(4 + x - place[2], 4) * 2 + lax.rem(place[1] + yh, 2)
                terms[at] = jnp.concatenate([upper, lower], axis=1).astype(BF)


def packed(plane):
    return jnp.concatenate([plane[128 * k : 128 * k + 128] for k in range(4)], axis=1)


def coarse_forward_kernel(slab, w, own, up, down, wide):
    wide[...] = along_depth(pad_rows(slab[...].reshape(32, 16, 256)), 1)
    total = None
    for b in range(3):
        columns = []
        for a in range(3):
            turned = w[3 * a + b].T
            columns.append(
                jnp.concatenate([turned[:, 64 * c : 64 * c + 64] for c in range(3)], axis=0)
            )
        right = jnp.concatenate(columns, axis=1)
        window = wide[b : b + 32].reshape(512, 768)
        term = jnp.dot(window, right, preferred_element_type=F32)
        total = term if b == 0 else total + term
    up[...] = packed(total[:, :64]).astype(BF)
    own[...] = total[:, 64:128]
    down[...] = packed(total[:, 128:]).astype(BF)


def coarse_out_kernel(own, lo, hi, out):
    for k in range(4):
        rows, columns = slice(128 * k, 128 * k + 128), slice(64 * k, 64 * k + 64)
        total = own[rows] + lo[:, columns].astype(F32) + hi[:, columns].astype(F32)
        out[rows] = total.astype(BF)


def fine_sum_kernel(scale, parts, out):
    total = parts[0].astype(F32)
    for k in range(1, 64):
        total = total + parts[k].astype(F32)
    total = total * scale
    out[pl.ds(0, 54, stride=2)] = total[:, :128]
    out[pl.ds(1, 54, stride=2)] = total[:, 128:]


def quad_kernel(own, first, second, third, out):
    total = own[...].astype(F32) + first[...].astype(F32)
    total = total + second[...].astype(F32) + third[...].astype(F32)
    out[...] = total.astype(BF)


def coarse_sum_kernel(scale, own, other, out):
    total = own[:224].astype(F32) + other[...].astype(F32)
    total = total * scale
    out[...] = jnp.concatenate([total[:, :64], total[:208, 64:]], axis=0).T


def swap_sides(up, down, axis):
    steps = range(lax.axis_size(axis) - 1)
    return (
        lax.ppermute(up, axis, [(i, i + 1) for i in steps]),
        lax.ppermute(down, axis, [(i + 1, i) for i in steps]),
    )


def body(inputs, weight_fine, weight_coarse, cotangent):
    cells = 65536
    place = [lax.axis_index(name) for name in ("c", "yh", "x", FL)]
    place = jnp.stack(place).astype(jnp.int32)
    turned_coarse = jnp.swapaxes(weight_coarse, 1, 2).reshape(9, 192, 256)

    pack = call(pack_kernel, (array(384, 256), array(384, 256)), [VMEM] * 2, limit=60)
    lo, hi = swap_sides(*pack(inputs, cotangent), SP)
    edge = call(edge_kernel, (array(256, 256), array(256, 256)), [VMEM] * 3)
    low, high = edge(inputs, lo, hi)
    ylo, yhi = swap_sides(high, low, FL)
    partial, wide_cot = call(
        coarse_back_kernel,
        (array(512, 256), array(3, 34, 16, 192)),
        [VMEM] * 4,
    )(cotangent, lo, hi, turned_coarse)
    blocks = (inputs, lo, hi, ylo, yhi)
    sent, slope, far = call(
        fine_forward_kernel,
        (array(8, 160, 256), array(640, 256, dtype=F32), array(768, 256)),
        [SMEM] + [VMEM] * 7,
        [
            pltpu.VMEM((4, 12, 32, 768), BF),
            pltpu.VMEM((640, 256), F32),
            pltpu.VMEM((2, 128, 128), F32),
            pltpu.VMEM((544, 256), BF),
        ],
    )(place, *blocks, partial, weight_fine.reshape(9, 768, 256))
    far = lax.ppermute(far, "c", SWAP)
    got = lax.all_to_all(sent, FL, 0, 0, tiled=True)
    grad, up, down, slab = call(
        fine_grad_kernel,
        (array(512, 256), array(320, 256), array(320, 256), array(512, 256)),
        [SMEM] + [VMEM] * 2,
        [pltpu.VMEM((2, 192, 128), F32)],
    )(place, got, slope)
    other = lax.ppermute(grad, "c", SWAP)
    lo, hi = swap_sides(up, down, SP)
    across = lax.ppermute(slab, "c", SWAP)
    terms = call(
        fine_weight_kernel,
        array(64, 54, 256),
        [SMEM] + [VMEM] * 8,
        [
            pltpu.VMEM((6, 10, 32, 768), BF),
            pltpu.VMEM((9, 6, 256, 256), BF),
            pltpu.VMEM((2, 432, 256), F32),
        ],
        limit=24,
    )(place, *blocks, far, grad, other)
    terms, lo, hi = lax.optimization_barrier((terms, lo, hi))
    spread = lax.all_to_all(terms, ("x", "yh", "z", "yl"), 0, 0, tiled=True)

    coarse_terms = call(
        coarse_weight_kernel,
        array(8, 224, 128),
        [SMEM] + [VMEM] * 4,
        [pltpu.VMEM((34, 16, 192), BF), pltpu.VMEM((6912, 64), F32)],
    )(place, slab, across, wide_cot, far)
    coarse_terms = coarse_terms.reshape(4, 448, 128)
    arrived = [
        lax.ppermute(coarse_terms[step], "x", [(i, (i + step) % 4) for i in range(4)])
        for step in range(1, 4)
    ]
    coarse_terms = call(quad_kernel, array(448, 128), [VMEM] * 4)(coarse_terms[0], *arrived)
    grad_input = call(
        fine_back_kernel,
        array(512, 256),
        [VMEM] * 5,
        [pltpu.VMEM((4, 10, 32, 768), BF), pltpu.VMEM((512, 256), F32)],
        flops=2**31,
    )(up, down, lo, hi, weight_fine.reshape(9, 3, 256, 256))
    grad_input, coarse_terms = lax.optimization_barrier((grad_input, coarse_terms))
    arrived = lax.ppermute(coarse_terms[224:], "yh", SWAP)
    centre, up, down = call(
        coarse_forward_kernel,
        (array(512, 64, dtype=F32), array(128, 256), array(128, 256)),
        [VMEM] * 2,
        [pltpu.VMEM((34, 16, 768), BF)],
    )(slab, turned_coarse)
    lo, hi = swap_sides(up, down, SP)
    coarse_out = call(coarse_out_kernel, array(512, 64), [VMEM] * 3)(centre, lo, hi)
    grad_coarse = call(
        functools.partial(coarse_sum_kernel, 1.0 / math.sqrt(cells // 8)),
        array(64, 432, dtype=F32),
        [VMEM] * 2,
    )(coarse_terms, arrived)
    grad_fine = call(
        functools.partial(fine_sum_kernel, 1.0 / math.sqrt(cells)),
        array(108, 128, dtype=F32),
        [VMEM],
        flops=2**31,
    )(spread)
    return (
        coarse_out.reshape(1, 32, 16, 64),
        grad_input.reshape(2, 8, 32, 256),
        grad_fine.reshape(-1),
        grad_coarse.T,
    )


def solution(mesh):
    fine_mesh = jax.sharding.Mesh(mesh.devices.reshape(4, 2, 2, 4, 2), SP + FL)
    return jax.shard_map(
        body,
        mesh=fine_mesh,
        in_specs=(P(SP, FL, None, None), P(), P(None, None, FL), P(SP, None, None, FL)),
        out_specs=(P(SP, None, None, FL), P(SP, FL, None, None), P(SP + FL), P(SP, FL)),
        check_vma=False,
    )
```

```python
import functools
import math

import jax
import jax.numpy as jnp
from jax import lax
from jax.experimental import pallas as pl
from jax.experimental.pallas import tpu as pltpu
from jax.sharding import PartitionSpec as P

SP = ("x", "yh", "c")
FL = ("z", "yl")
BF = jnp.bfloat16
F32 = jnp.float32
VMEM = pl.BlockSpec(memory_space=pltpu.VMEM)
SMEM = pl.BlockSpec(memory_space=pltpu.SMEM)
SWAP = [(0, 1), (1, 0)]


def call(kernel, out_shape, in_specs, scratch=(), limit=12, flops=2**20):
    return pl.pallas_call(
        kernel,
        out_shape=out_shape,
        in_specs=in_specs,
        out_specs=jax.tree.map(lambda _: VMEM, out_shape),
        scratch_shapes=list(scratch),
        compiler_params=pltpu.CompilerParams(vmem_limit_bytes=limit * 2**20),
        cost_estimate=pl.CostEstimate(flops=flops, bytes_accessed=2**16, transcendentals=0),
    )


def array(*shape, dtype=BF):
    return jax.ShapeDtypeStruct(shape, dtype)


def along_depth(rows, order):
    count, depth, width = rows.shape
    flat = rows.astype(F32).reshape(count * depth, width)
    place = lax.broadcasted_iota(jnp.int32, flat.shape, 0) & (depth - 1)
    before = jnp.where(place == 0, 0.0, pltpu.roll(flat, 1, 0)).astype(BF)
    after = jnp.where(place == depth - 1, 0.0, pltpu.roll(flat, count * depth - 1, 0)).astype(BF)
    middle = flat.astype(BF)
    trio = (before, middle, after) if order > 0 else (after, middle, before)
    return jnp.concatenate(trio, axis=1).reshape(count, depth, 3 * width)


def pad_rows(plane):
    edge = jnp.zeros((1,) + plane.shape[1:], plane.dtype)
    return jnp.concatenate([edge, plane, edge], axis=0)


def unpacked(block):
    strips = [block[:, 64 * k : 64 * k + 64] for k in range(4)]
    return jnp.concatenate(strips, axis=0).reshape(32, 16, 64)


def packed(plane):
    return jnp.concatenate([plane[128 * k : 128 * k + 128] for k in range(4)], axis=1)


def ordered(first, inner, outer):
    return jnp.where(first, outer, inner), jnp.where(first, inner, outer)


def pack_kernel(place, own, cot, inner, outer):
    first = place[0] == 0
    low, high = own[0].reshape(256, 256), own[1].reshape(256, 256)
    inner[:256] = jnp.where(first, high, low)
    outer[:256] = jnp.where(first, low, high)
    flat = cot[0].reshape(512, 64)
    inner[256:] = packed(flat)
    outer[256:] = packed(flat)


def planes_of(place, own, inner, outer):
    lo, hi = ordered(place[0] == 0, inner[:256], outer[:256])
    return lo.reshape(8, 32, 256), own[0], own[1], hi.reshape(8, 32, 256)


def edge_kernel(place, own, inner, outer, yinner, youter):
    first = lax.rem(place[3], 2) == 0
    for x, plane in enumerate(planes_of(place, own, inner, outer)):
        low, high = plane[:2].reshape(64, 256), plane[6:].reshape(64, 256)
        yinner[64 * x : 64 * x + 64] = jnp.where(first, high, low)
        youter[64 * x : 64 * x + 64] = jnp.where(first, low, high)


def whole_plane(place, plane, yinner, youter, x):
    rows = slice(64 * x, 64 * x + 64)
    below, above = ordered(lax.rem(place[3], 2) == 0, yinner[rows], youter[rows])
    return jnp.concatenate(
        [below.reshape(2, 32, 256), plane, above.reshape(2, 32, 256)], axis=0
    )


def coarse_back_kernel(place, cot, inner, outer, w, partial, wide):
    lo, hi = ordered(place[0] == 0, inner[256:], outer[256:])
    for x, plane in enumerate((unpacked(lo), cot[0], unpacked(hi))):
        wide[x] = along_depth(pad_rows(plane), -1)
    total = None
    for k in range(9):
        a, b = divmod(k, 3)
        window = wide[2 - a, 2 - b : 34 - b].reshape(512, 192)
        term = jnp.dot(window, w[k], preferred_element_type=F32)
        total = term if k == 0 else total + term
    partial[...] = total.astype(BF)


def fine_forward_kernel(
    place, own, inner, outer, yinner, youter, partial, w,
    sent, slope, far, wide, pre, sums, padded,
):
    for x, plane in enumerate(planes_of(place, own, inner, outer)):
        plane = whole_plane(place, plane, yinner, youter, x)
        wide[x] = along_depth(plane, 1)

        @pl.when(place[0] == x // 2)
        def _():
            far[320 * (x % 2) : 320 * (x % 2) + 320] = plane[1:11].reshape(320, 256)

    far[640:] = outer[256:]
    for k in range(9):
        a, b = divmod(k, 3)
        window = wide[a : a + 2, b : b + 10].reshape(640, 768)
        term = jnp.dot(window, w[k], preferred_element_type=F32)
        pre[...] = term if k == 0 else pre[...] + term
    for y in range(6):
        total = jnp.zeros((32, 256), F32)
        for x in range(2):
            for row in (2 * y - 1, 2 * y):
                if 0 <= row < 10:
                    at = x * 320 + row * 32
                    value = pre[at : at + 32]
                    sigma = 1.0 / (1.0 + jnp.exp(-value))
                    total = total + (value * sigma).astype(BF).astype(F32)
                    slope[at : at + 32] = 0.125 * sigma * (1.0 + value * (1.0 - sigma))
        if 0 < y < 5:
            sums[0, y * 32 - 32 : y * 32] = total[:, :128]
            sums[1, y * 32 - 32 : y * 32] = total[:, 128:]
    pooled = []
    for side in range(2):
        even = sums[side, pl.ds(0, 64, stride=2)]
        odd = sums[side, pl.ds(1, 64, stride=2)]
        pooled.append(((even + odd) * 0.125).astype(BF))
    pooled = jnp.concatenate(pooled, axis=1)
    padded[:16] = jnp.zeros((16, 256), BF)
    padded[16:528] = partial[...]
    padded[528:] = jnp.zeros((16, 256), BF)
    for k in range(8):
        sent[k, :64] = pooled
        sent[k, 64:] = padded[64 * k : 64 * k + 96]


def fine_grad_kernel(place, got, slope, grad, slab, spread):
    for y in range(6):
        rows = slice(64 + 16 * y, 80 + 16 * y)
        total = got[0, rows].astype(F32)
        for k in range(1, 8):
            total = total + got[k, rows].astype(F32)
        total = total.astype(BF).astype(F32)
        if y == 0:
            total = jnp.where(place[3] > 0, total, 0.0)
        if y == 5:
            total = jnp.where(place[3] < 7, total, 0.0)
        for side in range(2):
            half = total[:, side * 128 : side * 128 + 128]
            spread[side, pl.ds(32 * y, 16, stride=2)] = half
            spread[side, pl.ds(32 * y + 1, 16, stride=2)] = half
        at = slice(y * 32, y * 32 + 32)
        wide = jnp.concatenate([spread[0, at], spread[1, at]], axis=1)
        for x in range(2):
            for row in (2 * y - 1, 2 * y):
                if 0 <= row < 10:
                    at = x * 320 + row * 32
                    grad[at : at + 32] = (wide * slope[at : at + 32]).astype(BF)
    for k in range(8):
        slab[64 * k : 64 * k + 64] = got[k, :64]


def fine_weight_kernel(
    place, own, inner, outer, yinner, youter, far, grad, other, terms, wide, turned, total
):
    for core in range(2):

        @pl.when(place[0] == core)
        def _():
            planes, windows = set(), set()
            sides = [side[:256].reshape(8, 32, 256) for side in (inner, outer)]
            blocks = (sides[1 - core], own[0], own[1], sides[core])

            def prepare(bc, slot):
                if (bc, slot) in windows:
                    return
                windows.add((bc, slot))
                if slot not in planes:
                    planes.add(slot)
                    x = slot - 2 * core
                    if 0 <= x < 4:
                        rows = whole_plane(place, blocks[x], yinner, youter, x)[1:11]
                    else:
                        at = 320 * (slot % 2)
                        rows = far[at : at + 320].reshape(10, 32, 256)
                    wide[slot] = along_depth(rows, 1)
                b, c = divmod(bc, 3)
                window = wide[slot, b : b + 8, :, c * 256 : c * 256 + 256]
                turned[bc, slot] = window.reshape(256, 256).T

            pair = (grad, other) if core == 0 else (other, grad)
            right = jnp.concatenate(
                [side[at : at + 256] for side in pair for at in (32, 352)], axis=0
            )
            for k in range(8):
                at = 432 * (2 * k + core)
                end = at + 432
                pieces = []
                while at < end:
                    tap, low = divmod(at, 256)
                    high = min(256, low + end - at)
                    a, bc = divmod(tap, 9)
                    for plane in range(4):
                        prepare(bc, a + plane)
                    strips = [turned[bc, a + plane, low:high] for plane in range(4)]
                    pieces.append(jnp.concatenate(strips, axis=1))
                    at += high - low
                left = jnp.concatenate(pieces, axis=0)
                total[k % 2] = jnp.dot(left, right, preferred_element_type=F32)
                for f in range(8):
                    terms[k * 8 + f] = total[k % 2, f * 54 : f * 54 + 54].astype(BF)


def fine_back_kernel(place, grad, other, w, total, rest, wide):
    first = place[0] == 0
    none = jnp.zeros((320, 256), BF)
    planes = (
        jnp.where(first, none, other[320:]),
        grad[:320],
        grad[320:],
        jnp.where(first, other[:320], none),
    )
    for x, plane in enumerate(planes):
        wide[x] = along_depth(plane.reshape(10, 32, 256), -1)
    for k in range(9):
        a, b = divmod(k, 3)
        window = wide[2 - a : 4 - a, 2 - b : 10 - b].reshape(512, 768)
        right = jnp.concatenate([w[k, 0], w[k, 1], w[k, 2]], axis=1)
        term = lax.dot_general(window, right, (((1,), (1,)), ((), ())), preferred_element_type=F32)
        total[...] = term if k == 0 else total[...] + term
    for b in range(3):
        for c in range(3):
            at = slice(256 * c, 256 * c + 256)
            rest[b, :, at] = jnp.where(first, w[6 + b, c], w[b, c])


def fine_rest_kernel(place, total, outer, rest, out):
    wide = along_depth(outer[:320].reshape(10, 32, 256), -1)
    more = None
    for b in range(3):
        window = wide[2 - b : 10 - b].reshape(256, 768)
        term = lax.dot_general(
            window, rest[b], (((1,), (1,)), ((), ())), preferred_element_type=F32
        )
        more = term if b == 0 else more + term
    first = place[0] == 0
    out[:256] = (total[:256] + jnp.where(first, more, 0.0)).astype(BF)
    out[256:] = (total[256:] + jnp.where(first, 0.0, more)).astype(BF)


def coarse_weight_kernel(place, slab, other, wide, far, terms, outer, total):
    outer[...] = along_depth(pad_rows(unpacked(far[640:768])), -1)
    left = jnp.concatenate([slab[...].T, other[...].T], axis=1)
    for core in range(2):

        @pl.when(place[0] == core)
        def _():
            for k in range(9):
                a, b = divmod(k, 3)
                rows = slice(2 - b, 34 - b)
                at = 2 - a + (1 if core == 0 else -1)
                across = wide[at, rows] if 0 <= at < 3 else outer[rows]
                right = jnp.concatenate(
                    [wide[2 - a, rows].reshape(512, 192), across.reshape(512, 192)], axis=0
                )
                term = jnp.dot(left, right, preferred_element_type=F32)
                for c in range(3):
                    row = (3 * k + c) * 256
                    total[row : row + 256] = term[:, c * 64 : c * 64 + 64]
            for block in range(8):
                x, yh = divmod(block, 2)
                row = (2 * block + core) * 432
                upper = total[row : row + 224]
                lower = jnp.concatenate(
                    [total[row + 224 : row + 432], jnp.zeros((16, 64), F32)], axis=0
                )
                at = lax.rem(4 + x - place[2], 4) * 2 + lax.rem(place[1] + yh, 2)
                terms[at] = jnp.concatenate([upper, lower], axis=1).astype(BF)


def coarse_forward_kernel(place, slab, w, grad, own, inner, outer, wide):
    first = place[0] == 0
    outer[:320] = jnp.where(first, grad[:320], grad[320:])
    wide[...] = along_depth(pad_rows(slab[...].reshape(32, 16, 256)), 1)
    total = None
    for b in range(3):
        columns = []
        for a in range(3):
            turned = w[3 * a + b].T
            columns.append(
                jnp.concatenate([turned[:, 64 * c : 64 * c + 64] for c in range(3)], axis=0)
            )
        right = jnp.concatenate(columns, axis=1)
        window = wide[b : b + 32].reshape(512, 768)
        term = jnp.dot(window, right, preferred_element_type=F32)
        total = term if b == 0 else total + term
    own[...] = total[:, 64:128]
    up, down = packed(total[:, :64]).astype(BF), packed(total[:, 128:]).astype(BF)
    inner[...] = jnp.where(first, up, down)
    outer[320:] = jnp.where(first, down, up)


def coarse_out_kernel(own, inner, outer, out):
    for k in range(4):
        rows, columns = slice(128 * k, 128 * k + 128), slice(64 * k, 64 * k + 64)
        total = own[rows] + inner[:, columns].astype(F32) + outer[320:, columns].astype(F32)
        out[rows] = total.astype(BF)


def fine_sum_kernel(scale, parts, out):
    total = parts[0].astype(F32)
    for k in range(1, 64):
        total = total + parts[k].astype(F32)
    total = total * scale
    out[pl.ds(0, 54, stride=2)] = total[:, :128]
    out[pl.ds(1, 54, stride=2)] = total[:, 128:]


def quad_kernel(own, first, second, third, out):
    total = own[...].astype(F32) + first[...].astype(F32)
    total = total + second[...].astype(F32) + third[...].astype(F32)
    out[...] = total.astype(BF)


def coarse_sum_kernel(scale, own, other, out):
    total = own[:224].astype(F32) + other[...].astype(F32)
    total = total * scale
    out[...] = jnp.concatenate([total[:, :64], total[:208, 64:]], axis=0).T


def swap(inner, outer, axis):
    partner = axis[-1]
    pairs = [(i, i + 1) for i in range(1, lax.axis_size(axis) - 1, 2)]
    pairs += [(j, i) for i, j in pairs]
    return lax.ppermute(inner, partner, SWAP), lax.ppermute(outer, axis, pairs)


def body(inputs, weight_fine, weight_coarse, cotangent):
    cells = 65536
    place = [lax.axis_index(name) for name in ("c", "yh", "x", FL)]
    place = jnp.stack(place).astype(jnp.int32)
    turned_coarse = jnp.swapaxes(weight_coarse, 1, 2).reshape(9, 192, 256)

    pack = call(pack_kernel, (array(384, 256), array(384, 256)), [SMEM] + [VMEM] * 2, limit=60)
    inner, outer = swap(*pack(place, inputs, cotangent), SP)
    edge = call(edge_kernel, (array(256, 256), array(256, 256)), [SMEM] + [VMEM] * 3)
    yinner, youter = swap(*edge(place, inputs, inner, outer), FL)
    partial, wide_cot = call(
        coarse_back_kernel,
        (array(512, 256), array(3, 34, 16, 192)),
        [SMEM] + [VMEM] * 4,
    )(place, cotangent, inner, outer, turned_coarse)
    blocks = (inputs, inner, outer, yinner, youter)
    sent, slope, far = call(
        fine_forward_kernel,
        (array(8, 160, 256), array(640, 256, dtype=F32), array(768, 256)),
        [SMEM] + [VMEM] * 7,
        [
            pltpu.VMEM((4, 12, 32, 768), BF),
            pltpu.VMEM((640, 256), F32),
            pltpu.VMEM((2, 128, 128), F32),
            pltpu.VMEM((544, 256), BF),
        ],
    )(place, *blocks, partial, weight_fine.reshape(9, 768, 256))
    far = lax.ppermute(far, "c", SWAP)
    got = lax.all_to_all(sent, FL, 0, 0, tiled=True)
    grad, slab = call(
        fine_grad_kernel,
        (array(640, 256), array(512, 256)),
        [SMEM] + [VMEM] * 2,
        [pltpu.VMEM((2, 192, 128), F32)],
    )(place, got, slope)
    other = lax.ppermute(grad, "c", SWAP)
    across = lax.ppermute(slab, "c", SWAP)
    terms = call(
        fine_weight_kernel,
        array(64, 54, 256),
        [SMEM] + [VMEM] * 8,
        [
            pltpu.VMEM((6, 10, 32, 768), BF),
            pltpu.VMEM((9, 6, 256, 256), BF),
            pltpu.VMEM((2, 432, 256), F32),
        ],
        limit=24,
    )(place, *blocks, far, grad, other)
    spread = lax.all_to_all(terms, ("x", "yh", "z", "yl"), 0, 0, tiled=True)

    coarse_terms = call(
        coarse_weight_kernel,
        array(8, 224, 128),
        [SMEM] + [VMEM] * 4,
        [pltpu.VMEM((34, 16, 192), BF), pltpu.VMEM((6912, 64), F32)],
    )(place, slab, across, wide_cot, far)
    coarse_terms, other = lax.optimization_barrier((coarse_terms, other))
    coarse_terms = coarse_terms.reshape(4, 448, 128)
    arrived = [
        lax.ppermute(coarse_terms[step], "x", [(i, (i + step) % 4) for i in range(4)])
        for step in range(1, 4)
    ]
    coarse_terms = call(quad_kernel, array(448, 128), [VMEM] * 4)(coarse_terms[0], *arrived)
    centre, inner, outer = call(
        coarse_forward_kernel,
        (array(512, 64, dtype=F32), array(128, 256), array(448, 256)),
        [SMEM] + [VMEM] * 3,
        [pltpu.VMEM((34, 16, 768), BF)],
    )(place, slab, turned_coarse, grad)
    inner, outer = swap(inner, outer, SP)
    total, rest = call(
        fine_back_kernel,
        (array(512, 256, dtype=F32), array(3, 256, 768)),
        [SMEM] + [VMEM] * 3,
        [pltpu.VMEM((4, 10, 32, 768), BF)],
        flops=2**31,
    )(place, grad, other, weight_fine.reshape(9, 3, 256, 256))
    coarse_terms, inner, outer, total = lax.optimization_barrier(
        (coarse_terms, inner, outer, total)
    )
    grad_input = call(fine_rest_kernel, array(512, 256), [SMEM] + [VMEM] * 3, flops=2**30)(
        place, total, outer, rest
    )
    arrived = lax.ppermute(coarse_terms[224:], "yh", SWAP)
    coarse_out = call(coarse_out_kernel, array(512, 64), [VMEM] * 3)(centre, inner, outer)
    grad_fine = call(
        functools.partial(fine_sum_kernel, 1.0 / math.sqrt(cells)),
        array(108, 128, dtype=F32),
        [VMEM],
    )(spread)
    grad_fine, arrived = lax.optimization_barrier((grad_fine, arrived))
    grad_coarse = call(
        functools.partial(coarse_sum_kernel, 1.0 / math.sqrt(cells // 8)),
        array(64, 432, dtype=F32),
        [VMEM] * 2,
    )(coarse_terms, arrived)
    return (
        coarse_out.reshape(1, 32, 16, 64),
        grad_input.reshape(2, 8, 32, 256),
        grad_fine.reshape(-1),
        grad_coarse.T,
    )


def solution(mesh):
    fine_mesh = jax.sharding.Mesh(mesh.devices.reshape(4, 2, 2, 4, 2), SP + FL)
    return jax.shard_map(
        body,
        mesh=fine_mesh,
        in_specs=(P(SP, FL, None, None), P(), P(None, None, FL), P(SP, None, None, FL)),
        out_specs=(P(SP, None, None, FL), P(SP, FL, None, None), P(SP + FL), P(SP, FL)),
        check_vma=False,
    )
```

```python
import functools
import math

import jax
import jax.numpy as jnp
from jax import lax
from jax.experimental import pallas as pl
from jax.experimental.pallas import tpu as pltpu
from jax.sharding import PartitionSpec as P

SP = ("x", "yh", "c")
FL = ("z", "yl")
BF = jnp.bfloat16
F32 = jnp.float32
VMEM = pl.BlockSpec(memory_space=pltpu.VMEM)
ANY = pl.BlockSpec(memory_space=pl.ANY)
SWAP = [(0, 1), (1, 0)]


def call(kernel, out_shape, in_specs, scratch=(), limit=12, flops=2**20):
    return pl.pallas_call(
        kernel,
        out_shape=out_shape,
        in_specs=in_specs,
        out_specs=jax.tree.map(lambda _: VMEM, out_shape),
        scratch_shapes=list(scratch),
        compiler_params=pltpu.CompilerParams(vmem_limit_bytes=limit * 2**20),
        cost_estimate=pl.CostEstimate(flops=flops, bytes_accessed=2**16, transcendentals=0),
    )


def array(*shape, dtype=BF):
    return jax.ShapeDtypeStruct(shape, dtype)


def along_depth(rows, order):
    count, depth, width = rows.shape
    flat = rows.astype(F32).reshape(count * depth, width)
    place = lax.broadcasted_iota(jnp.int32, flat.shape, 0) & (depth - 1)
    before = jnp.where(place == 0, 0.0, pltpu.roll(flat, 1, 0)).astype(BF)
    after = jnp.where(place == depth - 1, 0.0, pltpu.roll(flat, count * depth - 1, 0)).astype(BF)
    middle = flat.astype(BF)
    trio = (before, middle, after) if order > 0 else (after, middle, before)
    return jnp.concatenate(trio, axis=1).reshape(count, depth, 3 * width)


def pad_rows(plane):
    edge = jnp.zeros((1,) + plane.shape[1:], plane.dtype)
    return jnp.concatenate([edge, plane, edge], axis=0)


def unpacked(block):
    strips = [block[:, 64 * k : 64 * k + 64] for k in range(4)]
    return jnp.concatenate(strips, axis=0).reshape(32, 16, 64)


def packed(plane):
    return jnp.concatenate([plane[128 * k : 128 * k + 128] for k in range(4)], axis=1)


def position():
    row = 2 * lax.axis_index("z") + lax.axis_index("yl")
    return lax.axis_index("c"), lax.axis_index("yh"), lax.axis_index("x"), row


def ordered(first, inner, outer):
    return jnp.where(first, outer, inner), jnp.where(first, inner, outer)


def pack_kernel(own, cot, inner, outer):
    place = position()
    first = place[0] == 0
    low, high = own[0].reshape(256, 256), own[1].reshape(256, 256)
    inner[:256] = jnp.where(first, high, low)
    outer[:256] = jnp.where(first, low, high)
    flat = cot[0].reshape(512, 64)
    inner[256:] = packed(flat)
    outer[256:] = packed(flat)


def stage_kernel(token, w_hbm, wc_hbm, own_hbm, cot_hbm, w, wc, own, cot, sems):
    copies = [pltpu.make_async_copy(w_hbm.at[k], w.at[k], sems.at[k]) for k in range(9)]
    copies += [
        pltpu.make_async_copy(wc_hbm, wc, sems.at[9]),
        pltpu.make_async_copy(own_hbm, own, sems.at[10]),
        pltpu.make_async_copy(cot_hbm, cot, sems.at[11]),
    ]
    for copy in copies:
        copy.start()
    for copy in copies:
        copy.wait()


def planes_of(place, own, inner, outer):
    lo, hi = ordered(place[0] == 0, inner[:256], outer[:256])
    return lo.reshape(8, 32, 256), own[0], own[1], hi.reshape(8, 32, 256)


def edge_kernel(own, inner, outer, yinner, youter):
    place = position()
    first = lax.rem(place[3], 2) == 0
    for x, plane in enumerate(planes_of(place, own, inner, outer)):
        low, high = plane[:2].reshape(64, 256), plane[6:].reshape(64, 256)
        yinner[64 * x : 64 * x + 64] = jnp.where(first, high, low)
        youter[64 * x : 64 * x + 64] = jnp.where(first, low, high)


def whole_plane(place, plane, yinner, youter, x):
    rows = slice(64 * x, 64 * x + 64)
    below, above = ordered(lax.rem(place[3], 2) == 0, yinner[rows], youter[rows])
    return jnp.concatenate(
        [below.reshape(2, 32, 256), plane, above.reshape(2, 32, 256)], axis=0
    )


def coarse_back_kernel(cot, inner, outer, w, partial, wide):
    place = position()
    lo, hi = ordered(place[0] == 0, inner[256:], outer[256:])
    for x, plane in enumerate((unpacked(lo), cot[0], unpacked(hi))):
        wide[x] = along_depth(pad_rows(plane), -1)
    total = None
    for k in range(9):
        a, b = divmod(k, 3)
        window = wide[2 - a, 2 - b : 34 - b].reshape(512, 192)
        term = jnp.dot(window, w[k], preferred_element_type=F32)
        total = term if k == 0 else total + term
    partial[...] = total.astype(BF)


def fine_forward_kernel(
    own, inner, outer, yinner, youter, partial, w,
    sent, slope, far, wide, pre, sums, padded,
):
    place = position()
    for x, plane in enumerate(planes_of(place, own, inner, outer)):
        plane = whole_plane(place, plane, yinner, youter, x)
        wide[x] = along_depth(plane, 1)

        @pl.when(place[0] == x // 2)
        def _():
            far[320 * (x % 2) : 320 * (x % 2) + 320] = plane[1:11].reshape(320, 256)

    far[640:] = outer[256:]
    for k in range(9):
        a, b = divmod(k, 3)
        window = wide[a : a + 2, b : b + 10].reshape(640, 768)
        term = jnp.dot(window, w[k], preferred_element_type=F32)
        pre[...] = term if k == 0 else pre[...] + term
    for y in range(6):
        total = jnp.zeros((32, 256), F32)
        for x in range(2):
            for row in (2 * y - 1, 2 * y):
                if 0 <= row < 10:
                    at = x * 320 + row * 32
                    value = pre[at : at + 32]
                    sigma = 1.0 / (1.0 + jnp.exp(-value))
                    total = total + (value * sigma).astype(BF).astype(F32)
                    slope[at : at + 32] = 0.125 * sigma * (1.0 + value * (1.0 - sigma))
        if 0 < y < 5:
            sums[0, y * 32 - 32 : y * 32] = total[:, :128]
            sums[1, y * 32 - 32 : y * 32] = total[:, 128:]
    pooled = []
    for side in range(2):
        even = sums[side, pl.ds(0, 64, stride=2)]
        odd = sums[side, pl.ds(1, 64, stride=2)]
        pooled.append(((even + odd) * 0.125).astype(BF))
    pooled = jnp.concatenate(pooled, axis=1)
    padded[:16] = jnp.zeros((16, 256), BF)
    padded[16:528] = partial[...]
    padded[528:] = jnp.zeros((16, 256), BF)
    for k in range(8):
        sent[k, :64] = pooled
        sent[k, 64:] = padded[64 * k : 64 * k + 96]


def fine_grad_kernel(got, slope, grad, slab, spread):
    place = position()
    for y in range(6):
        rows = slice(64 + 16 * y, 80 + 16 * y)
        total = got[0, rows].astype(F32)
        for k in range(1, 8):
            total = total + got[k, rows].astype(F32)
        total = total.astype(BF).astype(F32)
        if y == 0:
            total = jnp.where(place[3] > 0, total, 0.0)
        if y == 5:
            total = jnp.where(place[3] < 7, total, 0.0)
        for side in range(2):
            half = total[:, side * 128 : side * 128 + 128]
            spread[side, pl.ds(32 * y, 16, stride=2)] = half
            spread[side, pl.ds(32 * y + 1, 16, stride=2)] = half
        at = slice(y * 32, y * 32 + 32)
        wide = jnp.concatenate([spread[0, at], spread[1, at]], axis=1)
        for x in range(2):
            for row in (2 * y - 1, 2 * y):
                if 0 <= row < 10:
                    at = x * 320 + row * 32
                    grad[at : at + 32] = (wide * slope[at : at + 32]).astype(BF)
    for k in range(8):
        slab[64 * k : 64 * k + 64] = got[k, :64]


def fine_weight_kernel(
    own, inner, outer, yinner, youter, far, grad, other, terms, wide, turned, total
):
    place = position()
    for core in range(2):

        @pl.when(place[0] == core)
        def _():
            planes, windows = set(), set()
            sides = [side[:256].reshape(8, 32, 256) for side in (inner, outer)]
            blocks = (sides[1 - core], own[0], own[1], sides[core])

            def prepare(bc, slot):
                if (bc, slot) in windows:
                    return
                windows.add((bc, slot))
                if slot not in planes:
                    planes.add(slot)
                    x = slot - 2 * core
                    if 0 <= x < 4:
                        rows = whole_plane(place, blocks[x], yinner, youter, x)[1:11]
                    else:
                        at = 320 * (slot % 2)
                        rows = far[at : at + 320].reshape(10, 32, 256)
                    wide[slot] = along_depth(rows, 1)
                b, c = divmod(bc, 3)
                window = wide[slot, b : b + 8, :, c * 256 : c * 256 + 256]
                turned[bc, slot] = window.reshape(256, 256).T

            pair = (grad, other) if core == 0 else (other, grad)
            right = jnp.concatenate(
                [side[at : at + 256] for side in pair for at in (32, 352)], axis=0
            )
            for k in range(8):
                at = 432 * (2 * k + core)
                end = at + 432
                pieces = []
                while at < end:
                    tap, low = divmod(at, 256)
                    high = min(256, low + end - at)
                    a, bc = divmod(tap, 9)
                    for plane in range(4):
                        prepare(bc, a + plane)
                    strips = [turned[bc, a + plane, low:high] for plane in range(4)]
                    pieces.append(jnp.concatenate(strips, axis=1))
                    at += high - low
                left = jnp.concatenate(pieces, axis=0)
                total[k % 2] = jnp.dot(left, right, preferred_element_type=F32)
                for f in range(8):
                    terms[k * 8 + f] = total[k % 2, f * 54 : f * 54 + 54].astype(BF)


def fine_back_kernel(grad, other, w, total, rest, wide):
    place = position()
    first = place[0] == 0
    none = jnp.zeros((320, 256), BF)
    planes = (
        jnp.where(first, none, other[320:]),
        grad[:320],
        grad[320:],
        jnp.where(first, other[:320], none),
    )
    for x, plane in enumerate(planes):
        wide[x] = along_depth(plane.reshape(10, 32, 256), -1)
    for k in range(9):
        a, b = divmod(k, 3)
        window = wide[2 - a : 4 - a, 2 - b : 10 - b].reshape(512, 768)
        right = jnp.concatenate([w[k, 0], w[k, 1], w[k, 2]], axis=1)
        term = lax.dot_general(window, right, (((1,), (1,)), ((), ())), preferred_element_type=F32)
        total[...] = term if k == 0 else total[...] + term
    for b in range(3):
        for c in range(3):
            at = slice(256 * c, 256 * c + 256)
            rest[b, :, at] = jnp.where(first, w[6 + b, c], w[b, c])


def fine_rest_kernel(total, outer, rest, out):
    place = position()
    wide = along_depth(outer[:320].reshape(10, 32, 256), -1)
    more = None
    for b in range(3):
        window = wide[2 - b : 10 - b].reshape(256, 768)
        term = lax.dot_general(
            window, rest[b], (((1,), (1,)), ((), ())), preferred_element_type=F32
        )
        more = term if b == 0 else more + term
    first = place[0] == 0
    out[:256] = (total[:256] + jnp.where(first, more, 0.0)).astype(BF)
    out[256:] = (total[256:] + jnp.where(first, 0.0, more)).astype(BF)


def coarse_weight_kernel(slab, other, wide, far, terms, outer, total):
    place = position()
    outer[...] = along_depth(pad_rows(unpacked(far[640:768])), -1)
    left = jnp.concatenate([slab[...].T, other[...].T], axis=1)
    for core in range(2):

        @pl.when(place[0] == core)
        def _():
            for k in range(9):
                a, b = divmod(k, 3)
                rows = slice(2 - b, 34 - b)
                at = 2 - a + (1 if core == 0 else -1)
                across = wide[at, rows] if 0 <= at < 3 else outer[rows]
                right = jnp.concatenate(
                    [wide[2 - a, rows].reshape(512, 192), across.reshape(512, 192)], axis=0
                )
                term = jnp.dot(left, right, preferred_element_type=F32)
                for c in range(3):
                    row = (3 * k + c) * 256
                    total[row : row + 256] = term[:, c * 64 : c * 64 + 64]
            for block in range(8):
                x, yh = divmod(block, 2)
                row = (2 * block + core) * 432
                upper = total[row : row + 224]
                lower = jnp.concatenate(
                    [total[row + 224 : row + 432], jnp.zeros((16, 64), F32)], axis=0
                )
                at = lax.rem(4 + x - place[2], 4) * 2 + lax.rem(place[1] + yh, 2)
                terms[at] = jnp.concatenate([upper, lower], axis=1).astype(BF)


def coarse_forward_kernel(slab, w, grad, own, inner, outer, wide):
    place = position()
    first = place[0] == 0
    outer[:320] = jnp.where(first, grad[:320], grad[320:])
    wide[...] = along_depth(pad_rows(slab[...].reshape(32, 16, 256)), 1)
    total = None
    for b in range(3):
        columns = []
        for a in range(3):
            turned = w[3 * a + b].T
            columns.append(
                jnp.concatenate([turned[:, 64 * c : 64 * c + 64] for c in range(3)], axis=0)
            )
        right = jnp.concatenate(columns, axis=1)
        window = wide[b : b + 32].reshape(512, 768)
        term = jnp.dot(window, right, preferred_element_type=F32)
        total = term if b == 0 else total + term
    own[...] = total[:, 64:128]
    up, down = packed(total[:, :64]).astype(BF), packed(total[:, 128:]).astype(BF)
    inner[...] = jnp.where(first, up, down)
    outer[320:] = jnp.where(first, down, up)


def coarse_out_kernel(own, inner, outer, out):
    for k in range(4):
        rows, columns = slice(128 * k, 128 * k + 128), slice(64 * k, 64 * k + 64)
        total = own[rows] + inner[:, columns].astype(F32) + outer[320:, columns].astype(F32)
        out[rows] = total.astype(BF)


def fine_sum_kernel(scale, parts, out):
    total = parts[0].astype(F32)
    for k in range(1, 64):
        total = total + parts[k].astype(F32)
    total = total * scale
    out[pl.ds(0, 54, stride=2)] = total[:, :128]
    out[pl.ds(1, 54, stride=2)] = total[:, 128:]


def quad_kernel(own, first, second, third, out):
    total = own[...].astype(F32) + first[...].astype(F32)
    total = total + second[...].astype(F32) + third[...].astype(F32)
    out[...] = total.astype(BF)


def coarse_sum_kernel(scale, own, other, out):
    total = own[:224].astype(F32) + other[...].astype(F32)
    total = total * scale
    out[...] = jnp.concatenate([total[:, :64], total[:208, 64:]], axis=0).T


def swap(inner, outer, axis):
    partner = axis[-1]
    pairs = [(i, i + 1) for i in range(1, lax.axis_size(axis) - 1, 2)]
    pairs += [(j, i) for i, j in pairs]
    return lax.ppermute(inner, partner, SWAP), lax.ppermute(outer, axis, pairs)


def body(inputs, weight_fine, weight_coarse, cotangent):
    cells = 65536
    turned_coarse = jnp.swapaxes(weight_coarse, 1, 2).reshape(9, 192, 256)

    pack = call(pack_kernel, (array(384, 256), array(384, 256)), [VMEM] * 2, limit=60)
    inner, outer = pack(inputs, cotangent)
    staged = call(
        stage_kernel,
        (array(9, 768, 256), array(9, 192, 256), array(2, 8, 32, 256), array(1, 32, 16, 64)),
        [ANY] * 5,
        [pltpu.SemaphoreType.DMA((12,))],
    )(inner, weight_fine.reshape(9, 768, 256), turned_coarse, inputs, cotangent)
    inner, outer = swap(inner, outer, SP)
    inner, outer, staged = lax.optimization_barrier((inner, outer, staged))
    near_fine, near_coarse, near_inputs, near_cotangent = staged
    edge = call(edge_kernel, (array(256, 256), array(256, 256)), [VMEM] * 3)
    yinner, youter = swap(*edge(near_inputs, inner, outer), FL)
    partial, wide_cot = call(
        coarse_back_kernel,
        (array(512, 256), array(3, 34, 16, 192)),
        [VMEM] * 4,
    )(near_cotangent, inner, outer, near_coarse)
    blocks = (inputs, inner, outer, yinner, youter)
    sent, slope, far = call(
        fine_forward_kernel,
        (array(8, 160, 256), array(640, 256, dtype=F32), array(768, 256)),
        [VMEM] * 7,
        [
            pltpu.VMEM((4, 12, 32, 768), BF),
            pltpu.VMEM((640, 256), F32),
            pltpu.VMEM((2, 128, 128), F32),
            pltpu.VMEM((544, 256), BF),
        ],
    )(near_inputs, *blocks[1:], partial, near_fine)
    far = lax.ppermute(far, "c", SWAP)
    got = lax.all_to_all(sent, FL, 0, 0, tiled=True)
    grad, slab = call(
        fine_grad_kernel,
        (array(640, 256), array(512, 256)),
        [VMEM] * 2,
        [pltpu.VMEM((2, 192, 128), F32)],
    )(got, slope)
    other = lax.ppermute(grad, "c", SWAP)
    across = lax.ppermute(slab, "c", SWAP)
    terms = call(
        fine_weight_kernel,
        array(64, 54, 256),
        [VMEM] * 8,
        [
            pltpu.VMEM((6, 10, 32, 768), BF),
            pltpu.VMEM((9, 6, 256, 256), BF),
            pltpu.VMEM((2, 432, 256), F32),
        ],
        limit=24,
    )(*blocks, far, grad, other)
    spread = lax.all_to_all(terms, ("x", "yh", "z", "yl"), 0, 0, tiled=True)

    coarse_terms = call(
        coarse_weight_kernel,
        array(8, 224, 128),
        [VMEM] * 4,
        [pltpu.VMEM((34, 16, 192), BF), pltpu.VMEM((6912, 64), F32)],
    )(slab, across, wide_cot, far)
    coarse_terms, other = lax.optimization_barrier((coarse_terms, other))
    coarse_terms = coarse_terms.reshape(4, 448, 128)
    arrived = [
        lax.ppermute(coarse_terms[step], "x", [(i, (i + step) % 4) for i in range(4)])
        for step in range(1, 4)
    ]
    coarse_terms = call(quad_kernel, array(448, 128), [VMEM] * 4)(coarse_terms[0], *arrived)
    centre, inner, outer = call(
        coarse_forward_kernel,
        (array(512, 64, dtype=F32), array(128, 256), array(448, 256)),
        [VMEM] * 3,
        [pltpu.VMEM((34, 16, 768), BF)],
    )(slab, turned_coarse, grad)
    inner, outer = swap(inner, outer, SP)
    total, rest = call(
        fine_back_kernel,
        (array(512, 256, dtype=F32), array(3, 256, 768)),
        [VMEM] * 3,
        [pltpu.VMEM((4, 10, 32, 768), BF)],
        flops=2**31,
    )(grad, other, weight_fine.reshape(9, 3, 256, 256))
    coarse_terms, inner, outer, total = lax.optimization_barrier(
        (coarse_terms, inner, outer, total)
    )
    grad_input = call(fine_rest_kernel, array(512, 256), [VMEM] * 3, flops=2**30)(total, outer, rest)
    arrived = lax.ppermute(coarse_terms[224:], "yh", SWAP)
    coarse_out = call(coarse_out_kernel, array(512, 64), [VMEM] * 3)(centre, inner, outer)
    grad_fine = call(
        functools.partial(fine_sum_kernel, 1.0 / math.sqrt(cells)),
        array(108, 128, dtype=F32),
        [VMEM],
    )(spread)
    grad_fine, arrived = lax.optimization_barrier((grad_fine, arrived))
    grad_coarse = call(
        functools.partial(coarse_sum_kernel, 1.0 / math.sqrt(cells // 8)),
        array(64, 432, dtype=F32),
        [VMEM] * 2,
    )(coarse_terms, arrived)
    return (
        coarse_out.reshape(1, 32, 16, 64),
        grad_input.reshape(2, 8, 32, 256),
        grad_fine.reshape(-1),
        grad_coarse.T,
    )


def solution(mesh):
    fine_mesh = jax.sharding.Mesh(mesh.devices.reshape(4, 2, 2, 4, 2), SP + FL)
    return jax.shard_map(
        body,
        mesh=fine_mesh,
        in_specs=(P(SP, FL, None, None), P(), P(None, None, FL), P(SP, None, None, FL)),
        out_specs=(P(SP, None, None, FL), P(SP, FL, None, None), P(SP + FL), P(SP, FL)),
        check_vma=False,
    )
```

```python
import functools
import math

import jax
import jax.numpy as jnp
from jax import lax
from jax.experimental import pallas as pl
from jax.experimental.pallas import tpu as pltpu
from jax.sharding import PartitionSpec as P

SP = ("x", "yh", "c")
FL = ("z", "yl")
BF = jnp.bfloat16
F32 = jnp.float32
VMEM = pl.BlockSpec(memory_space=pltpu.VMEM)
ANY = pl.BlockSpec(memory_space=pl.ANY)
SWAP = [(0, 1), (1, 0)]


def call(kernel, out_shape, in_specs, scratch=(), limit=12, flops=2**20):
    return pl.pallas_call(
        kernel,
        out_shape=out_shape,
        in_specs=in_specs,
        out_specs=jax.tree.map(lambda _: VMEM, out_shape),
        scratch_shapes=list(scratch),
        compiler_params=pltpu.CompilerParams(vmem_limit_bytes=limit * 2**20),
        cost_estimate=pl.CostEstimate(flops=flops, bytes_accessed=2**16, transcendentals=0),
    )


def array(*shape, dtype=BF):
    return jax.ShapeDtypeStruct(shape, dtype)


def along_depth(rows, order):
    count, depth, width = rows.shape
    flat = rows.astype(F32).reshape(count * depth, width)
    place = lax.broadcasted_iota(jnp.int32, flat.shape, 0) & (depth - 1)
    before = jnp.where(place == 0, 0.0, pltpu.roll(flat, 1, 0)).astype(BF)
    after = jnp.where(place == depth - 1, 0.0, pltpu.roll(flat, count * depth - 1, 0)).astype(BF)
    middle = flat.astype(BF)
    trio = (before, middle, after) if order > 0 else (after, middle, before)
    return jnp.concatenate(trio, axis=1).reshape(count, depth, 3 * width)


def pad_rows(plane):
    edge = jnp.zeros((1,) + plane.shape[1:], plane.dtype)
    return jnp.concatenate([edge, plane, edge], axis=0)


def unpacked(block):
    strips = [block[:, 64 * k : 64 * k + 64] for k in range(4)]
    return jnp.concatenate(strips, axis=0).reshape(32, 16, 64)


def packed(plane):
    return jnp.concatenate([plane[128 * k : 128 * k + 128] for k in range(4)], axis=1)


def position():
    row = 2 * lax.axis_index("z") + lax.axis_index("yl")
    return lax.axis_index("c"), lax.axis_index("yh"), lax.axis_index("x"), row


def ordered(first, inner, outer):
    return jnp.where(first, outer, inner), jnp.where(first, inner, outer)


def pack_kernel(own, cot, inner, outer):
    place = position()
    first = place[0] == 0
    low, high = own[0].reshape(256, 256), own[1].reshape(256, 256)
    inner[:256] = jnp.where(first, high, low)
    outer[:256] = jnp.where(first, low, high)
    flat = cot[0].reshape(512, 64)
    inner[256:] = packed(flat)
    outer[256:] = packed(flat)


def stage_kernel(token, wc_hbm, own_hbm, cot_hbm, wc, own, cot, sems):
    pairs = ((wc_hbm, wc), (own_hbm, own), (cot_hbm, cot))
    copies = [pltpu.make_async_copy(*pair, sems.at[k]) for k, pair in enumerate(pairs)]
    for copy in copies:
        copy.start()
    for copy in copies:
        copy.wait()


def planes_of(place, own, inner, outer):
    lo, hi = ordered(place[0] == 0, inner[:256], outer[:256])
    return lo.reshape(8, 32, 256), own[0], own[1], hi.reshape(8, 32, 256)


def edge_kernel(own, inner, outer, yinner, youter):
    place = position()
    first = lax.rem(place[3], 2) == 0
    for x, plane in enumerate(planes_of(place, own, inner, outer)):
        low, high = plane[:2].reshape(64, 256), plane[6:].reshape(64, 256)
        yinner[64 * x : 64 * x + 64] = jnp.where(first, high, low)
        youter[64 * x : 64 * x + 64] = jnp.where(first, low, high)


def whole_plane(place, plane, yinner, youter, x):
    rows = slice(64 * x, 64 * x + 64)
    below, above = ordered(lax.rem(place[3], 2) == 0, yinner[rows], youter[rows])
    return jnp.concatenate(
        [below.reshape(2, 32, 256), plane, above.reshape(2, 32, 256)], axis=0
    )


def coarse_back_kernel(cot, inner, outer, w, partial, wide, padded):
    place = position()
    lo, hi = ordered(place[0] == 0, inner[256:], outer[256:])
    for x, plane in enumerate((unpacked(lo), cot[0], unpacked(hi))):
        wide[x] = along_depth(pad_rows(plane), -1)
    total = None
    for k in range(9):
        a, b = divmod(k, 3)
        window = wide[2 - a, 2 - b : 34 - b].reshape(512, 192)
        term = jnp.dot(window, w[k], preferred_element_type=F32)
        total = term if k == 0 else total + term
    padded[:16] = jnp.zeros((16, 256), BF)
    padded[16:528] = total.astype(BF)
    padded[528:] = jnp.zeros((16, 256), BF)
    for k in range(8):
        partial[k] = padded[64 * k : 64 * k + 96]


def fine_forward_kernel(
    own, inner, outer, yinner, youter, w, sent, slope, far, wide, pre, sums,
):
    place = position()
    for x, plane in enumerate(planes_of(place, own, inner, outer)):
        plane = whole_plane(place, plane, yinner, youter, x)
        wide[x] = along_depth(plane, 1)

        @pl.when(place[0] == x // 2)
        def _():
            far[320 * (x % 2) : 320 * (x % 2) + 320] = plane[1:11].reshape(320, 256)

    far[640:] = outer[256:]
    for k in range(9):
        a, b = divmod(k, 3)
        window = wide[a : a + 2, b : b + 10].reshape(640, 768)
        term = jnp.dot(window, w[k], preferred_element_type=F32)
        pre[...] = term if k == 0 else pre[...] + term
    for y in range(6):
        total = jnp.zeros((32, 256), F32)
        for x in range(2):
            for row in (2 * y - 1, 2 * y):
                if 0 <= row < 10:
                    at = x * 320 + row * 32
                    value = pre[at : at + 32]
                    sigma = 1.0 / (1.0 + jnp.exp(-value))
                    total = total + (value * sigma).astype(BF).astype(F32)
                    slope[at : at + 32] = 0.125 * sigma * (1.0 + value * (1.0 - sigma))
        if 0 < y < 5:
            sums[0, y * 32 - 32 : y * 32] = total[:, :128]
            sums[1, y * 32 - 32 : y * 32] = total[:, 128:]
    pooled = []
    for side in range(2):
        even = sums[side, pl.ds(0, 64, stride=2)]
        odd = sums[side, pl.ds(1, 64, stride=2)]
        pooled.append(((even + odd) * 0.125).astype(BF))
    pooled = jnp.concatenate(pooled, axis=1)
    for k in range(8):
        sent[k] = pooled


def fine_grad_kernel(parts, slope, grad, spread):
    place = position()
    for y in range(6):
        rows = slice(16 * y, 16 * y + 16)
        total = parts[0, rows].astype(F32)
        for k in range(1, 8):
            total = total + parts[k, rows].astype(F32)
        total = total.astype(BF).astype(F32)
        if y == 0:
            total = jnp.where(place[3] > 0, total, 0.0)
        if y == 5:
            total = jnp.where(place[3] < 7, total, 0.0)
        for side in range(2):
            half = total[:, side * 128 : side * 128 + 128]
            spread[side, pl.ds(32 * y, 16, stride=2)] = half
            spread[side, pl.ds(32 * y + 1, 16, stride=2)] = half
        at = slice(y * 32, y * 32 + 32)
        wide = jnp.concatenate([spread[0, at], spread[1, at]], axis=1)
        for x in range(2):
            for row in (2 * y - 1, 2 * y):
                if 0 <= row < 10:
                    at = x * 320 + row * 32
                    grad[at : at + 32] = (wide * slope[at : at + 32]).astype(BF)


def fine_weight_kernel(
    own, inner, outer, yinner, youter, far, grad, other, terms, wide, turned, total
):
    place = position()
    for core in range(2):

        @pl.when(place[0] == core)
        def _():
            planes, windows = set(), set()
            sides = [side[:256].reshape(8, 32, 256) for side in (inner, outer)]
            blocks = (sides[1 - core], own[0], own[1], sides[core])

            def prepare(bc, slot):
                if (bc, slot) in windows:
                    return
                windows.add((bc, slot))
                if slot not in planes:
                    planes.add(slot)
                    x = slot - 2 * core
                    if 0 <= x < 4:
                        rows = whole_plane(place, blocks[x], yinner, youter, x)[1:11]
                    else:
                        at = 320 * (slot % 2)
                        rows = far[at : at + 320].reshape(10, 32, 256)
                    wide[slot] = along_depth(rows, 1)
                b, c = divmod(bc, 3)
                window = wide[slot, b : b + 8, :, c * 256 : c * 256 + 256]
                turned[bc, slot] = window.reshape(256, 256).T

            pair = (grad, other) if core == 0 else (other, grad)
            right = jnp.concatenate(
                [side[at : at + 256] for side in pair for at in (32, 352)], axis=0
            )
            for k in range(8):
                at = 432 * (2 * k + core)
                end = at + 432
                pieces = []
                while at < end:
                    tap, low = divmod(at, 256)
                    high = min(256, low + end - at)
                    a, bc = divmod(tap, 9)
                    for plane in range(4):
                        prepare(bc, a + plane)
                    strips = [turned[bc, a + plane, low:high] for plane in range(4)]
                    pieces.append(jnp.concatenate(strips, axis=1))
                    at += high - low
                left = jnp.concatenate(pieces, axis=0)
                total[k % 2] = jnp.dot(left, right, preferred_element_type=F32)
                for f in range(8):
                    terms[k * 8 + f] = total[k % 2, f * 54 : f * 54 + 54].astype(BF)


def fine_back_kernel(grad, other, w, total, rest, wide):
    place = position()
    first = place[0] == 0
    none = jnp.zeros((320, 256), BF)
    planes = (
        jnp.where(first, none, other[320:]),
        grad[:320],
        grad[320:],
        jnp.where(first, other[:320], none),
    )
    for x, plane in enumerate(planes):
        wide[x] = along_depth(plane.reshape(10, 32, 256), -1)
    for k in range(9):
        a, b = divmod(k, 3)
        window = wide[2 - a : 4 - a, 2 - b : 10 - b].reshape(512, 768)
        right = jnp.concatenate([w[k, 0], w[k, 1], w[k, 2]], axis=1)
        term = lax.dot_general(window, right, (((1,), (1,)), ((), ())), preferred_element_type=F32)
        total[...] = term if k == 0 else total[...] + term
    for b in range(3):
        for c in range(3):
            at = slice(256 * c, 256 * c + 256)
            rest[b, :, at] = jnp.where(first, w[6 + b, c], w[b, c])


def fine_rest_kernel(total, outer, rest, out):
    place = position()
    wide = along_depth(outer[:320].reshape(10, 32, 256), -1)
    more = None
    for b in range(3):
        window = wide[2 - b : 10 - b].reshape(256, 768)
        term = lax.dot_general(
            window, rest[b], (((1,), (1,)), ((), ())), preferred_element_type=F32
        )
        more = term if b == 0 else more + term
    first = place[0] == 0
    out[:256] = (total[:256] + jnp.where(first, more, 0.0)).astype(BF)
    out[256:] = (total[256:] + jnp.where(first, 0.0, more)).astype(BF)


def coarse_weight_kernel(slab, other, wide, far, terms, outer, total):
    place = position()
    outer[...] = along_depth(pad_rows(unpacked(far[640:768])), -1)
    left = jnp.concatenate([slab[...].T, other[...].T], axis=1)
    for core in range(2):

        @pl.when(place[0] == core)
        def _():
            for k in range(9):
                a, b = divmod(k, 3)
                rows = slice(2 - b, 34 - b)
                at = 2 - a + (1 if core == 0 else -1)
                across = wide[at, rows] if 0 <= at < 3 else outer[rows]
                right = jnp.concatenate(
                    [wide[2 - a, rows].reshape(512, 192), across.reshape(512, 192)], axis=0
                )
                term = jnp.dot(left, right, preferred_element_type=F32)
                for c in range(3):
                    row = (3 * k + c) * 256
                    total[row : row + 256] = term[:, c * 64 : c * 64 + 64]
            for block in range(8):
                x, yh = divmod(block, 2)
                row = (2 * block + core) * 432
                upper = total[row : row + 224]
                lower = jnp.concatenate(
                    [total[row + 224 : row + 432], jnp.zeros((16, 64), F32)], axis=0
                )
                at = lax.rem(4 + x - place[2], 4) * 2 + lax.rem(place[1] + yh, 2)
                terms[at] = jnp.concatenate([upper, lower], axis=1).astype(BF)


def coarse_forward_kernel(slab, w, grad, own, inner, outer, wide):
    place = position()
    first = place[0] == 0
    outer[:320] = jnp.where(first, grad[:320], grad[320:])
    wide[...] = along_depth(pad_rows(slab[...].reshape(32, 16, 256)), 1)
    total = None
    for b in range(3):
        columns = []
        for a in range(3):
            turned = w[3 * a + b].T
            columns.append(
                jnp.concatenate([turned[:, 64 * c : 64 * c + 64] for c in range(3)], axis=0)
            )
        right = jnp.concatenate(columns, axis=1)
        window = wide[b : b + 32].reshape(512, 768)
        term = jnp.dot(window, right, preferred_element_type=F32)
        total = term if b == 0 else total + term
    own[...] = total[:, 64:128]
    up, down = packed(total[:, :64]).astype(BF), packed(total[:, 128:]).astype(BF)
    inner[...] = jnp.where(first, up, down)
    outer[320:] = jnp.where(first, down, up)


def coarse_out_kernel(own, inner, outer, out):
    for k in range(4):
        rows, columns = slice(128 * k, 128 * k + 128), slice(64 * k, 64 * k + 64)
        total = own[rows] + inner[:, columns].astype(F32) + outer[320:, columns].astype(F32)
        out[rows] = total.astype(BF)


def fine_sum_kernel(scale, parts, out):
    total = parts[0].astype(F32)
    for k in range(1, 64):
        total = total + parts[k].astype(F32)
    total = total * scale
    out[pl.ds(0, 54, stride=2)] = total[:, :128]
    out[pl.ds(1, 54, stride=2)] = total[:, 128:]


def quad_kernel(own, first, second, third, out):
    total = own[...].astype(F32) + first[...].astype(F32)
    total = total + second[...].astype(F32) + third[...].astype(F32)
    out[...] = total.astype(BF)


def coarse_sum_kernel(scale, own, other, out):
    total = own[:224].astype(F32) + other[...].astype(F32)
    total = total * scale
    out[...] = jnp.concatenate([total[:, :64], total[:208, 64:]], axis=0).T


def swap(inner, outer, axis):
    partner = axis[-1]
    pairs = [(i, i + 1) for i in range(1, lax.axis_size(axis) - 1, 2)]
    pairs += [(j, i) for i, j in pairs]
    return lax.ppermute(inner, partner, SWAP), lax.ppermute(outer, axis, pairs)


def body(inputs, weight_fine, weight_coarse, cotangent):
    cells = 65536
    turned_coarse = jnp.swapaxes(weight_coarse, 1, 2).reshape(9, 192, 256)

    pack = call(pack_kernel, (array(384, 256), array(384, 256)), [VMEM] * 2, limit=60)
    inner, outer = pack(inputs, cotangent)
    staged = call(
        stage_kernel,
        (array(9, 192, 256), array(2, 8, 32, 256), array(1, 32, 16, 64)),
        [ANY] * 4,
        [pltpu.SemaphoreType.DMA((3,))],
    )(inner, turned_coarse, inputs, cotangent)
    inner, outer = swap(inner, outer, SP)
    inner, outer, staged = lax.optimization_barrier((inner, outer, staged))
    near_coarse, near_inputs, near_cotangent = staged
    edge = call(edge_kernel, (array(256, 256), array(256, 256)), [VMEM] * 3)
    yinner, youter = swap(*edge(near_inputs, inner, outer), FL)
    partial, wide_cot = call(
        coarse_back_kernel,
        (array(8, 96, 256), array(3, 34, 16, 192)),
        [VMEM] * 4,
        [pltpu.VMEM((544, 256), BF)],
    )(near_cotangent, inner, outer, near_coarse)
    partial, yinner, youter = lax.optimization_barrier((partial, yinner, youter))
    parts = lax.all_to_all(partial, FL, 0, 0, tiled=True)
    blocks = (inputs, inner, outer, yinner, youter)
    sent, slope, far = call(
        fine_forward_kernel,
        (array(8, 64, 256), array(640, 256, dtype=F32), array(768, 256)),
        [VMEM] * 6,
        [
            pltpu.VMEM((4, 12, 32, 768), BF),
            pltpu.VMEM((640, 256), F32),
            pltpu.VMEM((2, 128, 128), F32),
        ],
    )(*blocks, weight_fine.reshape(9, 768, 256))
    far = lax.ppermute(far, "c", SWAP)
    got = lax.all_to_all(sent, FL, 0, 0, tiled=True)
    slab = got.reshape(512, 256)
    grad = call(
        fine_grad_kernel,
        array(640, 256),
        [VMEM] * 2,
        [pltpu.VMEM((2, 192, 128), F32)],
    )(parts, slope)
    other = lax.ppermute(grad, "c", SWAP)
    terms = call(
        fine_weight_kernel,
        array(64, 54, 256),
        [VMEM] * 8,
        [
            pltpu.VMEM((6, 10, 32, 768), BF),
            pltpu.VMEM((9, 6, 256, 256), BF),
            pltpu.VMEM((2, 432, 256), F32),
        ],
        limit=24,
    )(*blocks, far, grad, other)
    terms, slab = lax.optimization_barrier((terms, slab))
    spread = lax.all_to_all(terms, ("x", "yh", "z", "yl"), 0, 0, tiled=True)

    across = lax.ppermute(slab, "c", SWAP)
    coarse_terms = call(
        coarse_weight_kernel,
        array(8, 224, 128),
        [VMEM] * 4,
        [pltpu.VMEM((34, 16, 192), BF), pltpu.VMEM((6912, 64), F32)],
    )(slab, across, wide_cot, far)
    coarse_terms, other = lax.optimization_barrier((coarse_terms, other))
    coarse_terms = coarse_terms.reshape(4, 448, 128)
    arrived = [
        lax.ppermute(coarse_terms[step], "x", [(i, (i + step) % 4) for i in range(4)])
        for step in range(1, 4)
    ]
    coarse_terms = call(quad_kernel, array(448, 128), [VMEM] * 4)(coarse_terms[0], *arrived)
    centre, inner, outer = call(
        coarse_forward_kernel,
        (array(512, 64, dtype=F32), array(128, 256), array(448, 256)),
        [VMEM] * 3,
        [pltpu.VMEM((34, 16, 768), BF)],
    )(slab, turned_coarse, grad)
    inner, outer = swap(inner, outer, SP)
    total, rest = call(
        fine_back_kernel,
        (array(512, 256, dtype=F32), array(3, 256, 768)),
        [VMEM] * 3,
        [pltpu.VMEM((4, 10, 32, 768), BF)],
        flops=2**31,
    )(grad, other, weight_fine.reshape(9, 3, 256, 256))
    coarse_terms, inner, outer, total = lax.optimization_barrier(
        (coarse_terms, inner, outer, total)
    )
    grad_input = call(fine_rest_kernel, array(512, 256), [VMEM] * 3, flops=2**30)(total, outer, rest)
    arrived = lax.ppermute(coarse_terms[224:], "yh", SWAP)
    coarse_out = call(coarse_out_kernel, array(512, 64), [VMEM] * 3)(centre, inner, outer)
    grad_fine = call(
        functools.partial(fine_sum_kernel, 1.0 / math.sqrt(cells)),
        array(108, 128, dtype=F32),
        [VMEM],
    )(spread)
    grad_fine, arrived = lax.optimization_barrier((grad_fine, arrived))
    grad_coarse = call(
        functools.partial(coarse_sum_kernel, 1.0 / math.sqrt(cells // 8)),
        array(64, 432, dtype=F32),
        [VMEM] * 2,
    )(coarse_terms, arrived)
    return (
        coarse_out.reshape(1, 32, 16, 64),
        grad_input.reshape(2, 8, 32, 256),
        grad_fine.reshape(-1),
        grad_coarse.T,
    )


def solution(mesh):
    fine_mesh = jax.sharding.Mesh(mesh.devices.reshape(4, 2, 2, 4, 2), SP + FL)
    return jax.shard_map(
        body,
        mesh=fine_mesh,
        in_specs=(P(SP, FL, None, None), P(), P(None, None, FL), P(SP, None, None, FL)),
        out_specs=(P(SP, None, None, FL), P(SP, FL, None, None), P(SP + FL), P(SP, FL)),
        check_vma=False,
    )
```

```python
import functools
import math

import jax
import jax.numpy as jnp
from jax import lax
from jax.experimental import pallas as pl
from jax.experimental.pallas import tpu as pltpu
from jax.sharding import PartitionSpec as P

SP = ("x", "yh", "c")
FL = ("z", "yl")
BF = jnp.bfloat16
F32 = jnp.float32
VMEM = pl.BlockSpec(memory_space=pltpu.VMEM)
ANY = pl.BlockSpec(memory_space=pl.ANY)
SWAP = [(0, 1), (1, 0)]


def call(kernel, out_shape, in_specs, scratch=(), limit=12, flops=2**20):
    return pl.pallas_call(
        kernel,
        out_shape=out_shape,
        in_specs=in_specs,
        out_specs=jax.tree.map(lambda _: VMEM, out_shape),
        scratch_shapes=list(scratch),
        compiler_params=pltpu.CompilerParams(vmem_limit_bytes=limit * 2**20),
        cost_estimate=pl.CostEstimate(flops=flops, bytes_accessed=2**16, transcendentals=0),
    )


def array(*shape, dtype=BF):
    return jax.ShapeDtypeStruct(shape, dtype)


def along_depth(rows, order):
    count, depth, width = rows.shape
    flat = rows.astype(F32).reshape(count * depth, width)
    place = lax.broadcasted_iota(jnp.int32, flat.shape, 0) & (depth - 1)
    before = jnp.where(place == 0, 0.0, pltpu.roll(flat, 1, 0)).astype(BF)
    after = jnp.where(place == depth - 1, 0.0, pltpu.roll(flat, count * depth - 1, 0)).astype(BF)
    middle = flat.astype(BF)
    trio = (before, middle, after) if order > 0 else (after, middle, before)
    return jnp.concatenate(trio, axis=1).reshape(count, depth, 3 * width)


def pad_rows(plane):
    edge = jnp.zeros((1,) + plane.shape[1:], plane.dtype)
    return jnp.concatenate([edge, plane, edge], axis=0)


def unpacked(block):
    strips = [block[:, 64 * k : 64 * k + 64] for k in range(4)]
    return jnp.concatenate(strips, axis=0).reshape(32, 16, 64)


def packed(plane):
    return jnp.concatenate([plane[128 * k : 128 * k + 128] for k in range(4)], axis=1)


def position():
    row = 2 * lax.axis_index("z") + lax.axis_index("yl")
    return lax.axis_index("c"), lax.axis_index("yh"), lax.axis_index("x"), row


def ordered(first, inner, outer):
    return jnp.where(first, outer, inner), jnp.where(first, inner, outer)


def pack_kernel(own, cot, inner, outer):
    place = position()
    first = place[0] == 0
    low, high = own[0].reshape(256, 256), own[1].reshape(256, 256)
    inner[:256] = jnp.where(first, high, low)
    outer[:256] = jnp.where(first, low, high)
    flat = cot[0].reshape(512, 64)
    inner[256:] = packed(flat)
    outer[256:] = packed(flat)


def stage_kernel(token, wc_hbm, own_hbm, cot_hbm, wc, own, cot, sems):
    pairs = ((wc_hbm, wc), (own_hbm, own), (cot_hbm, cot))
    copies = [pltpu.make_async_copy(*pair, sems.at[k]) for k, pair in enumerate(pairs)]
    for copy in copies:
        copy.start()
    for copy in copies:
        copy.wait()


def planes_of(place, own, inner, outer):
    lo, hi = ordered(place[0] == 0, inner[:256], outer[:256])
    return lo.reshape(8, 32, 256), own[0], own[1], hi.reshape(8, 32, 256)


def edge_kernel(own, inner, outer, yinner, youter):
    place = position()
    first = lax.rem(place[3], 2) == 0
    for x, plane in enumerate(planes_of(place, own, inner, outer)):
        low, high = plane[:2].reshape(64, 256), plane[6:].reshape(64, 256)
        yinner[64 * x : 64 * x + 64] = jnp.where(first, high, low)
        youter[64 * x : 64 * x + 64] = jnp.where(first, low, high)


def whole_plane(place, plane, yinner, youter, x):
    rows = slice(64 * x, 64 * x + 64)
    below, above = ordered(lax.rem(place[3], 2) == 0, yinner[rows], youter[rows])
    return jnp.concatenate(
        [below.reshape(2, 32, 256), plane, above.reshape(2, 32, 256)], axis=0
    )


def coarse_back_kernel(cot, inner, outer, w, partial, wide, padded):
    place = position()
    lo, hi = ordered(place[0] == 0, inner[256:], outer[256:])
    for x, plane in enumerate((unpacked(lo), cot[0], unpacked(hi))):
        wide[x] = along_depth(pad_rows(plane), -1)
    total = None
    for k in range(9):
        a, b = divmod(k, 3)
        window = wide[2 - a, 2 - b : 34 - b].reshape(512, 192)
        term = jnp.dot(window, w[k], preferred_element_type=F32)
        total = term if k == 0 else total + term
    padded[:16] = jnp.zeros((16, 256), BF)
    padded[16:528] = total.astype(BF)
    padded[528:] = jnp.zeros((16, 256), BF)
    for k in range(8):
        partial[k] = padded[64 * k : 64 * k + 96]


def fine_forward_kernel(
    own, inner, outer, yinner, youter, w, sent, slope, far, wide, pre, sums,
):
    place = position()
    for x, plane in enumerate(planes_of(place, own, inner, outer)):
        plane = whole_plane(place, plane, yinner, youter, x)
        wide[x] = along_depth(plane, 1)

        @pl.when(place[0] == x // 2)
        def _():
            far[320 * (x % 2) : 320 * (x % 2) + 320] = plane[1:11].reshape(320, 256)

    far[640:] = outer[256:]
    for k in range(9):
        a, b = divmod(k, 3)
        window = wide[a : a + 2, b : b + 10].reshape(640, 768)
        term = jnp.dot(window, w[k], preferred_element_type=F32)
        pre[...] = term if k == 0 else pre[...] + term
    for y in range(6):
        total = jnp.zeros((32, 256), F32)
        for x in range(2):
            for row in (2 * y - 1, 2 * y):
                if 0 <= row < 10:
                    at = x * 320 + row * 32
                    value = pre[at : at + 32]
                    sigma = 1.0 / (1.0 + jnp.exp(-value))
                    total = total + (value * sigma).astype(BF).astype(F32)
                    slope[at : at + 32] = 0.125 * sigma * (1.0 + value * (1.0 - sigma))
        if 0 < y < 5:
            sums[0, y * 32 - 32 : y * 32] = total[:, :128]
            sums[1, y * 32 - 32 : y * 32] = total[:, 128:]
    pooled = []
    for side in range(2):
        even = sums[side, pl.ds(0, 64, stride=2)]
        odd = sums[side, pl.ds(1, 64, stride=2)]
        pooled.append(((even + odd) * 0.125).astype(BF))
    pooled = jnp.concatenate(pooled, axis=1)
    for k in range(8):
        sent[k] = pooled


def fine_grad_kernel(parts, slope, grad, spread):
    place = position()
    for y in range(6):
        rows = slice(16 * y, 16 * y + 16)
        total = parts[0, rows].astype(F32)
        for k in range(1, 8):
            total = total + parts[k, rows].astype(F32)
        total = total.astype(BF).astype(F32)
        if y == 0:
            total = jnp.where(place[3] > 0, total, 0.0)
        if y == 5:
            total = jnp.where(place[3] < 7, total, 0.0)
        for side in range(2):
            half = total[:, side * 128 : side * 128 + 128]
            spread[side, pl.ds(32 * y, 16, stride=2)] = half
            spread[side, pl.ds(32 * y + 1, 16, stride=2)] = half
        at = slice(y * 32, y * 32 + 32)
        wide = jnp.concatenate([spread[0, at], spread[1, at]], axis=1)
        for x in range(2):
            for row in (2 * y - 1, 2 * y):
                if 0 <= row < 10:
                    at = x * 320 + row * 32
                    grad[at : at + 32] = (wide * slope[at : at + 32]).astype(BF)


def fine_weight_kernel(
    own, inner, outer, yinner, youter, far, grad, other, terms, wide, turned, total
):
    place = position()
    for core in range(2):

        @pl.when(place[0] == core)
        def _():
            planes, windows = set(), set()
            sides = [side[:256].reshape(8, 32, 256) for side in (inner, outer)]
            blocks = (sides[1 - core], own[0], own[1], sides[core])

            def prepare(bc, slot):
                if (bc, slot) in windows:
                    return
                windows.add((bc, slot))
                if slot not in planes:
                    planes.add(slot)
                    x = slot - 2 * core
                    if 0 <= x < 4:
                        rows = whole_plane(place, blocks[x], yinner, youter, x)[1:11]
                    else:
                        at = 320 * (slot % 2)
                        rows = far[at : at + 320].reshape(10, 32, 256)
                    wide[slot] = along_depth(rows, 1)
                b, c = divmod(bc, 3)
                window = wide[slot, b : b + 8, :, c * 256 : c * 256 + 256]
                turned[bc, slot] = window.reshape(256, 256).T

            pair = (grad, other) if core == 0 else (other, grad)
            right = jnp.concatenate(
                [side[at : at + 256] for side in pair for at in (32, 352)], axis=0
            )
            for k in range(8):
                at = 432 * (2 * k + core)
                end = at + 432
                pieces = []
                while at < end:
                    tap, low = divmod(at, 256)
                    high = min(256, low + end - at)
                    a, bc = divmod(tap, 9)
                    for plane in range(4):
                        prepare(bc, a + plane)
                    strips = [turned[bc, a + plane, low:high] for plane in range(4)]
                    pieces.append(jnp.concatenate(strips, axis=1))
                    at += high - low
                left = jnp.concatenate(pieces, axis=0)
                total[k % 2] = jnp.dot(left, right, preferred_element_type=F32)
                for f in range(8):
                    terms[k * 8 + f] = total[k % 2, f * 54 : f * 54 + 54].astype(BF)


def fine_back_kernel(grad, other, w, total, rest, wide):
    place = position()
    first = place[0] == 0
    none = jnp.zeros((320, 256), BF)
    planes = (
        jnp.where(first, none, other[320:]),
        grad[:320],
        grad[320:],
        jnp.where(first, other[:320], none),
    )
    for x, plane in enumerate(planes):
        wide[x] = along_depth(plane.reshape(10, 32, 256), -1)
    for k in range(9):
        a, b = divmod(k, 3)
        window = wide[2 - a : 4 - a, 2 - b : 10 - b].reshape(512, 768)
        right = jnp.concatenate([w[k, 0], w[k, 1], w[k, 2]], axis=1)
        term = lax.dot_general(window, right, (((1,), (1,)), ((), ())), preferred_element_type=F32)
        total[...] = term if k == 0 else total[...] + term
    for b in range(3):
        for c in range(3):
            at = slice(256 * c, 256 * c + 256)
            rest[b, :, at] = jnp.where(first, w[6 + b, c], w[b, c])


def fine_rest_kernel(total, outer, rest, out):
    place = position()
    wide = along_depth(outer[:320].reshape(10, 32, 256), -1)
    more = None
    for b in range(3):
        window = wide[2 - b : 10 - b].reshape(256, 768)
        term = lax.dot_general(
            window, rest[b], (((1,), (1,)), ((), ())), preferred_element_type=F32
        )
        more = term if b == 0 else more + term
    first = place[0] == 0
    out[:256] = (total[:256] + jnp.where(first, more, 0.0)).astype(BF)
    out[256:] = (total[256:] + jnp.where(first, 0.0, more)).astype(BF)


def coarse_weight_kernel(slab, other, wide, far, terms, outer, total):
    place = position()
    outer[...] = along_depth(pad_rows(unpacked(far[640:768])), -1)
    left = jnp.concatenate([slab[...].T, other[...].T], axis=1)
    for core in range(2):

        @pl.when(place[0] == core)
        def _():
            for k in range(9):
                a, b = divmod(k, 3)
                rows = slice(2 - b, 34 - b)
                at = 2 - a + (1 if core == 0 else -1)
                across = wide[at, rows] if 0 <= at < 3 else outer[rows]
                right = jnp.concatenate(
                    [wide[2 - a, rows].reshape(512, 192), across.reshape(512, 192)], axis=0
                )
                term = jnp.dot(left, right, preferred_element_type=F32)
                for c in range(3):
                    row = (3 * k + c) * 256
                    total[row : row + 256] = term[:, c * 64 : c * 64 + 64]
    for step in range(4):
        for c in range(2):
            block = lax.rem(place[2] + step, 4) * 4 + lax.rem(place[1] + place[0], 2) * 2 + c
            row = pl.multiple_of(block * 432, 16)
            upper = total[pl.ds(row, 224)]
            lower = total[pl.ds(pl.multiple_of(row + 224, 16), 208)]
            lower = jnp.concatenate([lower, jnp.zeros((16, 64), F32)], axis=0)
            both = jnp.concatenate([upper, lower], axis=1).astype(BF)
            terms[step, 224 * c : 224 * c + 224] = both


def coarse_forward_kernel(slab, w, grad, own, inner, outer, wide):
    place = position()
    first = place[0] == 0
    outer[:320] = jnp.where(first, grad[:320], grad[320:])
    wide[...] = along_depth(pad_rows(slab[...].reshape(32, 16, 256)), 1)
    total = None
    for b in range(3):
        columns = []
        for a in range(3):
            turned = w[3 * a + b].T
            columns.append(
                jnp.concatenate([turned[:, 64 * c : 64 * c + 64] for c in range(3)], axis=0)
            )
        right = jnp.concatenate(columns, axis=1)
        window = wide[b : b + 32].reshape(512, 768)
        term = jnp.dot(window, right, preferred_element_type=F32)
        total = term if b == 0 else total + term
    own[...] = total[:, 64:128]
    up, down = packed(total[:, :64]).astype(BF), packed(total[:, 128:]).astype(BF)
    inner[...] = jnp.where(first, up, down)
    outer[320:] = jnp.where(first, down, up)


def coarse_out_kernel(own, inner, outer, out):
    for k in range(4):
        rows, columns = slice(128 * k, 128 * k + 128), slice(64 * k, 64 * k + 64)
        total = own[rows] + inner[:, columns].astype(F32) + outer[320:, columns].astype(F32)
        out[rows] = total.astype(BF)


def fine_sum_kernel(scale, parts, out):
    total = parts[0].astype(F32)
    for k in range(1, 64):
        total = total + parts[k].astype(F32)
    total = total * scale
    out[pl.ds(0, 54, stride=2)] = total[:, :128]
    out[pl.ds(1, 54, stride=2)] = total[:, 128:]


def quad_kernel(own, beside, first, second, third, held, sent):
    core = lax.axis_index("c")
    total = jnp.where(core == 0, own[...], beside[...]).astype(F32)
    total = total + first[...].astype(F32) + second[...].astype(F32) + third[...].astype(F32)
    held[...] = jnp.where(core == 0, total[:224], total[224:]).astype(BF)
    sent[...] = jnp.where(core == 0, total[224:], total[:224]).astype(BF)


def coarse_sum_kernel(scale, own, other, out):
    total = own[...].astype(F32) + other[...].astype(F32)
    total = total * scale
    out[...] = jnp.concatenate([total[:, :64], total[:208, 64:]], axis=0).T


def swap(inner, outer, axis):
    partner = axis[-1]
    pairs = [(i, i + 1) for i in range(1, lax.axis_size(axis) - 1, 2)]
    pairs += [(j, i) for i, j in pairs]
    return lax.ppermute(inner, partner, SWAP), lax.ppermute(outer, axis, pairs)


def body(inputs, weight_fine, weight_coarse, cotangent):
    cells = 65536
    turned_coarse = jnp.swapaxes(weight_coarse, 1, 2).reshape(9, 192, 256)

    pack = call(pack_kernel, (array(384, 256), array(384, 256)), [VMEM] * 2, limit=60)
    inner, outer = pack(inputs, cotangent)
    staged = call(
        stage_kernel,
        (array(9, 192, 256), array(2, 8, 32, 256), array(1, 32, 16, 64)),
        [ANY] * 4,
        [pltpu.SemaphoreType.DMA((3,))],
    )(inner, turned_coarse, inputs, cotangent)
    inner, outer = swap(inner, outer, SP)
    inner, outer, staged = lax.optimization_barrier((inner, outer, staged))
    near_coarse, near_inputs, near_cotangent = staged
    edge = call(edge_kernel, (array(256, 256), array(256, 256)), [VMEM] * 3)
    yinner, youter = swap(*edge(near_inputs, inner, outer), FL)
    partial, wide_cot = call(
        coarse_back_kernel,
        (array(8, 96, 256), array(3, 34, 16, 192)),
        [VMEM] * 4,
        [pltpu.VMEM((544, 256), BF)],
    )(near_cotangent, inner, outer, near_coarse)
    partial, yinner, youter = lax.optimization_barrier((partial, yinner, youter))
    parts = lax.all_to_all(partial, FL, 0, 0, tiled=True)
    blocks = (inputs, inner, outer, yinner, youter)
    sent, slope, far = call(
        fine_forward_kernel,
        (array(8, 64, 256), array(640, 256, dtype=F32), array(768, 256)),
        [VMEM] * 6,
        [
            pltpu.VMEM((4, 12, 32, 768), BF),
            pltpu.VMEM((640, 256), F32),
            pltpu.VMEM((2, 128, 128), F32),
        ],
    )(*blocks, weight_fine.reshape(9, 768, 256))
    far = lax.ppermute(far, "c", SWAP)
    got = lax.all_to_all(sent, FL, 0, 0, tiled=True)
    slab = got.reshape(512, 256)
    grad = call(
        fine_grad_kernel,
        array(640, 256),
        [VMEM] * 2,
        [pltpu.VMEM((2, 192, 128), F32)],
    )(parts, slope)
    other = lax.ppermute(grad, "c", SWAP)
    terms = call(
        fine_weight_kernel,
        array(64, 54, 256),
        [VMEM] * 8,
        [
            pltpu.VMEM((6, 10, 32, 768), BF),
            pltpu.VMEM((9, 6, 256, 256), BF),
            pltpu.VMEM((2, 432, 256), F32),
        ],
        limit=24,
    )(*blocks, far, grad, other)
    terms, slab = lax.optimization_barrier((terms, slab))
    spread = lax.all_to_all(terms, ("x", "yh", "z", "yl"), 0, 0, tiled=True)

    across = lax.ppermute(slab, "c", SWAP)
    coarse_terms = call(
        coarse_weight_kernel,
        array(4, 448, 128),
        [VMEM] * 4,
        [pltpu.VMEM((34, 16, 192), BF), pltpu.VMEM((6912, 64), F32)],
    )(slab, across, wide_cot, far)
    coarse_terms, other = lax.optimization_barrier((coarse_terms, other))
    centre, inner, outer = call(
        coarse_forward_kernel,
        (array(512, 64, dtype=F32), array(128, 256), array(448, 256)),
        [VMEM] * 3,
        [pltpu.VMEM((34, 16, 768), BF)],
    )(slab, turned_coarse, grad)
    inner, outer = swap(inner, outer, SP)
    coarse_terms, inner = lax.optimization_barrier((coarse_terms, inner))
    arrived = []
    for step in range(4):
        pairs = [(4 * x + 2 * y, (4 * x + 4 * step) % 16 + 2 * y) for x in range(4) for y in range(2)]
        pairs = [pair for pair in pairs if step > 0]
        for x in range(4):
            pairs += [(4 * x + 2 * y + 1, (4 * x + 4 * step) % 16 + 3 - 2 * y) for y in range(2)]
        arrived.append(lax.ppermute(coarse_terms[step], SP, pairs))
    grad_fine = call(
        functools.partial(fine_sum_kernel, 1.0 / math.sqrt(cells)),
        array(108, 128, dtype=F32),
        [VMEM],
    )(spread)
    grad_fine, arrived = lax.optimization_barrier((grad_fine, arrived))
    held, sent = call(quad_kernel, (array(224, 128), array(224, 128)), [VMEM] * 5)(
        coarse_terms[0], *arrived
    )
    total, rest = call(
        fine_back_kernel,
        (array(512, 256, dtype=F32), array(3, 256, 768)),
        [VMEM] * 3,
        [pltpu.VMEM((4, 10, 32, 768), BF)],
        flops=2**31,
    )(grad, other, weight_fine.reshape(9, 3, 256, 256))
    _, inner, outer, total = lax.optimization_barrier((sent, inner, outer, total))
    grad_input = call(fine_rest_kernel, array(512, 256), [VMEM] * 3, flops=2**30)(total, outer, rest)
    arrived = lax.ppermute(sent, "c", SWAP)
    coarse_out = call(coarse_out_kernel, array(512, 64), [VMEM] * 3)(centre, inner, outer)
    grad_coarse = call(
        functools.partial(coarse_sum_kernel, 1.0 / math.sqrt(cells // 8)),
        array(64, 432, dtype=F32),
        [VMEM] * 2,
    )(held, arrived)
    return (
        coarse_out.reshape(1, 32, 16, 64),
        grad_input.reshape(2, 8, 32, 256),
        grad_fine.reshape(-1),
        grad_coarse.T,
    )


def solution(mesh):
    fine_mesh = jax.sharding.Mesh(mesh.devices.reshape(4, 2, 2, 4, 2), SP + FL)
    return jax.shard_map(
        body,
        mesh=fine_mesh,
        in_specs=(P(SP, FL, None, None), P(), P(None, None, FL), P(SP, None, None, FL)),
        out_specs=(P(SP, None, None, FL), P(SP, FL, None, None), P(SP + FL), P(SP, FL)),
        check_vma=False,
    )
```

```python
import functools
import math

import jax
import jax.numpy as jnp
from jax import lax
from jax.experimental import pallas as pl
from jax.experimental.pallas import tpu as pltpu
from jax.sharding import PartitionSpec as P

SP = ("x", "yh", "c")
FL = ("z", "yl")
BF = jnp.bfloat16
F32 = jnp.float32
VMEM = pl.BlockSpec(memory_space=pltpu.VMEM)
ANY = pl.BlockSpec(memory_space=pl.ANY)
SWAP = [(0, 1), (1, 0)]


def call(kernel, out_shape, in_specs, scratch=(), limit=12, flops=2**20):
    return pl.pallas_call(
        kernel,
        out_shape=out_shape,
        in_specs=in_specs,
        out_specs=jax.tree.map(lambda _: VMEM, out_shape),
        scratch_shapes=list(scratch),
        compiler_params=pltpu.CompilerParams(vmem_limit_bytes=limit * 2**20),
        cost_estimate=pl.CostEstimate(flops=flops, bytes_accessed=2**16, transcendentals=0),
    )


def array(*shape, dtype=BF):
    return jax.ShapeDtypeStruct(shape, dtype)


def along_depth(rows, order):
    count, depth, width = rows.shape
    flat = rows.astype(F32).reshape(count * depth, width)
    place = lax.broadcasted_iota(jnp.int32, flat.shape, 0) & (depth - 1)
    before = jnp.where(place == 0, 0.0, pltpu.roll(flat, 1, 0)).astype(BF)
    after = jnp.where(place == depth - 1, 0.0, pltpu.roll(flat, count * depth - 1, 0)).astype(BF)
    middle = flat.astype(BF)
    trio = (before, middle, after) if order > 0 else (after, middle, before)
    return jnp.concatenate(trio, axis=1).reshape(count, depth, 3 * width)


def pad_rows(plane):
    edge = jnp.zeros((1,) + plane.shape[1:], plane.dtype)
    return jnp.concatenate([edge, plane, edge], axis=0)


def unpacked(block):
    strips = [block[:, 64 * k : 64 * k + 64] for k in range(4)]
    return jnp.concatenate(strips, axis=0).reshape(32, 16, 64)


def packed(plane):
    return jnp.concatenate([plane[128 * k : 128 * k + 128] for k in range(4)], axis=1)


def position():
    row = 2 * lax.axis_index("z") + lax.axis_index("yl")
    return lax.axis_index("c"), lax.axis_index("yh"), lax.axis_index("x"), row


def ordered(first, inner, outer):
    return jnp.where(first, outer, inner), jnp.where(first, inner, outer)


def pack_kernel(own, cot, inner, outer):
    place = position()
    first = place[0] == 0
    low, high = own[0].reshape(256, 256), own[1].reshape(256, 256)
    inner[:256] = jnp.where(first, high, low)
    outer[:256] = jnp.where(first, low, high)
    flat = cot[0].reshape(512, 64)
    inner[256:] = packed(flat)
    outer[256:] = packed(flat)


def stage_kernel(token, wc_hbm, own_hbm, cot_hbm, wc, own, cot, sems):
    pairs = ((wc_hbm, wc), (own_hbm, own), (cot_hbm, cot))
    copies = [pltpu.make_async_copy(*pair, sems.at[k]) for k, pair in enumerate(pairs)]
    for copy in copies:
        copy.start()
    for copy in copies:
        copy.wait()


def planes_of(place, own, inner, outer):
    lo, hi = ordered(place[0] == 0, inner[:256], outer[:256])
    return lo.reshape(8, 32, 256), own[0], own[1], hi.reshape(8, 32, 256)


def edge_kernel(own, inner, outer, yinner, youter):
    place = position()
    first = lax.rem(place[3], 2) == 0
    for x, plane in enumerate(planes_of(place, own, inner, outer)):
        low, high = plane[:2].reshape(64, 256), plane[6:].reshape(64, 256)
        yinner[64 * x : 64 * x + 64] = jnp.where(first, high, low)
        youter[64 * x : 64 * x + 64] = jnp.where(first, low, high)


def whole_plane(place, plane, yinner, youter, x):
    rows = slice(64 * x, 64 * x + 64)
    below, above = ordered(lax.rem(place[3], 2) == 0, yinner[rows], youter[rows])
    return jnp.concatenate(
        [below.reshape(2, 32, 256), plane, above.reshape(2, 32, 256)], axis=0
    )


def coarse_back_kernel(cot, inner, outer, w, partial, wide, padded):
    place = position()
    lo, hi = ordered(place[0] == 0, inner[256:], outer[256:])
    for x, plane in enumerate((unpacked(lo), cot[0], unpacked(hi))):
        wide[x] = along_depth(pad_rows(plane), -1)
    total = None
    for k in range(9):
        a, b = divmod(k, 3)
        window = wide[2 - a, 2 - b : 34 - b].reshape(512, 192)
        term = jnp.dot(window, w[k], preferred_element_type=F32)
        total = term if k == 0 else total + term
    padded[:16] = jnp.zeros((16, 256), BF)
    padded[16:528] = total.astype(BF)
    padded[528:] = jnp.zeros((16, 256), BF)
    for k in range(8):
        partial[k] = padded[64 * k : 64 * k + 96]


def fine_forward_kernel(
    own, inner, outer, yinner, youter, w, sent, slope, far, wide, pre, sums,
):
    place = position()
    for x, plane in enumerate(planes_of(place, own, inner, outer)):
        plane = whole_plane(place, plane, yinner, youter, x)
        wide[x] = along_depth(plane, 1)

        @pl.when(place[0] == x // 2)
        def _():
            far[320 * (x % 2) : 320 * (x % 2) + 320] = plane[1:11].reshape(320, 256)

    far[640:] = outer[256:]
    for k in range(9):
        a, b = divmod(k, 3)
        window = wide[a : a + 2, b : b + 10].reshape(640, 768)
        term = jnp.dot(window, w[k], preferred_element_type=F32)
        pre[...] = term if k == 0 else pre[...] + term
    for y in range(6):
        total = jnp.zeros((32, 256), F32)
        for x in range(2):
            for row in (2 * y - 1, 2 * y):
                if 0 <= row < 10:
                    at = x * 320 + row * 32
                    value = pre[at : at + 32]
                    sigma = 1.0 / (1.0 + jnp.exp(-value))
                    total = total + (value * sigma).astype(BF).astype(F32)
                    slope[at : at + 32] = 0.125 * sigma * (1.0 + value * (1.0 - sigma))
        if 0 < y < 5:
            sums[0, y * 32 - 32 : y * 32] = total[:, :128]
            sums[1, y * 32 - 32 : y * 32] = total[:, 128:]
    pooled = []
    for side in range(2):
        even = sums[side, pl.ds(0, 64, stride=2)]
        odd = sums[side, pl.ds(1, 64, stride=2)]
        pooled.append(((even + odd) * 0.125).astype(BF))
    pooled = jnp.concatenate(pooled, axis=1)
    for k in range(8):
        sent[k] = pooled


def fine_grad_kernel(parts, slope, grad, spread):
    place = position()
    for y in range(6):
        rows = slice(16 * y, 16 * y + 16)
        total = parts[0, rows].astype(F32)
        for k in range(1, 8):
            total = total + parts[k, rows].astype(F32)
        total = total.astype(BF).astype(F32)
        if y == 0:
            total = jnp.where(place[3] > 0, total, 0.0)
        if y == 5:
            total = jnp.where(place[3] < 7, total, 0.0)
        for side in range(2):
            half = total[:, side * 128 : side * 128 + 128]
            spread[side, pl.ds(32 * y, 16, stride=2)] = half
            spread[side, pl.ds(32 * y + 1, 16, stride=2)] = half
        at = slice(y * 32, y * 32 + 32)
        wide = jnp.concatenate([spread[0, at], spread[1, at]], axis=1)
        for x in range(2):
            for row in (2 * y - 1, 2 * y):
                if 0 <= row < 10:
                    at = x * 320 + row * 32
                    grad[at : at + 32] = (wide * slope[at : at + 32]).astype(BF)


def fine_weight_kernel(
    own, inner, outer, yinner, youter, far, grad, other, terms, wide, turned, total
):
    place = position()
    for core in range(2):

        @pl.when(place[0] == core)
        def _():
            planes, windows = set(), set()
            sides = [side[:256].reshape(8, 32, 256) for side in (inner, outer)]
            blocks = (sides[1 - core], own[0], own[1], sides[core])

            def prepare(bc, slot):
                if (bc, slot) in windows:
                    return
                windows.add((bc, slot))
                if slot not in planes:
                    planes.add(slot)
                    x = slot - 2 * core
                    if 0 <= x < 4:
                        rows = whole_plane(place, blocks[x], yinner, youter, x)[1:11]
                    else:
                        at = 320 * (slot % 2)
                        rows = far[at : at + 320].reshape(10, 32, 256)
                    wide[slot] = along_depth(rows, 1)
                b, c = divmod(bc, 3)
                window = wide[slot, b : b + 8, :, c * 256 : c * 256 + 256]
                turned[bc, slot] = window.reshape(256, 256).T

            pair = (grad, other) if core == 0 else (other, grad)
            right = jnp.concatenate(
                [side[at : at + 256] for side in pair for at in (32, 352)], axis=0
            )
            for k in range(8):
                at = 432 * (2 * k + core)
                end = at + 432
                pieces = []
                while at < end:
                    tap, low = divmod(at, 256)
                    high = min(256, low + end - at)
                    a, bc = divmod(tap, 9)
                    for plane in range(4):
                        prepare(bc, a + plane)
                    strips = [turned[bc, a + plane, low:high] for plane in range(4)]
                    pieces.append(jnp.concatenate(strips, axis=1))
                    at += high - low
                left = jnp.concatenate(pieces, axis=0)
                total[k % 2] = jnp.dot(left, right, preferred_element_type=F32)
                for f in range(8):
                    terms[k * 8 + f] = total[k % 2, f * 54 : f * 54 + 54].astype(BF)


def fine_back_kernel(grad, other, w, total, rest, wide):
    place = position()
    first = place[0] == 0
    none = jnp.zeros((320, 256), BF)
    planes = (
        jnp.where(first, none, other[320:]),
        grad[:320],
        grad[320:],
        jnp.where(first, other[:320], none),
    )
    for x, plane in enumerate(planes):
        wide[x] = along_depth(plane.reshape(10, 32, 256), -1)
    for k in range(9):
        a, b = divmod(k, 3)
        window = wide[2 - a : 4 - a, 2 - b : 10 - b].reshape(512, 768)
        right = jnp.concatenate([w[k, 0], w[k, 1], w[k, 2]], axis=1)
        term = lax.dot_general(window, right, (((1,), (1,)), ((), ())), preferred_element_type=F32)
        total[...] = term if k == 0 else total[...] + term
    for b in range(3):
        for c in range(3):
            at = slice(256 * c, 256 * c + 256)
            rest[b, :, at] = jnp.where(first, w[6 + b, c], w[b, c])


def last_kernel(scale, total, outer, rest, centre, inner, parts, out, coarse, fine):
    place = position()
    wide = along_depth(outer[:320].reshape(10, 32, 256), -1)
    more = None
    for b in range(3):
        window = wide[2 - b : 10 - b].reshape(256, 768)
        term = lax.dot_general(
            window, rest[b], (((1,), (1,)), ((), ())), preferred_element_type=F32
        )
        more = term if b == 0 else more + term
    first = place[0] == 0
    out[:256] = (total[:256] + jnp.where(first, more, 0.0)).astype(BF)
    out[256:] = (total[256:] + jnp.where(first, 0.0, more)).astype(BF)
    for k in range(4):
        rows, columns = slice(128 * k, 128 * k + 128), slice(64 * k, 64 * k + 64)
        plane = centre[rows] + inner[:, columns].astype(F32) + outer[320:, columns].astype(F32)
        coarse[rows] = plane.astype(BF)
    terms = parts[0].astype(F32)
    for k in range(1, 64):
        terms = terms + parts[k].astype(F32)
    terms = terms * scale
    fine[pl.ds(0, 54, stride=2)] = terms[:, :128]
    fine[pl.ds(1, 54, stride=2)] = terms[:, 128:]


def coarse_weight_kernel(slab, other, wide, far, terms, outer, total):
    place = position()
    outer[...] = along_depth(pad_rows(unpacked(far[640:768])), -1)
    left = jnp.concatenate([slab[...].T, other[...].T], axis=1)
    for core in range(2):

        @pl.when(place[0] == core)
        def _():
            for k in range(9):
                a, b = divmod(k, 3)
                rows = slice(2 - b, 34 - b)
                at = 2 - a + (1 if core == 0 else -1)
                across = wide[at, rows] if 0 <= at < 3 else outer[rows]
                right = jnp.concatenate(
                    [wide[2 - a, rows].reshape(512, 192), across.reshape(512, 192)], axis=0
                )
                term = jnp.dot(left, right, preferred_element_type=F32)
                for c in range(3):
                    row = (3 * k + c) * 256
                    total[row : row + 256] = term[:, c * 64 : c * 64 + 64]
    for step in range(4):
        for c in range(2):
            block = lax.rem(place[2] + step, 4) * 4 + lax.rem(place[1] + place[0], 2) * 2 + c
            row = pl.multiple_of(block * 432, 16)
            upper = total[pl.ds(row, 224)]
            lower = total[pl.ds(pl.multiple_of(row + 224, 16), 208)]
            lower = jnp.concatenate([lower, jnp.zeros((16, 64), F32)], axis=0)
            both = jnp.concatenate([upper, lower], axis=1).astype(BF)
            terms[step, 224 * c : 224 * c + 224] = both


def coarse_forward_kernel(slab, w, grad, own, inner, outer, wide):
    place = position()
    first = place[0] == 0
    outer[:320] = jnp.where(first, grad[:320], grad[320:])
    wide[...] = along_depth(pad_rows(slab[...].reshape(32, 16, 256)), 1)
    total = None
    for b in range(3):
        columns = []
        for a in range(3):
            turned = w[3 * a + b].T
            columns.append(
                jnp.concatenate([turned[:, 64 * c : 64 * c + 64] for c in range(3)], axis=0)
            )
        right = jnp.concatenate(columns, axis=1)
        window = wide[b : b + 32].reshape(512, 768)
        term = jnp.dot(window, right, preferred_element_type=F32)
        total = term if b == 0 else total + term
    own[...] = total[:, 64:128]
    up, down = packed(total[:, :64]).astype(BF), packed(total[:, 128:]).astype(BF)
    inner[...] = jnp.where(first, up, down)
    outer[320:] = jnp.where(first, down, up)


def quad_kernel(own, beside, first, second, third, held, sent):
    core = lax.axis_index("c")
    total = jnp.where(core == 0, own[...], beside[...]).astype(F32)
    total = total + first[...].astype(F32) + second[...].astype(F32) + third[...].astype(F32)
    held[...] = jnp.where(core == 0, total[:224], total[224:]).astype(BF)
    sent[...] = jnp.where(core == 0, total[224:], total[:224]).astype(BF)


def coarse_sum_kernel(scale, own, other, out):
    total = own[...].astype(F32) + other[...].astype(F32)
    total = total * scale
    out[...] = jnp.concatenate([total[:, :64], total[:208, 64:]], axis=0).T


def swap(inner, outer, axis):
    partner = axis[-1]
    pairs = [(i, i + 1) for i in range(1, lax.axis_size(axis) - 1, 2)]
    pairs += [(j, i) for i, j in pairs]
    return lax.ppermute(inner, partner, SWAP), lax.ppermute(outer, axis, pairs)


def body(inputs, weight_fine, weight_coarse, cotangent):
    cells = 65536
    turned_coarse = jnp.swapaxes(weight_coarse, 1, 2).reshape(9, 192, 256)

    pack = call(pack_kernel, (array(384, 256), array(384, 256)), [VMEM] * 2, limit=60)
    inner, outer = pack(inputs, cotangent)
    staged = call(
        stage_kernel,
        (array(9, 192, 256), array(2, 8, 32, 256), array(1, 32, 16, 64)),
        [ANY] * 4,
        [pltpu.SemaphoreType.DMA((3,))],
    )(inner, turned_coarse, inputs, cotangent)
    inner, outer = swap(inner, outer, SP)
    inner, outer, staged = lax.optimization_barrier((inner, outer, staged))
    near_coarse, near_inputs, near_cotangent = staged
    edge = call(edge_kernel, (array(256, 256), array(256, 256)), [VMEM] * 3)
    yinner, youter = swap(*edge(near_inputs, inner, outer), FL)
    partial, wide_cot = call(
        coarse_back_kernel,
        (array(8, 96, 256), array(3, 34, 16, 192)),
        [VMEM] * 4,
        [pltpu.VMEM((544, 256), BF)],
    )(near_cotangent, inner, outer, near_coarse)
    partial, yinner, youter = lax.optimization_barrier((partial, yinner, youter))
    parts = lax.all_to_all(partial, FL, 0, 0, tiled=True)
    blocks = (inputs, inner, outer, yinner, youter)
    sent, slope, far = call(
        fine_forward_kernel,
        (array(8, 64, 256), array(640, 256, dtype=F32), array(768, 256)),
        [VMEM] * 6,
        [
            pltpu.VMEM((4, 12, 32, 768), BF),
            pltpu.VMEM((640, 256), F32),
            pltpu.VMEM((2, 128, 128), F32),
        ],
    )(*blocks, weight_fine.reshape(9, 768, 256))
    far = lax.ppermute(far, "c", SWAP)
    got = lax.all_to_all(sent, FL, 0, 0, tiled=True)
    slab = got.reshape(512, 256)
    grad = call(
        fine_grad_kernel,
        array(640, 256),
        [VMEM] * 2,
        [pltpu.VMEM((2, 192, 128), F32)],
    )(parts, slope)
    other = lax.ppermute(grad, "c", SWAP)
    terms = call(
        fine_weight_kernel,
        array(64, 54, 256),
        [VMEM] * 8,
        [
            pltpu.VMEM((6, 10, 32, 768), BF),
            pltpu.VMEM((9, 6, 256, 256), BF),
            pltpu.VMEM((2, 432, 256), F32),
        ],
        limit=24,
    )(*blocks, far, grad, other)
    terms, slab = lax.optimization_barrier((terms, slab))
    spread = lax.all_to_all(terms, ("x", "yh", "z", "yl"), 0, 0, tiled=True)

    across = lax.ppermute(slab, "c", SWAP)
    coarse_terms = call(
        coarse_weight_kernel,
        array(4, 448, 128),
        [VMEM] * 4,
        [pltpu.VMEM((34, 16, 192), BF), pltpu.VMEM((6912, 64), F32)],
    )(slab, across, wide_cot, far)
    coarse_terms, other = lax.optimization_barrier((coarse_terms, other))
    centre, inner, outer = call(
        coarse_forward_kernel,
        (array(512, 64, dtype=F32), array(128, 256), array(448, 256)),
        [VMEM] * 3,
        [pltpu.VMEM((34, 16, 768), BF)],
    )(slab, turned_coarse, grad)
    inner, outer = swap(inner, outer, SP)
    coarse_terms, inner = lax.optimization_barrier((coarse_terms, inner))
    arrived = []
    for step in range(4):
        pairs = [(4 * x + 2 * y, (4 * x + 4 * step) % 16 + 2 * y) for x in range(4) for y in range(2)]
        pairs = [pair for pair in pairs if step > 0]
        for x in range(4):
            pairs += [(4 * x + 2 * y + 1, (4 * x + 4 * step) % 16 + 3 - 2 * y) for y in range(2)]
        arrived.append(lax.ppermute(coarse_terms[step], SP, pairs))
    total, rest = call(
        fine_back_kernel,
        (array(512, 256, dtype=F32), array(3, 256, 768)),
        [VMEM] * 3,
        [pltpu.VMEM((4, 10, 32, 768), BF)],
        flops=2**31,
    )(grad, other, weight_fine.reshape(9, 3, 256, 256))
    total, rest, arrived = lax.optimization_barrier((total, rest, arrived))
    held, sent = call(quad_kernel, (array(224, 128), array(224, 128)), [VMEM] * 5)(
        coarse_terms[0], *arrived
    )
    _, inner, outer, total, spread = lax.optimization_barrier(
        (sent, inner, outer, total, spread)
    )
    grad_input, coarse_out, grad_fine = call(
        functools.partial(last_kernel, 1.0 / math.sqrt(cells)),
        (array(512, 256), array(512, 64), array(108, 128, dtype=F32)),
        [VMEM] * 6,
        flops=2**30,
    )(total, outer, rest, centre, inner, spread)
    arrived = lax.ppermute(sent, "c", SWAP)
    grad_coarse = call(
        functools.partial(coarse_sum_kernel, 1.0 / math.sqrt(cells // 8)),
        array(64, 432, dtype=F32),
        [VMEM] * 2,
    )(held, arrived)
    return (
        coarse_out.reshape(1, 32, 16, 64),
        grad_input.reshape(2, 8, 32, 256),
        grad_fine.reshape(-1),
        grad_coarse.T,
    )


def solution(mesh):
    fine_mesh = jax.sharding.Mesh(mesh.devices.reshape(4, 2, 2, 4, 2), SP + FL)
    return jax.shard_map(
        body,
        mesh=fine_mesh,
        in_specs=(P(SP, FL, None, None), P(), P(None, None, FL), P(SP, None, None, FL)),
        out_specs=(P(SP, None, None, FL), P(SP, FL, None, None), P(SP + FL), P(SP, FL)),
        check_vma=False,
    )
```

```python
import functools
import math

import jax
import jax.numpy as jnp
from jax import lax
from jax.experimental import pallas as pl
from jax.experimental.pallas import tpu as pltpu
from jax.sharding import PartitionSpec as P

SP = ("x", "yh", "c")
FL = ("z", "yl")
BF = jnp.bfloat16
F32 = jnp.float32
VMEM = pl.BlockSpec(memory_space=pltpu.VMEM)
ANY = pl.BlockSpec(memory_space=pl.ANY)
SWAP = [(0, 1), (1, 0)]


def call(kernel, out_shape, in_specs, scratch=(), limit=12, flops=2**20):
    return pl.pallas_call(
        kernel,
        out_shape=out_shape,
        in_specs=in_specs,
        out_specs=jax.tree.map(lambda _: VMEM, out_shape),
        scratch_shapes=list(scratch),
        compiler_params=pltpu.CompilerParams(vmem_limit_bytes=limit * 2**20),
        cost_estimate=pl.CostEstimate(flops=flops, bytes_accessed=2**16, transcendentals=0),
    )


def array(*shape, dtype=BF):
    return jax.ShapeDtypeStruct(shape, dtype)


def along_depth(rows, order):
    count, depth, width = rows.shape
    flat = rows.astype(F32).reshape(count * depth, width)
    place = lax.broadcasted_iota(jnp.int32, flat.shape, 0) & (depth - 1)
    before = jnp.where(place == 0, 0.0, pltpu.roll(flat, 1, 0)).astype(BF)
    after = jnp.where(place == depth - 1, 0.0, pltpu.roll(flat, count * depth - 1, 0)).astype(BF)
    middle = flat.astype(BF)
    trio = (before, middle, after) if order > 0 else (after, middle, before)
    return jnp.concatenate(trio, axis=1).reshape(count, depth, 3 * width)


def pad_rows(plane):
    edge = jnp.zeros((1,) + plane.shape[1:], plane.dtype)
    return jnp.concatenate([edge, plane, edge], axis=0)


def unpacked(block):
    strips = [block[:, 64 * k : 64 * k + 64] for k in range(4)]
    return jnp.concatenate(strips, axis=0).reshape(32, 16, 64)


def packed(plane):
    return jnp.concatenate([plane[128 * k : 128 * k + 128] for k in range(4)], axis=1)


def position():
    row = 2 * lax.axis_index("z") + lax.axis_index("yl")
    return lax.axis_index("c"), lax.axis_index("yh"), lax.axis_index("x"), row


def ordered(first, inner, outer):
    return jnp.where(first, outer, inner), jnp.where(first, inner, outer)


def pack_kernel(own, cot, inner, outer):
    place = position()
    first = place[0] == 0
    low, high = own[0].reshape(256, 256), own[1].reshape(256, 256)
    inner[:256] = jnp.where(first, high, low)
    outer[:256] = jnp.where(first, low, high)
    flat = cot[0].reshape(512, 64)
    inner[256:] = packed(flat)
    outer[256:] = packed(flat)


def stage_kernel(token, wc_hbm, own_hbm, cot_hbm, wc, own, cot, sems):
    pairs = ((wc_hbm, wc), (own_hbm, own), (cot_hbm, cot))
    copies = [pltpu.make_async_copy(*pair, sems.at[k]) for k, pair in enumerate(pairs)]
    for copy in copies:
        copy.start()
    for copy in copies:
        copy.wait()


def planes_of(place, own, inner, outer):
    lo, hi = ordered(place[0] == 0, inner[:256], outer[:256])
    return lo.reshape(8, 32, 256), own[0], own[1], hi.reshape(8, 32, 256)


def edge_kernel(own, inner, outer, yinner, youter):
    place = position()
    first = lax.rem(place[3], 2) == 0
    for x, plane in enumerate(planes_of(place, own, inner, outer)):
        low, high = plane[:2].reshape(64, 256), plane[6:].reshape(64, 256)
        yinner[64 * x : 64 * x + 64] = jnp.where(first, high, low)
        youter[64 * x : 64 * x + 64] = jnp.where(first, low, high)


def whole_plane(place, plane, yinner, youter, x):
    rows = slice(64 * x, 64 * x + 64)
    below, above = ordered(lax.rem(place[3], 2) == 0, yinner[rows], youter[rows])
    return jnp.concatenate(
        [below.reshape(2, 32, 256), plane, above.reshape(2, 32, 256)], axis=0
    )


def coarse_back_kernel(cot, inner, outer, w, partial, wide, padded):
    place = position()
    lo, hi = ordered(place[0] == 0, inner[256:], outer[256:])
    for x, plane in enumerate((unpacked(lo), cot[0], unpacked(hi))):
        wide[x] = along_depth(pad_rows(plane), -1)
    total = None
    for k in range(9):
        a, b = divmod(k, 3)
        window = wide[2 - a, 2 - b : 34 - b].reshape(512, 192)
        term = jnp.dot(window, w[k], preferred_element_type=F32)
        total = term if k == 0 else total + term
    padded[:16] = jnp.zeros((16, 256), BF)
    padded[16:528] = total.astype(BF)
    padded[528:] = jnp.zeros((16, 256), BF)
    for k in range(8):
        partial[k] = padded[64 * k : 64 * k + 96]


def fine_forward_kernel(
    own, inner, outer, yinner, youter, w, sent, slope, far, wide, pre, sums,
):
    place = position()
    for x, plane in enumerate(planes_of(place, own, inner, outer)):
        plane = whole_plane(place, plane, yinner, youter, x)
        wide[x] = along_depth(plane, 1)

        @pl.when(place[0] == x // 2)
        def _():
            far[320 * (x % 2) : 320 * (x % 2) + 320] = plane[1:11].reshape(320, 256)

    far[640:] = outer[256:]
    for k in range(9):
        a, b = divmod(k, 3)
        window = wide[a : a + 2, b : b + 10].reshape(640, 768)
        term = jnp.dot(window, w[k], preferred_element_type=F32)
        pre[...] = term if k == 0 else pre[...] + term
    for y in range(6):
        total = jnp.zeros((32, 256), F32)
        for x in range(2):
            for row in (2 * y - 1, 2 * y):
                if 0 <= row < 10:
                    at = x * 320 + row * 32
                    value = pre[at : at + 32]
                    sigma = 1.0 / (1.0 + jnp.exp(-value))
                    total = total + (value * sigma).astype(BF).astype(F32)
                    slope[at : at + 32] = 0.125 * sigma * (1.0 + value * (1.0 - sigma))
        if 0 < y < 5:
            sums[0, y * 32 - 32 : y * 32] = total[:, :128]
            sums[1, y * 32 - 32 : y * 32] = total[:, 128:]
    pooled = []
    for side in range(2):
        even = sums[side, pl.ds(0, 64, stride=2)]
        odd = sums[side, pl.ds(1, 64, stride=2)]
        pooled.append(((even + odd) * 0.125).astype(BF))
    pooled = jnp.concatenate(pooled, axis=1)
    for k in range(8):
        sent[k] = pooled


def fine_grad_kernel(parts, slope, grad, spread):
    place = position()
    for y in range(6):
        rows = slice(16 * y, 16 * y + 16)
        total = parts[0, rows].astype(F32)
        for k in range(1, 8):
            total = total + parts[k, rows].astype(F32)
        total = total.astype(BF).astype(F32)
        if y == 0:
            total = jnp.where(place[3] > 0, total, 0.0)
        if y == 5:
            total = jnp.where(place[3] < 7, total, 0.0)
        for side in range(2):
            half = total[:, side * 128 : side * 128 + 128]
            spread[side, pl.ds(32 * y, 16, stride=2)] = half
            spread[side, pl.ds(32 * y + 1, 16, stride=2)] = half
        at = slice(y * 32, y * 32 + 32)
        wide = jnp.concatenate([spread[0, at], spread[1, at]], axis=1)
        for x in range(2):
            for row in (2 * y - 1, 2 * y):
                if 0 <= row < 10:
                    at = x * 320 + row * 32
                    grad[at : at + 32] = (wide * slope[at : at + 32]).astype(BF)


def fine_weight_kernel(
    own, inner, outer, yinner, youter, far, grad, other, terms, wide, turned, total
):
    place = position()
    for core in range(2):

        @pl.when(place[0] == core)
        def _():
            planes, windows = set(), set()
            sides = [side[:256].reshape(8, 32, 256) for side in (inner, outer)]
            blocks = (sides[1 - core], own[0], own[1], sides[core])

            def prepare(bc, slot):
                if (bc, slot) in windows:
                    return
                windows.add((bc, slot))
                if slot not in planes:
                    planes.add(slot)
                    x = slot - 2 * core
                    if 0 <= x < 4:
                        rows = whole_plane(place, blocks[x], yinner, youter, x)[1:11]
                    else:
                        at = 320 * (slot % 2)
                        rows = far[at : at + 320].reshape(10, 32, 256)
                    wide[slot] = along_depth(rows, 1)
                b, c = divmod(bc, 3)
                window = wide[slot, b : b + 8, :, c * 256 : c * 256 + 256]
                turned[bc, slot] = window.reshape(256, 256).T

            pair = (grad, other) if core == 0 else (other, grad)
            right = jnp.concatenate(
                [side[at : at + 256] for side in pair for at in (32, 352)], axis=0
            )
            for k in range(8):
                at = 432 * (2 * k + core)
                end = at + 432
                pieces = []
                while at < end:
                    tap, low = divmod(at, 256)
                    high = min(256, low + end - at)
                    a, bc = divmod(tap, 9)
                    for plane in range(4):
                        prepare(bc, a + plane)
                    strips = [turned[bc, a + plane, low:high] for plane in range(4)]
                    pieces.append(jnp.concatenate(strips, axis=1))
                    at += high - low
                left = jnp.concatenate(pieces, axis=0)
                total[k % 2] = jnp.dot(left, right, preferred_element_type=F32)
                for f in range(8):
                    terms[k * 8 + f] = total[k % 2, f * 54 : f * 54 + 54].astype(BF)


def fine_back_kernel(grad, other, w, total, rest, wide):
    place = position()
    first = place[0] == 0
    none = jnp.zeros((320, 256), BF)
    planes = (
        jnp.where(first, none, other[320:]),
        grad[:320],
        grad[320:],
        jnp.where(first, other[:320], none),
    )
    for x, plane in enumerate(planes):
        wide[x] = along_depth(plane.reshape(10, 32, 256), -1)
    for k in range(9):
        a, b = divmod(k, 3)
        window = wide[2 - a : 4 - a, 2 - b : 10 - b].reshape(512, 768)
        right = jnp.concatenate([w[k, 0], w[k, 1], w[k, 2]], axis=1)
        term = lax.dot_general(window, right, (((1,), (1,)), ((), ())), preferred_element_type=F32)
        total[...] = term if k == 0 else total[...] + term
    for b in range(3):
        for c in range(3):
            at = slice(256 * c, 256 * c + 256)
            rest[b, :, at] = jnp.where(first, w[6 + b, c], w[b, c])


def last_kernel(scale, total, outer, rest, centre, inner, parts, out, coarse, fine):
    place = position()
    wide = along_depth(outer[:320].reshape(10, 32, 256), -1)
    more = None
    for b in range(3):
        window = wide[2 - b : 10 - b].reshape(256, 768)
        term = lax.dot_general(
            window, rest[b], (((1,), (1,)), ((), ())), preferred_element_type=F32
        )
        more = term if b == 0 else more + term
    first = place[0] == 0
    out[:256] = (total[:256] + jnp.where(first, more, 0.0)).astype(BF)
    out[256:] = (total[256:] + jnp.where(first, 0.0, more)).astype(BF)
    for k in range(4):
        rows, columns = slice(128 * k, 128 * k + 128), slice(64 * k, 64 * k + 64)
        plane = centre[rows] + inner[:, columns].astype(F32) + outer[320:, columns].astype(F32)
        coarse[rows] = plane.astype(BF)
    terms = parts[0].astype(F32)
    for k in range(1, 64):
        terms = terms + parts[k].astype(F32)
    terms = terms * scale
    fine[pl.ds(0, 54, stride=2)] = terms[:, :128]
    fine[pl.ds(1, 54, stride=2)] = terms[:, 128:]


def coarse_weight_kernel(slab, other, wide, far, terms, outer, total):
    place = position()
    outer[...] = along_depth(pad_rows(unpacked(far[640:768])), -1)
    left = jnp.concatenate([slab[...].T, other[...].T], axis=1)
    for core in range(2):

        @pl.when(place[0] == core)
        def _():
            for k in range(9):
                a, b = divmod(k, 3)
                rows = slice(2 - b, 34 - b)
                at = 2 - a + (1 if core == 0 else -1)
                across = wide[at, rows] if 0 <= at < 3 else outer[rows]
                right = jnp.concatenate(
                    [wide[2 - a, rows].reshape(512, 192), across.reshape(512, 192)], axis=0
                )
                term = jnp.dot(left, right, preferred_element_type=F32)
                for c in range(3):
                    row = (3 * k + c) * 256
                    total[row : row + 256] = term[:, c * 64 : c * 64 + 64]
    for step in range(4):
        for c in range(2):
            block = lax.rem(place[2] + step, 4) * 4 + lax.rem(place[1] + place[0], 2) * 2 + c
            row = pl.multiple_of(block * 432, 16)
            upper = total[pl.ds(row, 224)]
            lower = total[pl.ds(pl.multiple_of(row + 224, 16), 208)]
            lower = jnp.concatenate([lower, jnp.zeros((16, 64), F32)], axis=0)
            both = jnp.concatenate([upper, lower], axis=1).astype(BF)
            terms[step, 224 * c : 224 * c + 224] = both


def coarse_forward_kernel(slab, w, grad, own, inner, outer, wide):
    place = position()
    first = place[0] == 0
    outer[:320] = jnp.where(first, grad[:320], grad[320:])
    wide[...] = along_depth(pad_rows(slab[...].reshape(32, 16, 256)), 1)
    total = None
    for b in range(3):
        columns = []
        for a in range(3):
            turned = w[3 * a + b].T
            columns.append(
                jnp.concatenate([turned[:, 64 * c : 64 * c + 64] for c in range(3)], axis=0)
            )
        right = jnp.concatenate(columns, axis=1)
        window = wide[b : b + 32].reshape(512, 768)
        term = jnp.dot(window, right, preferred_element_type=F32)
        total = term if b == 0 else total + term
    own[...] = total[:, 64:128]
    up, down = packed(total[:, :64]).astype(BF), packed(total[:, 128:]).astype(BF)
    inner[...] = jnp.where(first, up, down)
    outer[320:] = jnp.where(first, down, up)


def quad_kernel(own, beside, first, second, third, held, sent):
    core = lax.axis_index("c")
    total = jnp.where(core == 0, own[...], beside[...]).astype(F32)
    total = total + first[...].astype(F32) + second[...].astype(F32) + third[...].astype(F32)
    held[...] = jnp.where(core == 0, total[:224], total[224:]).astype(BF)
    sent[...] = jnp.where(core == 0, total[224:], total[:224]).astype(BF)


def coarse_sum_kernel(scale, own, other, out):
    total = own[...].astype(F32) + other[...].astype(F32)
    total = total * scale
    out[...] = jnp.concatenate([total[:, :64], total[:208, 64:]], axis=0).T


def swap(inner, outer, axis):
    partner = axis[-1]
    pairs = [(i, i + 1) for i in range(1, lax.axis_size(axis) - 1, 2)]
    pairs += [(j, i) for i, j in pairs]
    return lax.ppermute(inner, partner, SWAP), lax.ppermute(outer, axis, pairs)


def body(inputs, weight_fine, weight_coarse, cotangent):
    cells = 65536
    turned_coarse = jnp.swapaxes(weight_coarse, 1, 2).reshape(9, 192, 256)

    pack = call(pack_kernel, (array(384, 256), array(384, 256)), [VMEM] * 2, limit=60)
    inner, outer = pack(inputs, cotangent)
    staged = call(
        stage_kernel,
        (array(9, 192, 256), array(2, 8, 32, 256), array(1, 32, 16, 64)),
        [ANY] * 4,
        [pltpu.SemaphoreType.DMA((3,))],
    )(inner, turned_coarse, inputs, cotangent)
    inner, outer = swap(inner, outer, SP)
    inner, outer, staged = lax.optimization_barrier((inner, outer, staged))
    near_coarse, near_inputs, near_cotangent = staged
    edge = call(edge_kernel, (array(256, 256), array(256, 256)), [VMEM] * 3)
    yinner, youter = swap(*edge(near_inputs, inner, outer), FL)
    partial, wide_cot = call(
        coarse_back_kernel,
        (array(8, 96, 256), array(3, 34, 16, 192)),
        [VMEM] * 4,
        [pltpu.VMEM((544, 256), BF)],
    )(near_cotangent, inner, outer, near_coarse)
    partial, yinner, youter = lax.optimization_barrier((partial, yinner, youter))
    parts = lax.all_to_all(partial, FL, 0, 0, tiled=True)
    blocks = (inputs, inner, outer, yinner, youter)
    sent, slope, far = call(
        fine_forward_kernel,
        (array(8, 64, 256), array(640, 256, dtype=F32), array(768, 256)),
        [VMEM] * 6,
        [
            pltpu.VMEM((4, 12, 32, 768), BF),
            pltpu.VMEM((640, 256), F32),
            pltpu.VMEM((2, 128, 128), F32),
        ],
    )(*blocks, weight_fine.reshape(9, 768, 256))
    far = lax.ppermute(far, "c", SWAP)
    got = lax.all_to_all(sent, FL, 0, 0, tiled=True)
    slab = got.reshape(512, 256)
    grad = call(
        fine_grad_kernel,
        array(640, 256),
        [VMEM] * 2,
        [pltpu.VMEM((2, 192, 128), F32)],
    )(parts, slope)
    other = lax.ppermute(grad, "c", SWAP)
    terms = call(
        fine_weight_kernel,
        array(64, 54, 256),
        [VMEM] * 8,
        [
            pltpu.VMEM((6, 10, 32, 768), BF),
            pltpu.VMEM((9, 6, 256, 256), BF),
            pltpu.VMEM((2, 432, 256), F32),
        ],
        limit=24,
    )(*blocks, far, grad, other)
    terms, slab = lax.optimization_barrier((terms, slab))
    spread = lax.all_to_all(terms, ("x", "yh", "z", "yl"), 0, 0, tiled=True)

    across = lax.ppermute(slab, "c", SWAP)
    coarse_terms = call(
        coarse_weight_kernel,
        array(4, 448, 128),
        [VMEM] * 4,
        [pltpu.VMEM((34, 16, 192), BF), pltpu.VMEM((6912, 64), F32)],
    )(slab, across, wide_cot, far)
    coarse_terms, other = lax.optimization_barrier((coarse_terms, other))
    centre, inner, outer = call(
        coarse_forward_kernel,
        (array(512, 64, dtype=F32), array(128, 256), array(448, 256)),
        [VMEM] * 3,
        [pltpu.VMEM((34, 16, 768), BF)],
    )(slab, turned_coarse, grad)
    inner, outer = swap(inner, outer, SP)
    coarse_terms, inner = lax.optimization_barrier((coarse_terms, inner))
    arrived = []
    for step in range(4):
        pairs = [(4 * x + 2 * y, (4 * x + 4 * step) % 16 + 2 * y) for x in range(4) for y in range(2)]
        pairs = [pair for pair in pairs if step > 0]
        for x in range(4):
            pairs += [(4 * x + 2 * y + 1, (4 * x + 4 * step) % 16 + 3 - 2 * y) for y in range(2)]
        arrived.append(lax.ppermute(coarse_terms[step], SP, pairs))
    total, rest = call(
        fine_back_kernel,
        (array(512, 256, dtype=F32), array(3, 256, 768)),
        [VMEM] * 3,
        [pltpu.VMEM((4, 10, 32, 768), BF)],
        flops=2**31,
    )(grad, other, weight_fine.reshape(9, 3, 256, 256))
    total, rest, arrived = lax.optimization_barrier((total, rest, arrived))
    held, sent = call(quad_kernel, (array(224, 128), array(224, 128)), [VMEM] * 5)(
        coarse_terms[0], *arrived
    )
    _, inner, outer, total, spread = lax.optimization_barrier(
        (sent, inner, outer, total, spread)
    )
    grad_input, coarse_out, grad_fine = call(
        functools.partial(last_kernel, 1.0 / math.sqrt(cells)),
        (array(512, 256), array(512, 64), array(108, 128, dtype=F32)),
        [VMEM] * 6,
        flops=2**30,
    )(total, outer, rest, centre, inner, spread)
    arrived = lax.ppermute(sent, "c", SWAP)
    grad_fine, arrived = lax.optimization_barrier((grad_fine, arrived))
    grad_coarse = call(
        functools.partial(coarse_sum_kernel, 1.0 / math.sqrt(cells // 8)),
        array(64, 432, dtype=F32),
        [VMEM] * 2,
    )(held, arrived)
    return (
        coarse_out.reshape(1, 32, 16, 64),
        grad_input.reshape(2, 8, 32, 256),
        grad_fine.reshape(-1),
        grad_coarse.T,
    )


def solution(mesh):
    fine_mesh = jax.sharding.Mesh(mesh.devices.reshape(4, 2, 2, 4, 2), SP + FL)
    return jax.shard_map(
        body,
        mesh=fine_mesh,
        in_specs=(P(SP, FL, None, None), P(), P(None, None, FL), P(SP, None, None, FL)),
        out_specs=(P(SP, None, None, FL), P(SP, FL, None, None), P(SP + FL), P(SP, FL)),
        check_vma=False,
    )
```

```python
import functools
import math

import jax
import jax.numpy as jnp
from jax import lax
from jax.experimental import pallas as pl
from jax.experimental.pallas import tpu as pltpu
from jax.sharding import PartitionSpec as P

SP = ("x", "yh", "c")
FL = ("z", "yl")
BF = jnp.bfloat16
F32 = jnp.float32
VMEM = pl.BlockSpec(memory_space=pltpu.VMEM)
ANY = pl.BlockSpec(memory_space=pl.ANY)
SWAP = [(0, 1), (1, 0)]


def call(kernel, out_shape, in_specs, scratch=(), limit=12, flops=2**20):
    return pl.pallas_call(
        kernel,
        out_shape=out_shape,
        in_specs=in_specs,
        out_specs=jax.tree.map(lambda _: VMEM, out_shape),
        scratch_shapes=list(scratch),
        compiler_params=pltpu.CompilerParams(vmem_limit_bytes=limit * 2**20),
        cost_estimate=pl.CostEstimate(flops=flops, bytes_accessed=2**16, transcendentals=0),
    )


def array(*shape, dtype=BF):
    return jax.ShapeDtypeStruct(shape, dtype)


def along_depth(rows, order):
    count, depth, width = rows.shape
    flat = rows.astype(F32).reshape(count * depth, width)
    place = lax.broadcasted_iota(jnp.int32, flat.shape, 0) & (depth - 1)
    before = jnp.where(place == 0, 0.0, pltpu.roll(flat, 1, 0)).astype(BF)
    after = jnp.where(place == depth - 1, 0.0, pltpu.roll(flat, count * depth - 1, 0)).astype(BF)
    middle = flat.astype(BF)
    trio = (before, middle, after) if order > 0 else (after, middle, before)
    return jnp.concatenate(trio, axis=1).reshape(count, depth, 3 * width)


def pad_rows(plane):
    edge = jnp.zeros((1,) + plane.shape[1:], plane.dtype)
    return jnp.concatenate([edge, plane, edge], axis=0)


def unpacked(block):
    strips = [block[:, 64 * k : 64 * k + 64] for k in range(4)]
    return jnp.concatenate(strips, axis=0).reshape(32, 16, 64)


def packed(plane):
    return jnp.concatenate([plane[128 * k : 128 * k + 128] for k in range(4)], axis=1)


def position():
    row = 2 * lax.axis_index("z") + lax.axis_index("yl")
    return lax.axis_index("c"), lax.axis_index("yh"), lax.axis_index("x"), row


def ordered(first, inner, outer):
    return jnp.where(first, outer, inner), jnp.where(first, inner, outer)


def pack_kernel(own, cot, inner, outer):
    place = position()
    first = place[0] == 0
    low, high = own[0].reshape(256, 256), own[1].reshape(256, 256)
    inner[:256] = jnp.where(first, high, low)
    outer[:256] = jnp.where(first, low, high)
    flat = cot[0].reshape(512, 64)
    inner[256:] = packed(flat)
    outer[256:] = packed(flat)


def stage_kernel(token, wc_hbm, own_hbm, cot_hbm, wc, own, cot, sems):
    pairs = ((wc_hbm, wc), (own_hbm, own), (cot_hbm, cot))
    copies = [pltpu.make_async_copy(*pair, sems.at[k]) for k, pair in enumerate(pairs)]
    for copy in copies:
        copy.start()
    for copy in copies:
        copy.wait()


def planes_of(place, own, inner, outer):
    lo, hi = ordered(place[0] == 0, inner[:256], outer[:256])
    return lo.reshape(8, 32, 256), own[0], own[1], hi.reshape(8, 32, 256)


def edge_kernel(own, inner, outer, yinner, youter):
    place = position()
    first = lax.rem(place[3], 2) == 0
    for x, plane in enumerate(planes_of(place, own, inner, outer)):
        low, high = plane[:2].reshape(64, 256), plane[6:].reshape(64, 256)
        yinner[64 * x : 64 * x + 64] = jnp.where(first, high, low)
        youter[64 * x : 64 * x + 64] = jnp.where(first, low, high)


def whole_plane(place, plane, yinner, youter, x):
    rows = slice(64 * x, 64 * x + 64)
    below, above = ordered(lax.rem(place[3], 2) == 0, yinner[rows], youter[rows])
    return jnp.concatenate(
        [below.reshape(2, 32, 256), plane, above.reshape(2, 32, 256)], axis=0
    )


def coarse_back_kernel(cot, inner, outer, w, partial, wide, padded):
    place = position()
    lo, hi = ordered(place[0] == 0, inner[256:], outer[256:])
    for x, plane in enumerate((unpacked(lo), cot[0], unpacked(hi))):
        wide[x] = along_depth(pad_rows(plane), -1)
    total = None
    for k in range(9):
        a, b = divmod(k, 3)
        window = wide[2 - a, 2 - b : 34 - b].reshape(512, 192)
        term = jnp.dot(window, w[k], preferred_element_type=F32)
        total = term if k == 0 else total + term
    padded[:16] = jnp.zeros((16, 256), BF)
    padded[16:528] = total.astype(BF)
    padded[528:] = jnp.zeros((16, 256), BF)
    for k in range(8):
        partial[k] = padded[64 * k : 64 * k + 96]


def fine_forward_kernel(
    own, inner, outer, yinner, youter, w, sent, slope, far, wide, pre, sums,
):
    place = position()
    for x, plane in enumerate(planes_of(place, own, inner, outer)):
        plane = whole_plane(place, plane, yinner, youter, x)
        wide[x] = along_depth(plane, 1)

        @pl.when(place[0] == x // 2)
        def _():
            far[320 * (x % 2) : 320 * (x % 2) + 320] = plane[1:11].reshape(320, 256)

    far[640:] = outer[256:]
    for k in range(9):
        a, b = divmod(k, 3)
        window = wide[a : a + 2, b : b + 10].reshape(640, 768)
        term = jnp.dot(window, w[k], preferred_element_type=F32)
        pre[...] = term if k == 0 else pre[...] + term
    for y in range(6):
        total = jnp.zeros((32, 256), F32)
        for x in range(2):
            for row in (2 * y - 1, 2 * y):
                if 0 <= row < 10:
                    at = x * 320 + row * 32
                    value = pre[at : at + 32]
                    sigma = 1.0 / (1.0 + jnp.exp(-value))
                    total = total + (value * sigma).astype(BF).astype(F32)
                    slope[at : at + 32] = 0.125 * sigma * (1.0 + value * (1.0 - sigma))
        if 0 < y < 5:
            sums[0, y * 32 - 32 : y * 32] = total[:, :128]
            sums[1, y * 32 - 32 : y * 32] = total[:, 128:]
    pooled = []
    for side in range(2):
        even = sums[side, pl.ds(0, 64, stride=2)]
        odd = sums[side, pl.ds(1, 64, stride=2)]
        pooled.append(((even + odd) * 0.125).astype(BF))
    pooled = jnp.concatenate(pooled, axis=1)
    for k in range(8):
        sent[k] = pooled


def fine_grad_kernel(parts, slope, grad, spread):
    place = position()
    for y in range(6):
        rows = slice(16 * y, 16 * y + 16)
        total = parts[0, rows].astype(F32)
        for k in range(1, 8):
            total = total + parts[k, rows].astype(F32)
        total = total.astype(BF).astype(F32)
        if y == 0:
            total = jnp.where(place[3] > 0, total, 0.0)
        if y == 5:
            total = jnp.where(place[3] < 7, total, 0.0)
        for side in range(2):
            half = total[:, side * 128 : side * 128 + 128]
            spread[side, pl.ds(32 * y, 16, stride=2)] = half
            spread[side, pl.ds(32 * y + 1, 16, stride=2)] = half
        at = slice(y * 32, y * 32 + 32)
        wide = jnp.concatenate([spread[0, at], spread[1, at]], axis=1)
        for x in range(2):
            for row in (2 * y - 1, 2 * y):
                if 0 <= row < 10:
                    at = x * 320 + row * 32
                    grad[at : at + 32] = (wide * slope[at : at + 32]).astype(BF)


def fine_weight_kernel(
    own, inner, outer, yinner, youter, far, grad, other, terms, wide, turned, total
):
    place = position()
    for core in range(2):

        @pl.when(place[0] == core)
        def _():
            planes, windows = set(), set()
            sides = [side[:256].reshape(8, 32, 256) for side in (inner, outer)]
            blocks = (sides[1 - core], own[0], own[1], sides[core])

            def prepare(bc, slot):
                if (bc, slot) in windows:
                    return
                windows.add((bc, slot))
                if slot not in planes:
                    planes.add(slot)
                    x = slot - 2 * core
                    if 0 <= x < 4:
                        rows = whole_plane(place, blocks[x], yinner, youter, x)[1:11]
                    else:
                        at = 320 * (slot % 2)
                        rows = far[at : at + 320].reshape(10, 32, 256)
                    wide[slot] = along_depth(rows, 1)
                b, c = divmod(bc, 3)
                window = wide[slot, b : b + 8, :, c * 256 : c * 256 + 256]
                turned[bc, slot] = window.reshape(256, 256).T

            pair = (grad, other) if core == 0 else (other, grad)
            right = jnp.concatenate(
                [side[at : at + 256] for side in pair for at in (32, 352)], axis=0
            )
            for k in range(8):
                at = 432 * (2 * k + core)
                end = at + 432
                pieces = []
                while at < end:
                    tap, low = divmod(at, 256)
                    high = min(256, low + end - at)
                    a, bc = divmod(tap, 9)
                    for plane in range(4):
                        prepare(bc, a + plane)
                    strips = [turned[bc, a + plane, low:high] for plane in range(4)]
                    pieces.append(jnp.concatenate(strips, axis=1))
                    at += high - low
                left = jnp.concatenate(pieces, axis=0)
                total[k % 2] = jnp.dot(left, right, preferred_element_type=F32)
                for f in range(8):
                    terms[k * 8 + f] = total[k % 2, f * 54 : f * 54 + 54].astype(BF)


def fine_back_kernel(grad, other, w, total, rest, wide):
    place = position()
    first = place[0] == 0
    none = jnp.zeros((320, 256), BF)
    planes = (
        jnp.where(first, none, other[320:]),
        grad[:320],
        grad[320:],
        jnp.where(first, other[:320], none),
    )
    for x, plane in enumerate(planes):
        wide[x] = along_depth(plane.reshape(10, 32, 256), -1)
    for k in range(9):
        a, b = divmod(k, 3)
        window = wide[2 - a : 4 - a, 2 - b : 10 - b].reshape(512, 768)
        right = jnp.concatenate([w[k, 0], w[k, 1], w[k, 2]], axis=1)
        term = lax.dot_general(window, right, (((1,), (1,)), ((), ())), preferred_element_type=F32)
        total[...] = term if k == 0 else total[...] + term
    for b in range(3):
        for c in range(3):
            at = slice(256 * c, 256 * c + 256)
            rest[b, :, at] = jnp.where(first, w[6 + b, c], w[b, c])


def last_kernel(scale, total, outer, rest, centre, inner, parts, out, coarse, fine):
    place = position()
    wide = along_depth(outer[:320].reshape(10, 32, 256), -1)
    more = None
    for b in range(3):
        window = wide[2 - b : 10 - b].reshape(256, 768)
        term = lax.dot_general(
            window, rest[b], (((1,), (1,)), ((), ())), preferred_element_type=F32
        )
        more = term if b == 0 else more + term
    first = place[0] == 0
    out[:256] = (total[:256] + jnp.where(first, more, 0.0)).astype(BF)
    out[256:] = (total[256:] + jnp.where(first, 0.0, more)).astype(BF)
    for k in range(4):
        rows, columns = slice(128 * k, 128 * k + 128), slice(64 * k, 64 * k + 64)
        plane = centre[rows] + inner[:, columns].astype(F32) + outer[320:, columns].astype(F32)
        coarse[rows] = plane.astype(BF)
    terms = parts[0].astype(F32)
    for k in range(1, 64):
        terms = terms + parts[k].astype(F32)
    terms = terms * scale
    fine[pl.ds(0, 54, stride=2)] = terms[:, :128]
    fine[pl.ds(1, 54, stride=2)] = terms[:, 128:]


def coarse_weight_kernel(slab, other, wide, far, terms, outer, total):
    place = position()
    outer[...] = along_depth(pad_rows(unpacked(far[640:768])), -1)
    left = jnp.concatenate([slab[...].T, other[...].T], axis=1)
    for core in range(2):

        @pl.when(place[0] == core)
        def _():
            for k in range(9):
                a, b = divmod(k, 3)
                rows = slice(2 - b, 34 - b)
                at = 2 - a + (1 if core == 0 else -1)
                across = wide[at, rows] if 0 <= at < 3 else outer[rows]
                right = jnp.concatenate(
                    [wide[2 - a, rows].reshape(512, 192), across.reshape(512, 192)], axis=0
                )
                term = jnp.dot(left, right, preferred_element_type=F32)
                for c in range(3):
                    row = (3 * k + c) * 256
                    total[row : row + 256] = term[:, c * 64 : c * 64 + 64]
    for step in range(4):
        for c in range(2):
            block = lax.rem(place[2] + step, 4) * 4 + lax.rem(place[1] + place[0], 2) * 2 + c
            row = pl.multiple_of(block * 432, 16)
            upper = total[pl.ds(row, 224)]
            lower = total[pl.ds(pl.multiple_of(row + 224, 16), 208)]
            lower = jnp.concatenate([lower, jnp.zeros((16, 64), F32)], axis=0)
            both = jnp.concatenate([upper, lower], axis=1).astype(BF)
            terms[step, 224 * c : 224 * c + 224] = both


def coarse_forward_kernel(slab, w, grad, own, inner, outer, wide):
    place = position()
    first = place[0] == 0
    outer[:320] = jnp.where(first, grad[:320], grad[320:])
    wide[...] = along_depth(pad_rows(slab[...].reshape(32, 16, 256)), 1)
    total = None
    for b in range(3):
        columns = []
        for a in range(3):
            turned = w[3 * a + b].T
            columns.append(
                jnp.concatenate([turned[:, 64 * c : 64 * c + 64] for c in range(3)], axis=0)
            )
        right = jnp.concatenate(columns, axis=1)
        window = wide[b : b + 32].reshape(512, 768)
        term = jnp.dot(window, right, preferred_element_type=F32)
        total = term if b == 0 else total + term
    own[...] = total[:, 64:128]
    up, down = packed(total[:, :64]).astype(BF), packed(total[:, 128:]).astype(BF)
    inner[...] = jnp.where(first, up, down)
    outer[320:] = jnp.where(first, down, up)


def quad_kernel(own, beside, first, second, third, held, sent):
    core = lax.axis_index("c")
    total = jnp.where(core == 0, own[...], beside[...]).astype(F32)
    total = total + first[...].astype(F32) + second[...].astype(F32) + third[...].astype(F32)
    held[...] = jnp.where(core == 0, total[:224], total[224:]).astype(BF)
    sent[...] = jnp.where(core == 0, total[224:], total[:224]).astype(BF)


def coarse_sum_kernel(scale, own, other, out):
    total = own[...].astype(F32) + other[...].astype(F32)
    total = total * scale
    out[...] = jnp.concatenate([total[:, :64], total[:208, 64:]], axis=0).T


def swap(inner, outer, axis):
    partner = axis[-1]
    pairs = [(i, i + 1) for i in range(1, lax.axis_size(axis) - 1, 2)]
    pairs += [(j, i) for i, j in pairs]
    return lax.ppermute(inner, partner, SWAP), lax.ppermute(outer, axis, pairs)


def body(inputs, weight_fine, weight_coarse, cotangent):
    cells = 65536
    turned_coarse = jnp.swapaxes(weight_coarse, 1, 2).reshape(9, 192, 256)

    pack = call(pack_kernel, (array(384, 256), array(384, 256)), [VMEM] * 2, limit=60)
    inner, outer = pack(inputs, cotangent)
    staged = call(
        stage_kernel,
        (array(9, 192, 256), array(2, 8, 32, 256), array(1, 32, 16, 64)),
        [ANY] * 4,
        [pltpu.SemaphoreType.DMA((3,))],
    )(inner, turned_coarse, inputs, cotangent)
    inner, outer = swap(inner, outer, SP)
    inner, outer, staged = lax.optimization_barrier((inner, outer, staged))
    near_coarse, near_inputs, near_cotangent = staged
    edge = call(edge_kernel, (array(256, 256), array(256, 256)), [VMEM] * 3)
    yinner, youter = swap(*edge(near_inputs, inner, outer), FL)
    partial, wide_cot = call(
        coarse_back_kernel,
        (array(8, 96, 256), array(3, 34, 16, 192)),
        [VMEM] * 4,
        [pltpu.VMEM((544, 256), BF)],
    )(near_cotangent, inner, outer, near_coarse)
    partial, yinner, youter = lax.optimization_barrier((partial, yinner, youter))
    parts = lax.all_to_all(partial, FL, 0, 0, tiled=True)
    blocks = (inputs, inner, outer, yinner, youter)
    sent, slope, far = call(
        fine_forward_kernel,
        (array(8, 64, 256), array(640, 256, dtype=F32), array(768, 256)),
        [VMEM] * 6,
        [
            pltpu.VMEM((4, 12, 32, 768), BF),
            pltpu.VMEM((640, 256), F32),
            pltpu.VMEM((2, 128, 128), F32),
        ],
    )(*blocks, weight_fine.reshape(9, 768, 256))
    far = lax.ppermute(far, "c", SWAP)
    got = lax.all_to_all(sent, FL, 0, 0, tiled=True)
    slab = got.reshape(512, 256)
    grad = call(
        fine_grad_kernel,
        array(640, 256),
        [VMEM] * 2,
        [pltpu.VMEM((2, 192, 128), F32)],
    )(parts, slope)
    other = lax.ppermute(grad, "c", SWAP)
    terms = call(
        fine_weight_kernel,
        array(64, 54, 256),
        [VMEM] * 8,
        [
            pltpu.VMEM((6, 10, 32, 768), BF),
            pltpu.VMEM((9, 6, 256, 256), BF),
            pltpu.VMEM((2, 432, 256), F32),
        ],
        limit=24,
    )(*blocks, far, grad, other)
    terms, slab = lax.optimization_barrier((terms, slab))
    spread = lax.all_to_all(terms, ("x", "yh", "z", "yl"), 0, 0, tiled=True)

    across = lax.ppermute(slab, "c", SWAP)
    coarse_terms = call(
        coarse_weight_kernel,
        array(4, 448, 128),
        [VMEM] * 4,
        [pltpu.VMEM((34, 16, 192), BF), pltpu.VMEM((6912, 64), F32)],
    )(slab, across, wide_cot, far)
    coarse_terms, other = lax.optimization_barrier((coarse_terms, other))
    centre, inner, outer = call(
        coarse_forward_kernel,
        (array(512, 64, dtype=F32), array(128, 256), array(448, 256)),
        [VMEM] * 3,
        [pltpu.VMEM((34, 16, 768), BF)],
    )(slab, turned_coarse, grad)
    inner, outer = swap(inner, outer, SP)
    coarse_terms, inner = lax.optimization_barrier((coarse_terms, inner))
    arrived = []
    for step in range(4):
        pairs = [(4 * x + 2 * y, (4 * x + 4 * step) % 16 + 2 * y) for x in range(4) for y in range(2)]
        pairs = [pair for pair in pairs if step > 0]
        for x in range(4):
            pairs += [(4 * x + 2 * y + 1, (4 * x + 4 * step) % 16 + 3 - 2 * y) for y in range(2)]
        arrived.append(lax.ppermute(coarse_terms[step], SP, pairs))
    total, rest = call(
        fine_back_kernel,
        (array(512, 256, dtype=F32), array(3, 256, 768)),
        [VMEM] * 3,
        [pltpu.VMEM((4, 10, 32, 768), BF)],
        flops=2**31,
    )(grad, other, weight_fine.reshape(9, 3, 256, 256))
    total, rest, arrived = lax.optimization_barrier((total, rest, arrived))
    held, sent = call(quad_kernel, (array(224, 128), array(224, 128)), [VMEM] * 5)(
        coarse_terms[0], *arrived
    )
    _, inner, outer, total, spread = lax.optimization_barrier(
        (sent, inner, outer, total, spread)
    )
    grad_input, coarse_out, grad_fine = call(
        functools.partial(last_kernel, 1.0 / math.sqrt(cells)),
        (array(512, 256), array(512, 64), array(108, 128, dtype=F32)),
        [VMEM] * 6,
        limit=60,
        flops=2**30,
    )(total, outer, rest, centre, inner, spread)
    arrived = lax.ppermute(sent, "c", SWAP)
    grad_coarse = call(
        functools.partial(coarse_sum_kernel, 1.0 / math.sqrt(cells // 8)),
        array(64, 432, dtype=F32),
        [VMEM] * 2,
    )(held, arrived)
    return (
        coarse_out.reshape(1, 32, 16, 64),
        grad_input.reshape(2, 8, 32, 256),
        grad_fine.reshape(-1),
        grad_coarse.T,
    )


def solution(mesh):
    fine_mesh = jax.sharding.Mesh(mesh.devices.reshape(4, 2, 2, 4, 2), SP + FL)
    return jax.shard_map(
        body,
        mesh=fine_mesh,
        in_specs=(P(SP, FL, None, None), P(), P(None, None, FL), P(SP, None, None, FL)),
        out_specs=(P(SP, None, None, FL), P(SP, FL, None, None), P(SP + FL), P(SP, FL)),
        check_vma=False,
    )
```
